32 devices in a mesh: row: 8 (over y, x, core), col: 4 (over z).
Axes of the slice: x: 2, y: 2, z: 4, core: 2. Of those that a mesh axis runs over, the one named last changes fastest.
Arguments:
- orbitals_in: float32 [4096, 256], P(('row', 'col')), may hold values from -6 to 6
- hblocks: bfloat16 [64, 32, 4096], P('row', 'col'), may hold values from -0.09375 to 0.09375
- block_cols: int32 [64, 32], P('row', 'col'), may hold values from 0 to 15, as said below
- live_counts: int32 [64, 4], P('row', 'col'), may hold values from 0 to 8, as said below
- onsite: bfloat16 [64, 4096], P(('row', 'col')), may hold values from -3 to 1, as said below
- cut_low: float32 [1], replicated, may hold values from -1.6 to -1
- top_bound: float32 [1], replicated, may hold values from 2.4 to 3.2
Outputs:
- orbitals: float32 [4096, 256], P(('row', 'col'))
- projected: float32 [256, 256], replicated
The draws below stay inside these ranges and needn't reach their ends.
Inputs may be any that keep to these rules, and one draw needn't show every extreme that they name: `block_cols`: in block row b and column group c the first live_counts[b, c] slots name distinct block columns whose global block index exceeds b (strict upper triangle); the other slots are padding and are ignored. `live_counts`: block row 0 fills all 8 slots of every column group; the last block row has no live slot. `onsite`: every block is symmetric.
All inputs are finite; a program needn't handle non-finite values.
Results may differ from the reference program's by a relative error of at most 0.0008.
The reference program's roundings to bfloat16 on the way count: a program that leaves them out, or rounds other values in their place, can miss the bound.
Values may be sent and summed in bfloat16 or wider, within the bound.
No kernel may reach another device: no remote copies, remote signals or barrier semaphores. Data moves between devices by JAX's collectives and lax.ppermute only.
A program may use at most 128 MiB of HBM per device.

```python
import jax
import jax.numpy as jnp
from jax import lax

BS = 64
K = 256
PB = 2
DEG = 3
NBR = 8
NBC = 16
SLOTS = 8
ROW_SLOTS = 32
NB = 64
M = 4096
N_ROW = 8
N_COL = 4


def sparsity_pattern(key):
    folded = jax.random.fold_in(key, 11)
    key_order, key_count = jax.random.split(folded)
    groups = NBR // PB
    block_rows = jnp.arange(NB, dtype=jnp.int32)[:, None, None]
    group_index = jnp.arange(groups, dtype=jnp.int32)[None, :, None]
    local_cols = jnp.arange(NBC, dtype=jnp.int32)[None, None, :]
    global_cols = (local_cols // PB * groups + group_index) * PB + local_cols % PB
    eligible = (global_cols > block_rows).astype(jnp.int32)
    noise = jax.random.randint(key_order, (NB, groups, NBC), 0, 1 << 20)
    scores = (eligible * (1 << 21) + noise) * NBC + local_cols
    ordering = jnp.argsort(-scores, axis=-1).astype(jnp.int32)
    chosen = ordering[:, :, :SLOTS]
    available = jnp.sum(eligible, axis=-1)
    wanted = jax.random.randint(key_count, (NB, groups), 1, SLOTS + 1)
    wanted = wanted.at[0].set(SLOTS)
    counts = jnp.minimum(available, wanted).astype(jnp.int32)
    return (chosen.reshape(NB, groups * SLOTS), counts)


def draw_block_cols(key, part):
    return sparsity_pattern(key)[0]


def draw_live_counts(key, part):
    return sparsity_pattern(key)[1]


def draw_onsite(key, part):
    key_off, key_diag = jax.random.split(jax.random.fold_in(key, 5))
    offdiag = jnp.clip(0.1 * jax.random.normal(key_off, (NB, BS, BS)), -0.45, 0.45)
    energies = jax.random.uniform(key_diag, (NB, BS), minval=-2.5, maxval=0.5)
    offdiag = 0.5 * (offdiag + jnp.swapaxes(offdiag, 1, 2))
    blocks = offdiag + energies[:, :, None] * jnp.eye(BS, dtype=jnp.float32)[None, :, :]
    return blocks.reshape(NB, BS * BS).astype(jnp.bfloat16)


def block_scale(key, extent, cuts, least, top_value):
    def one(dim, blocks):
        steps = jax.random.uniform(jax.random.fold_in(jax.random.fold_in(key, 6), dim), (blocks,), jnp.float32, least / len(cuts), top_value / len(cuts))
        return jnp.repeat(jnp.exp(steps), extent[dim] // blocks).reshape((-1,) + (1,) * (len(extent) - dim - 1))

    level = one(*cuts[0])
    for cut in cuts[1:]:
        level = level * one(*cut)
    return level


def centred(key, extent, width, bound, pieces=(), held_as=jnp.bfloat16):
    factor_of = block_scale(key, extent, pieces, -0.22, 0.18) if pieces else 1.0
    entries = jax.random.normal(key, extent, jnp.float32) * width * factor_of
    return jnp.minimum(jnp.maximum(entries, -bound), bound).astype(held_as)


def setup_inputs(seed: int = 0) -> dict:
    arg_keys = jax.random.split(jax.random.key(seed), 8)
    return {
        "orbitals_in": centred(arg_keys[0], (M, K), 1.0, 6.0, ((0, 32),), jnp.float32),
        "hblocks": centred(arg_keys[1], (NB, ROW_SLOTS, BS * BS), (BS * NB) ** -0.5, 0.09375, ((0, 8), (1, 4))),
        "block_cols": draw_block_cols(jax.random.fold_in(arg_keys[7], 71), 0),
        "live_counts": draw_live_counts(jax.random.fold_in(arg_keys[7], 71), 0),
        "onsite": draw_onsite(jax.random.fold_in(arg_keys[7], 71), 0),
        "cut_low": jnp.clip(jax.random.uniform(arg_keys[5], (1,), jnp.float32, -1.6, -1.0), -1.6, -1.0),
        "top_bound": jnp.clip(jax.random.uniform(arg_keys[6], (1,), jnp.float32, 2.4, 3.2), 2.4, 3.2),
    }


def global_columns(block_cols):
    slot_index = jnp.arange(N_COL * SLOTS, dtype=jnp.int32)
    group_index = slot_index // SLOTS
    return (block_cols // PB * N_COL + group_index[None, :]) * PB + block_cols % PB

def reference(orbitals_in, hblocks, block_cols, live_counts, onsite, cut_low, top_bound):
    gcols = global_columns(block_cols)
    occupied = (jnp.arange(SLOTS, dtype=jnp.int32)[None, None, :] < live_counts[:, :, None]).reshape(NB, N_COL * SLOTS)
    blocks = hblocks.reshape(NB, N_COL * SLOTS, BS, BS) * occupied[:, :, None, None].astype(jnp.bfloat16)
    onsite_blocks = onsite.reshape(NB, BS, BS).astype(jnp.float32)

    def apply(rounded):
        vblocks = rounded.reshape(NB, BS, K)
        onsite_part = jnp.einsum('nab,nbk->nak', onsite_blocks, vblocks.astype(jnp.float32))

        def group(running, group_row):
            offset = group_row * NBR
            hrows = lax.dynamic_slice_in_dim(blocks, offset, NBR, 0).astype(jnp.float32)
            grows = lax.dynamic_slice_in_dim(gcols, offset, NBR, 0)
            gathered = vblocks[grows].astype(jnp.float32)
            own_rows = lax.dynamic_slice_in_dim(vblocks, offset, NBR, 0).astype(jnp.float32)
            direct = jnp.einsum('isab,isbk->iak', hrows, gathered)
            terms = jnp.einsum('isab,iak->isbk', hrows, own_rows)
            column_part = jnp.zeros((NB, BS, K), jnp.float32).at[grows.reshape(-1)].add(terms.reshape(-1, BS, K))
            return (running + column_part, direct)
        column_sum, row_parts = lax.scan(group, jnp.zeros((NB, BS, K), jnp.float32), jnp.arange(N_ROW, dtype=jnp.int32))
        return (onsite_part + row_parts.reshape(NB, BS, K) + column_sum).reshape(M, K)
    centre = 0.5 * (top_bound[0] + cut_low[0])
    halfwidth = 0.5 * (top_bound[0] - cut_low[0])
    previous = orbitals_in
    current = (apply(orbitals_in.astype(jnp.bfloat16)) - centre * orbitals_in) / halfwidth
    for degree in range(DEG - 1):
        following = 2.0 * (apply(current.astype(jnp.bfloat16)) - centre * current) / halfwidth - previous
        previous, current = (current, following)
    rounded = current.astype(jnp.bfloat16)
    image = apply(rounded)
    as_float = rounded.astype(jnp.float32)
    dims = (((0,), (0,)), ((), ()))
    gram_matrix = lax.dot_general(rounded.astype(jnp.float32), rounded.astype(jnp.float32), dims, preferred_element_type=jnp.float32) / M
    cross = lax.dot_general(as_float, image, dims, precision=lax.Precision.HIGHEST)
    ritz_matrix = (cross + cross.T) / (2.0 * M)
    factor = jnp.linalg.cholesky(gram_matrix)
    orbitals = jax.scipy.linalg.solve_triangular(factor, current.T, lower=True).T
    inner = jax.scipy.linalg.solve_triangular(factor, ritz_matrix, lower=True)
    projected = jax.scipy.linalg.solve_triangular(factor, inner.T, lower=True)
    return (orbitals, projected)
```

```python
import jax
import jax.numpy as jnp
from jax import lax
from jax.sharding import PartitionSpec as P

BS = 64
PB = 2
DEG = 3


def shifted(x, axis, size, step):
    return lax.ppermute(x, axis, [(i, (i + step) % size) for i in range(size)])


def core_swap(x, rows):
    return lax.ppermute(x, "row", [(i, i ^ 1) for i in range(rows)])


def chip_shifted(x, rows, step):
    return lax.ppermute(x, "row", [(i, (i + 2 * step) % rows) for i in range(rows)])


def local(orbitals_in, hblocks, block_cols, live_counts, onsite, cut_low, top_bound):
    rows = lax.axis_size("row")
    cols = lax.axis_size("col")
    chips = rows // 2
    row = lax.axis_index("row")
    col = lax.axis_index("col")
    chip, core = row // 2, row % 2
    row_blocks, slots, _ = hblocks.shape
    k = orbitals_in.shape[1]
    local_rows = PB * BS
    total_rows = rows * cols * local_rows

    live = jnp.arange(slots, dtype=jnp.int32)[None, :] < live_counts
    codes = jnp.where(live, block_cols, -1)

    pieces = hblocks.reshape(cols, PB, slots, BS * BS)
    code_pieces = codes.reshape(cols, PB, slots)
    own_raw, own_codes = [], []
    for step in range(cols):
        target = (col + step) % cols
        raw = lax.dynamic_index_in_dim(pieces, target, 0, keepdims=False)
        code = lax.dynamic_index_in_dim(code_pieces, target, 0, keepdims=False)
        own_raw.append(shifted(raw, "col", cols, step) if step else raw)
        own_codes.append(shifted(code, "col", cols, step) if step else code)
    own_raw = jnp.stack(own_raw)
    own_codes = jnp.stack(own_codes)

    def gather_rows(v):
        near = jnp.concatenate([v] + [shifted(v, "col", cols, s) for s in range(1, cols)], 0)
        return near, core_swap(near, rows)

    first = orbitals_in.astype(jnp.bfloat16)
    first_gathered = gather_rows(first)

    def selector(code, chip_distance, width):
        device, block = code // PB, code % PB
        distance = chip_distance(device // 2) % chips
        place = (distance * 2 + ((device % 2) ^ core)) * PB + block
        place = jnp.where(code < 0, -1, place)
        return (place[..., None] == jnp.arange(width, dtype=jnp.int32)).astype(jnp.bfloat16)

    width = chips * 2 * PB

    sel = selector(codes, lambda d: chip - d, width).reshape(row_blocks, slots, chips, 2, PB)
    mirrored = jnp.einsum(
        "isqjm,isab->jqmbia",
        sel,
        hblocks.reshape(row_blocks, slots, BS, BS),
        preferred_element_type=jnp.float32,
    ).astype(jnp.bfloat16)
    mirrored = mirrored.reshape(2, chips * local_rows, cols, local_rows)
    mirrored = jnp.stack(
        [lax.dynamic_index_in_dim(mirrored, (col - s) % cols, 2, keepdims=False) for s in range(cols)],
        2,
    ).reshape(2, chips, local_rows, cols * local_rows)
    mirrored = jnp.concatenate([mirrored[0], core_swap(mirrored[1], rows)], 2)

    sel = selector(own_codes, lambda d: d - chip, width).reshape(cols, PB, slots, 2 * chips, PB)
    direct = jnp.einsum(
        "cpsnm,cpsab->npacmb",
        sel,
        own_raw.reshape(cols, PB, slots, BS, BS),
        preferred_element_type=jnp.float32,
    ).astype(jnp.bfloat16)
    direct = direct.reshape(chips, 2, local_rows, cols * local_rows)
    direct = jnp.concatenate([direct[:, 0], direct[:, 1]], 2)
    direct = [direct[0]] + [chip_shifted(direct[s], rows, s) for s in range(1, chips)]

    onsite_blocks = onsite.reshape(PB, BS, BS)
    diagonal = jnp.concatenate(
        [jnp.pad(onsite_blocks[p], ((0, 0), (p * BS, (PB - 1 - p) * BS))) for p in range(PB)], 0
    )
    direct[0] = direct[0] + jnp.pad(diagonal, ((0, 0), (0, (2 * cols - 1) * local_rows)))
    tile = (mirrored + jnp.stack(direct)).reshape(chips * local_rows, 2 * cols * local_rows)
    tile_near, tile_far = tile[:, : cols * local_rows], tile[:, cols * local_rows :]

    def partial_product(gathered):
        near, far = gathered
        return jnp.dot(tile_near, near, preferred_element_type=jnp.float32) + jnp.dot(
            tile_far, far, preferred_element_type=jnp.float32
        )

    def apply(gathered):
        terms = partial_product(gathered).reshape(chips, local_rows, k)
        total = terms[0]
        for s in range(1, chips):
            total = total + chip_shifted(terms[s], rows, chips - s)
        return total

    centre = 0.5 * (top_bound[0] + cut_low[0])
    halfwidth = 0.5 * (top_bound[0] - cut_low[0])
    previous = orbitals_in
    current = (apply(first_gathered) - centre * orbitals_in) / halfwidth
    for degree in range(DEG - 1):
        gathered = gather_rows(current.astype(jnp.bfloat16))
        following = 2.0 * (apply(gathered) - centre * current) / halfwidth - previous
        previous, current = (current, following)

    rounded = current.astype(jnp.bfloat16)
    gathered = gather_rows(rounded)
    contract = (((0,), (0,)), ((), ()))
    plane_rows = jnp.concatenate(
        [rounded] + [chip_shifted(rounded, rows, s) for s in range(1, chips)], 0
    )
    gram_part = sum(
        lax.dot_general(g, g, contract, preferred_element_type=jnp.float32) for g in gathered
    )
    cross_part = lax.dot_general(
        plane_rows.astype(jnp.float32),
        partial_product(gathered),
        contract,
        precision=lax.Precision.HIGHEST,
    )

    share = k // rows

    def chunk(x, owner):
        return lax.dynamic_slice_in_dim(x, owner * share, share, 0)

    gram_share = chunk(gram_part, row)
    for s in range(1, chips):
        gram_share = gram_share + chip_shifted(
            chunk(gram_part, (row + 2 * s) % rows), rows, s
        )
    gram_matrix = lax.all_gather(gram_share, "row", axis=0, tiled=True) / total_rows

    cross_share = chunk(cross_part, row)
    for s in range(1, rows):
        cross_share = cross_share + shifted(chunk(cross_part, (row + s) % rows), "row", rows, s)
    cross_share = sum([shifted(cross_share, "col", cols, s) for s in range(1, cols)], cross_share)
    cross_total = lax.all_gather(cross_share, "row", axis=0, tiled=True)
    ritz_matrix = (cross_total + cross_total.T) / (2.0 * total_rows)

    factor = jnp.linalg.cholesky(gram_matrix)
    orbitals = jax.scipy.linalg.solve_triangular(factor, current.T, lower=True).T
    inner = jax.scipy.linalg.solve_triangular(factor, ritz_matrix, lower=True)
    projected = jax.scipy.linalg.solve_triangular(factor, inner.T, lower=True)
    return (orbitals, projected)


def solution(mesh):
    placed = (
        P(("row", "col"), None),
        P("row", "col", None),
        P("row", "col"),
        P("row", "col"),
        P(("row", "col"), None),
        P(),
        P(),
    )
    return jax.shard_map(
        local, mesh=mesh, in_specs=placed, out_specs=(P(("row", "col"), None), P()), check_vma=False
    )
```

```python
import functools

import jax
import jax.numpy as jnp
from jax import lax
from jax.experimental import pallas as pl
from jax.experimental.pallas import tpu as pltpu
from jax.sharding import PartitionSpec as P

BS = 64
PB = 2
DEG = 3
LANES = 128
PANEL = 32
HI = lax.Precision.HIGHEST


def widen(x, width):
    return jnp.concatenate([x] * (width // LANES), 1) if width > LANES else x

def finish_kernel(total_rows, gram_ref, cross_ref, y_ref, orbitals_ref, projected_ref, inverse_ref):
    k = gram_ref.shape[0]
    panels = k // PANEL
    row_id = lax.broadcasted_iota(jnp.int32, (PANEL, LANES), 0)
    scale = 1.0 / total_rows
    upper = [gram_ref[m * PANEL:(m + 1) * PANEL, :] * scale for m in range(panels)]
    inverse = []
    for m in range(panels):
        r = lax.broadcasted_iota(jnp.int32, (PANEL, k), 0) + m * PANEL
        inverse.append((r == lax.broadcasted_iota(jnp.int32, (PANEL, k), 1)).astype(jnp.float32))
    for p in range(panels):
        start = p * PANEL
        s_lo = start // LANES * LANES
        w_hi = (start + PANEL + LANES - 1) // LANES * LANES
        s, w = upper[p][:, s_lo:], inverse[p][:, :w_hi]
        columns = [
            jnp.broadcast_to(s[:, start - s_lo + t:start - s_lo + t + 1], (PANEL, LANES))
            for t in range(PANEL)
        ]
        pivots = jnp.zeros((PANEL, LANES), jnp.float32)
        for t in range(PANEL):
            column = columns[t]
            pivot_inv = 1.0 / column[t:t + 1, :]
            pivots = jnp.where(row_id == t, column, pivots)
            if t == PANEL - 1:
                break
            below = jnp.where(row_id > t, column, 0.0)
            for j in range(t + 1, PANEL):
                columns[j] = columns[j] - below * (column[j:j + 1, :] * pivot_inv)
            ratio = below * pivot_inv
            s = s - widen(ratio, s.shape[1]) * s[t:t + 1, :]
            w = w - widen(ratio, w.shape[1]) * w[t:t + 1, :]
        root = lax.rsqrt(pivots)
        s = s * widen(root, s.shape[1])
        w = w * widen(root, w.shape[1])
        inverse_ref[start:start + PANEL, :w_hi] = w
        if w_hi < k:
            inverse_ref[start:start + PANEL, w_hi:] = jnp.zeros((PANEL, k - w_hi), jnp.float32)
        if p == panels - 1:
            break
        st = s.T
        for lo, hi in ((p + 1, p + 2), (p + 2, panels)):
            if lo >= hi:
                continue
            left = st[lo * PANEL - s_lo:hi * PANEL - s_lo, :]
            s_lo2 = lo * PANEL // LANES * LANES
            ds = jnp.dot(left, s[:, s_lo2 - s_lo:], precision=HI, preferred_element_type=jnp.float32)
            dw = jnp.dot(left, w, precision=HI, preferred_element_type=jnp.float32)
            for m in range(lo, hi):
                o = (m - lo) * PANEL
                a = upper[m][:, s_lo2:] - ds[o:o + PANEL, :]
                upper[m] = a if s_lo2 == 0 else jnp.concatenate([upper[m][:, :s_lo2], a], 1)
                b = inverse[m][:, :w_hi] - dw[o:o + PANEL, :]
                inverse[m] = b if w_hi == k else jnp.concatenate([b, inverse[m][:, w_hi:]], 1)
    inv = inverse_ref[...]
    nt = (((1,), (1,)), ((), ()))
    orbitals_ref[...] = lax.dot_general(y_ref[...], inv, nt, precision=HI, preferred_element_type=jnp.float32)
    half = jnp.dot(inv, cross_ref[...], precision=HI, preferred_element_type=jnp.float32)
    full = lax.dot_general(half, inv, nt, precision=HI, preferred_element_type=jnp.float32)
    projected_ref[...] = (full + full.T) * (0.5 * scale)

def finish(gram, cross, y, total_rows):
    k = gram.shape[0]
    f32 = jnp.float32
    return pl.pallas_call(
        functools.partial(finish_kernel, total_rows),
        out_shape=(jax.ShapeDtypeStruct(y.shape, f32), jax.ShapeDtypeStruct((k, k), f32)),
        in_specs=[pl.BlockSpec(memory_space=pltpu.VMEM)] * 3,
        out_specs=(pl.BlockSpec(memory_space=pltpu.VMEM),) * 2,
        scratch_shapes=[pltpu.VMEM((k, k), f32)],
        compiler_params=pltpu.CompilerParams(vmem_limit_bytes=32 * 1024 * 1024),
        name="finish",
    )(gram, cross, y)


def core_swap(x, rows):
    return lax.ppermute(x, "row", [(i, i ^ 1) for i in range(rows)])


def local(orbitals_in, hblocks, block_cols, live_counts, onsite, cut_low, top_bound):
    rows = lax.axis_size("row")
    cols = lax.axis_size("col")
    chips = rows // 2
    row = lax.axis_index("row")
    col = lax.axis_index("col")
    core = row % 2
    row_blocks, slots, _ = hblocks.shape
    k = orbitals_in.shape[1]
    local_rows = PB * BS
    total_rows = rows * cols * local_rows
    same_core = [[2 * q + j for q in range(chips)] for j in range(2)]
    line = [[q * 2 * cols + i for i in range(2 * cols)] for q in range(chips)]

    def gather_rows(v):
        return lax.all_gather(v, ("row", "col"), axis_index_groups=line, axis=0, tiled=True)

    def swap_chips(x):
        return lax.all_to_all(x, "row", 0, 0, axis_index_groups=same_core)

    first_gathered = gather_rows(orbitals_in.astype(jnp.bfloat16))

    live = jnp.arange(slots, dtype=jnp.int32)[None, :] < live_counts
    codes = jnp.where(live, block_cols, -1)

    own_raw = lax.all_to_all(hblocks.reshape(cols, PB, slots, BS * BS), "col", 0, 0)
    own_codes = lax.all_to_all(codes.reshape(cols, PB, slots), "col", 0, 0)

    def selector(code):
        place = jnp.arange(rows * PB, dtype=jnp.int32)
        return (code[..., None] == place).astype(jnp.bfloat16)

    sel = selector(codes).reshape(row_blocks, slots, chips, 2, PB)
    mirrored = jnp.einsum(
        "isqjm,isab->jqmbia",
        sel,
        hblocks.reshape(row_blocks, slots, BS, BS),
        preferred_element_type=jnp.float32,
    ).astype(jnp.bfloat16)
    mirrored = mirrored.reshape(2, chips * local_rows, cols * local_rows)
    kept = lax.dynamic_index_in_dim(mirrored, core, 0, keepdims=False)
    other = core_swap(lax.dynamic_index_in_dim(mirrored, 1 - core, 0, keepdims=False), rows)
    mirrored = jnp.concatenate(
        [jnp.where(core == 0, kept, other), jnp.where(core == 0, other, kept)], 1
    )

    sel = selector(own_codes).reshape(cols, PB, slots, rows, PB)
    direct = jnp.einsum(
        "cpsnm,cpsab->npacmb",
        sel,
        own_raw.reshape(cols, PB, slots, BS, BS),
        preferred_element_type=jnp.float32,
    ).astype(jnp.bfloat16)
    direct = direct.reshape(chips, 2, local_rows, cols * local_rows)
    direct = swap_chips(jnp.concatenate([direct[:, 0], direct[:, 1]], 2))
    tile = mirrored + direct.reshape(chips * local_rows, 2 * cols * local_rows)

    onsite_blocks = onsite.reshape(PB, BS, BS)
    diagonal = jnp.concatenate(
        [jnp.pad(onsite_blocks[p], ((0, 0), (p * BS, (PB - 1 - p) * BS))) for p in range(PB)], 0
    )
    at = (row // 2 * local_rows, (core * cols + col) * local_rows)
    tile = tile + lax.dynamic_update_slice(jnp.zeros_like(tile), diagonal, at)

    def partial_product(gathered):
        return jnp.dot(tile, gathered, preferred_element_type=jnp.float32)

    def apply(gathered):
        terms = partial_product(gathered).reshape(chips, local_rows, k)
        return jnp.sum(swap_chips(terms), 0)

    centre = 0.5 * (top_bound[0] + cut_low[0])
    halfwidth = 0.5 * (top_bound[0] - cut_low[0])
    previous = orbitals_in
    current = (apply(first_gathered) - centre * orbitals_in) / halfwidth
    for degree in range(DEG - 1):
        gathered = gather_rows(current.astype(jnp.bfloat16))
        following = 2.0 * (apply(gathered) - centre * current) / halfwidth - previous
        previous, current = (current, following)

    rounded = current.astype(jnp.bfloat16)
    gathered = gather_rows(rounded)
    contract = (((0,), (0,)), ((), ()))
    plane_rows = lax.all_gather(rounded, "row", axis_index_groups=same_core, axis=0, tiled=True)
    gram_part = lax.dot_general(plane_rows, plane_rows, contract, preferred_element_type=jnp.float32)
    cross_part = lax.dot_general(
        plane_rows.astype(jnp.float32), partial_product(gathered), contract, precision=HI
    )

    share = k // rows
    parts = jnp.stack([gram_part / chips, cross_part]).reshape(2, rows, share, k)
    parts = jnp.sum(lax.all_to_all(parts, "row", 1, 1), 1)
    total = parts
    for s in range(1, cols):
        total = total + lax.ppermute(parts, "col", [(i, (i + s) % cols) for i in range(cols)])
    both = lax.all_gather(total, "row", axis=1, tiled=True)
    return finish(both[0], both[1], current, total_rows)


def solution(mesh):
    placed = (
        P(("row", "col"), None),
        P("row", "col", None),
        P("row", "col"),
        P("row", "col"),
        P(("row", "col"), None),
        P(),
        P(),
    )
    return jax.shard_map(
        local, mesh=mesh, in_specs=placed, out_specs=(P(("row", "col"), None), P()), check_vma=False
    )
```

```python
import functools

import jax
import jax.numpy as jnp
from jax import lax
from jax.experimental import pallas as pl
from jax.experimental.pallas import tpu as pltpu
from jax.sharding import PartitionSpec as P

BS = 64
PB = 2
DEG = 3
LANES = 128
PANEL = 32
HI = lax.Precision.HIGHEST
VMEM = pl.BlockSpec(memory_space=pltpu.VMEM)
SMEM = pl.BlockSpec(memory_space=pltpu.SMEM)


def widen(x, width):
    return jnp.concatenate([x] * (width // LANES), 1) if width > LANES else x

def finish_kernel(total_rows, packed_ref, diagonal_ref, y_ref, orbitals_ref, projected_ref, inverse_ref):
    k = packed_ref.shape[0]
    panels = k // PANEL
    packed = packed_ref[...]
    flipped = packed.T
    above = lax.broadcasted_iota(jnp.int32, (k, k), 0) - lax.broadcasted_iota(jnp.int32, (k, k), 1)
    gram = jnp.where(above <= 0, packed, flipped)
    cross = jnp.where(above > 0, packed, jnp.where(above < 0, flipped, diagonal_ref[...]))
    row_id = lax.broadcasted_iota(jnp.int32, (PANEL, LANES), 0)
    scale = 1.0 / total_rows
    upper = [gram[m * PANEL:(m + 1) * PANEL, :] * scale for m in range(panels)]
    inverse = []
    for m in range(panels):
        r = lax.broadcasted_iota(jnp.int32, (PANEL, k), 0) + m * PANEL
        inverse.append((r == lax.broadcasted_iota(jnp.int32, (PANEL, k), 1)).astype(jnp.float32))
    for p in range(panels):
        start = p * PANEL
        s_lo = start // LANES * LANES
        w_hi = (start + PANEL + LANES - 1) // LANES * LANES
        s, w = upper[p][:, s_lo:], inverse[p][:, :w_hi]
        columns = [
            jnp.broadcast_to(s[:, start - s_lo + t:start - s_lo + t + 1], (PANEL, LANES))
            for t in range(PANEL)
        ]
        pivots = jnp.zeros((PANEL, LANES), jnp.float32)
        for t in range(PANEL):
            column = columns[t]
            pivot_inv = 1.0 / column[t:t + 1, :]
            pivots = jnp.where(row_id == t, column, pivots)
            if t == PANEL - 1:
                break
            below = jnp.where(row_id > t, column, 0.0)
            for j in range(t + 1, PANEL):
                columns[j] = columns[j] - below * (column[j:j + 1, :] * pivot_inv)
            ratio = below * pivot_inv
            s = s - widen(ratio, s.shape[1]) * s[t:t + 1, :]
            w = w - widen(ratio, w.shape[1]) * w[t:t + 1, :]
        root = lax.rsqrt(pivots)
        s = s * widen(root, s.shape[1])
        w = w * widen(root, w.shape[1])
        inverse_ref[start:start + PANEL, :w_hi] = w
        if w_hi < k:
            inverse_ref[start:start + PANEL, w_hi:] = jnp.zeros((PANEL, k - w_hi), jnp.float32)
        if p == panels - 1:
            break
        st = s.T
        for lo, hi in ((p + 1, p + 2), (p + 2, panels)):
            if lo >= hi:
                continue
            left = st[lo * PANEL - s_lo:hi * PANEL - s_lo, :]
            s_lo2 = lo * PANEL // LANES * LANES
            ds = jnp.dot(left, s[:, s_lo2 - s_lo:], precision=HI, preferred_element_type=jnp.float32)
            dw = jnp.dot(left, w, precision=HI, preferred_element_type=jnp.float32)
            for m in range(lo, hi):
                o = (m - lo) * PANEL
                a = upper[m][:, s_lo2:] - ds[o:o + PANEL, :]
                upper[m] = a if s_lo2 == 0 else jnp.concatenate([upper[m][:, :s_lo2], a], 1)
                b = inverse[m][:, :w_hi] - dw[o:o + PANEL, :]
                inverse[m] = b if w_hi == k else jnp.concatenate([b, inverse[m][:, w_hi:]], 1)
    inv = inverse_ref[...]
    nt = (((1,), (1,)), ((), ()))
    orbitals_ref[...] = lax.dot_general(y_ref[...], inv, nt, precision=HI, preferred_element_type=jnp.float32)
    half = jnp.dot(inv, cross, precision=HI, preferred_element_type=jnp.float32)
    full = lax.dot_general(half, inv, nt, precision=HI, preferred_element_type=jnp.float32)
    projected_ref[...] = full * (0.5 * scale)

def finish(packed, diagonal, y, total_rows):
    k = packed.shape[0]
    f32 = jnp.float32
    return pl.pallas_call(
        functools.partial(finish_kernel, total_rows),
        out_shape=(jax.ShapeDtypeStruct(y.shape, f32), jax.ShapeDtypeStruct((k, k), f32)),
        in_specs=[pl.BlockSpec(memory_space=pltpu.VMEM)] * 3,
        out_specs=(pl.BlockSpec(memory_space=pltpu.VMEM),) * 2,
        scratch_shapes=[pltpu.VMEM((k, k), f32)],
        compiler_params=pltpu.CompilerParams(vmem_limit_bytes=32 * 1024 * 1024),
        name="finish",
    )(packed, diagonal, y)


def shifted(x, axis, size, step):
    return lax.ppermute(x, axis, [(i, (i + step) % size) for i in range(size)])


def core_swap(x, rows):
    return lax.ppermute(x, "row", [(i, i ^ 1) for i in range(rows)])


def chip_shifted(x, rows, step):
    return lax.ppermute(x, "row", [(i, (i + 2 * step) % rows) for i in range(rows)])


def pack_kernel(col_ref, blocks_ref, places_ref, *piece_refs):
    cols = len(piece_refs)
    for s, piece in enumerate(piece_refs):
        owner = lax.rem(col_ref[0] + s, cols)
        piece[:, : BS * BS] = blocks_ref[owner]
        piece[:, BS * BS :] = places_ref[owner]


def pack(col, blocks, places):
    cols, height, _ = blocks.shape
    shape = jax.ShapeDtypeStruct((height, BS * BS + LANES), jnp.bfloat16)
    return pl.pallas_call(
        pack_kernel,
        out_shape=(shape,) * cols,
        in_specs=[SMEM, VMEM, VMEM],
        out_specs=(VMEM,) * cols,
        name="pack",
    )(col, blocks, places)


def unflatten(flat_ref, square_ref, groups):
    lower = lax.broadcasted_iota(jnp.int32, (groups, LANES), 1) < BS
    for h in range(BS * BS // LANES):
        even = flat_ref[:groups, h * LANES : (h + 1) * LANES]
        odd = flat_ref[groups:, h * LANES : (h + 1) * LANES]
        first = jnp.where(lower, even, pltpu.roll(odd, BS, 1))
        second = jnp.where(lower, pltpu.roll(even, BS, 1), odd)
        square_ref[pl.ds(2 * h, groups, stride=BS), :] = first
        square_ref[pl.ds(2 * h + 1, groups, stride=BS), :] = second


def mirror_kernel(key_ref, blocks_ref, near_ref, far_ref, flat_ref, square_ref):
    height = near_ref.shape[1]
    groups = square_ref.shape[0] // BS
    places = lax.broadcasted_iota(jnp.int32, (2 * groups, key_ref.shape[1]), 0)
    chosen = (places == key_ref[...]).astype(jnp.float32).astype(jnp.bfloat16)
    flat_ref[...] = jnp.dot(chosen, blocks_ref[...], preferred_element_type=jnp.float32)
    unflatten(flat_ref, square_ref, groups)
    devices = square_ref.shape[0] // height
    for d in range(devices):
        out = near_ref if d < devices // 2 else far_ref
        at = d % (devices // 2) * LANES
        square = square_ref[d * height : (d + 1) * height, :]
        out[at : at + LANES, :] = square.T.astype(jnp.bfloat16)


def mirror(key, blocks, rows, row_blocks):
    half = (rows // 2 * PB * BS, row_blocks * BS)
    groups = rows * row_blocks
    return pl.pallas_call(
        mirror_kernel,
        out_shape=(jax.ShapeDtypeStruct(half, jnp.bfloat16),) * 2,
        in_specs=[VMEM, VMEM],
        out_specs=(VMEM, VMEM),
        scratch_shapes=[
            pltpu.VMEM((2 * groups, BS * BS), jnp.float32),
            pltpu.VMEM((groups * BS, LANES), jnp.float32),
        ],
        compiler_params=pltpu.CompilerParams(vmem_limit_bytes=40 * 1024 * 1024),
        name="mirror",
    )(key, blocks)


def direct_kernel(rows, slots, *refs):
    cols = len(refs) - 3 - rows // 2
    piece_refs, onsite_ref = refs[:cols], refs[cols]
    out_refs, (flat_ref, square_ref) = refs[cols + 1 : -2], refs[-2:]
    row_blocks = cols * PB
    groups = rows * row_blocks
    total = jnp.zeros((2 * groups, BS * BS), jnp.float32)
    for s, piece in enumerate(piece_refs):
        height = piece.shape[0]
        place = piece[0:1, BS * BS : BS * BS + height].astype(jnp.float32).astype(jnp.int32)
        block = lax.broadcasted_iota(jnp.int32, (1, height), 1) // slots
        key = place % 2 * groups + place // 2 * row_blocks + s * PB + block
        key = jnp.where(place < 0, -1, key)
        ids = lax.broadcasted_iota(jnp.int32, (2 * groups, height), 0)
        chosen = (ids == key).astype(jnp.float32).astype(jnp.bfloat16)
        total += jnp.dot(chosen, piece[:, : BS * BS], preferred_element_type=jnp.float32)
    flat_ref[...] = total
    for p in range(PB):
        at = p * groups + p
        flat_ref[at : at + 1, :] += onsite_ref[p : p + 1, :].astype(jnp.float32)
    unflatten(flat_ref, square_ref, groups)
    for chip, out in enumerate(out_refs):
        for g in range(2 * cols):
            at = (chip * 2 * cols + g) * LANES
            out[:, g * LANES : (g + 1) * LANES] = square_ref[at : at + LANES, :].astype(
                jnp.bfloat16
            )


def direct_rows(pieces, onsite, rows, slots):
    cols = len(pieces)
    groups = rows * cols * PB
    shape = jax.ShapeDtypeStruct((PB * BS, 2 * cols * LANES), jnp.bfloat16)
    return pl.pallas_call(
        functools.partial(direct_kernel, rows, slots),
        out_shape=(shape,) * (rows // 2),
        in_specs=[VMEM] * (cols + 1),
        out_specs=(VMEM,) * (rows // 2),
        scratch_shapes=[
            pltpu.VMEM((2 * groups, BS * BS), jnp.float32),
            pltpu.VMEM((groups * BS, LANES), jnp.float32),
        ],
        compiler_params=pltpu.CompilerParams(vmem_limit_bytes=48 * 1024 * 1024),
        name="direct_rows",
    )(*pieces, onsite)


def local(orbitals_in, hblocks, block_cols, live_counts, onsite, cut_low, top_bound):
    rows = lax.axis_size("row")
    cols = lax.axis_size("col")
    chips = rows // 2
    row = lax.axis_index("row")
    col = lax.axis_index("col")
    chip, core = row // 2, row % 2
    row_blocks, slots, _ = hblocks.shape
    k = orbitals_in.shape[1]
    local_rows = PB * BS
    total_rows = rows * cols * local_rows
    near_rows = cols * local_rows

    live = jnp.arange(slots, dtype=jnp.int32)[None, :] < live_counts
    device, block = block_cols // PB, block_cols % PB
    apart = (device % 2) ^ core
    ahead = (device // 2 - chip) % chips
    places = jnp.where(live, (ahead * 2 + apart) * PB + block, -1).astype(jnp.bfloat16)
    places = places.reshape(cols, 1, PB * slots)
    places = jnp.pad(places, ((0, 0), (0, PB * slots - 1), (0, LANES - PB * slots)))
    block_row = jnp.arange(row_blocks, dtype=jnp.int32)[:, None]
    near_row = (col - block_row // PB) % cols * PB + block_row % PB
    behind = (chips - ahead) % chips
    groups = rows * row_blocks
    key = block * groups + (apart * chips + behind) * row_blocks + near_row
    key = jnp.where(live, key, -1).reshape(1, row_blocks * slots)

    pieces = pack(col[None], hblocks.reshape(cols, PB * slots, BS * BS), places)
    pieces = [shifted(pieces[s], "col", cols, s) if s else pieces[s] for s in range(cols)]

    def gather_rows(v):
        near = jnp.concatenate([v] + [shifted(v, "col", cols, s) for s in range(1, cols)], 0)
        return near, core_swap(near, rows)

    near, far = mirror(key, hblocks.reshape(row_blocks * slots, BS * BS), rows, row_blocks)
    far = core_swap(far, rows)

    direct = direct_rows(pieces, onsite, rows, slots)
    direct = [chip_shifted(direct[s], rows, s) if s else direct[s] for s in range(chips)]
    first_gathered = gather_rows(orbitals_in.astype(jnp.bfloat16))
    tile = jnp.concatenate([near, far], 1) + jnp.concatenate(direct, 0)
    tile_near, tile_far = tile[:, :near_rows], tile[:, near_rows:]

    def partial_product(gathered):
        near, far = gathered
        return jnp.dot(tile_near, near, preferred_element_type=jnp.float32) + jnp.dot(
            tile_far, far, preferred_element_type=jnp.float32
        )

    def apply(gathered):
        terms = partial_product(gathered).reshape(chips, local_rows, k)
        total = terms[0]
        for s in range(1, chips):
            total = total + chip_shifted(terms[s], rows, chips - s)
        return total

    centre = 0.5 * (top_bound[0] + cut_low[0])
    halfwidth = 0.5 * (top_bound[0] - cut_low[0])
    previous = orbitals_in
    current = (apply(first_gathered) - centre * orbitals_in) / halfwidth
    for degree in range(DEG - 1):
        gathered = gather_rows(current.astype(jnp.bfloat16))
        following = 2.0 * (apply(gathered) - centre * current) / halfwidth - previous
        previous, current = (current, following)

    rounded = current.astype(jnp.bfloat16)
    plane_rows = jnp.concatenate(
        [rounded] + [chip_shifted(rounded, rows, s) for s in range(1, chips)], 0
    )
    gathered = gather_rows(rounded)
    contract = (((0,), (0,)), ((), ()))
    gram_part = lax.dot_general(
        gathered[0], gathered[0], contract, preferred_element_type=jnp.float32
    ) / cols
    cross_part = lax.dot_general(
        plane_rows.astype(jnp.float32), partial_product(gathered), contract, precision=HI
    )

    share = k // rows
    cross_part = cross_part + cross_part.T
    ids = jnp.arange(k, dtype=jnp.int32)
    packed = jnp.where(ids[:, None] <= ids[None, :], gram_part, cross_part)
    diagonal = jnp.sum(jnp.where(ids[:, None] == ids[None, :], cross_part, 0.0), 0)
    diagonal = jnp.broadcast_to(diagonal, (rows, 8, k))
    parts = jnp.concatenate([packed.reshape(rows, share, k), diagonal], 1)
    parts = jnp.sum(lax.all_to_all(parts, "row", 0, 0), 0)
    total = parts
    for s in range(1, cols):
        total = total + shifted(parts, "col", cols, s)
    both = lax.all_gather(total, "row", axis=0, tiled=False)
    packed = both[:, :share].reshape(k, k)
    return finish(packed, both[0, share : share + 1], current, total_rows)


def solution(mesh):
    placed = (
        P(("row", "col"), None),
        P("row", "col", None),
        P("row", "col"),
        P("row", "col"),
        P(("row", "col"), None),
        P(),
        P(),
    )
    return jax.shard_map(
        local, mesh=mesh, in_specs=placed, out_specs=(P(("row", "col"), None), P()), check_vma=False
    )
```

```python
import functools

import jax
import jax.numpy as jnp
from jax import lax
from jax.experimental import pallas as pl
from jax.experimental.pallas import tpu as pltpu
from jax.sharding import PartitionSpec as P

BS = 64
PB = 2
DEG = 3
LANES = 128
PANEL = 32
HI = lax.Precision.HIGHEST
VMEM = pl.BlockSpec(memory_space=pltpu.VMEM)
SMEM = pl.BlockSpec(memory_space=pltpu.SMEM)


def widen(x, width):
    return jnp.concatenate([x] * (width // LANES), 1) if width > LANES else x

def finish_kernel(total_rows, packed_ref, diagonal_ref, y_ref, orbitals_ref, projected_ref, inverse_ref):
    k = packed_ref.shape[0]
    panels = k // PANEL
    packed = packed_ref[...]
    flipped = packed.T
    above = lax.broadcasted_iota(jnp.int32, (k, k), 0) - lax.broadcasted_iota(jnp.int32, (k, k), 1)
    gram = jnp.where(above <= 0, packed, flipped)
    cross = jnp.where(above > 0, packed, jnp.where(above < 0, flipped, diagonal_ref[...]))
    row_id = lax.broadcasted_iota(jnp.int32, (PANEL, LANES), 0)
    scale = 1.0 / total_rows
    upper = [gram[m * PANEL:(m + 1) * PANEL, :] * scale for m in range(panels)]
    inverse = []
    for m in range(panels):
        r = lax.broadcasted_iota(jnp.int32, (PANEL, k), 0) + m * PANEL
        inverse.append((r == lax.broadcasted_iota(jnp.int32, (PANEL, k), 1)).astype(jnp.float32))
    for p in range(panels):
        start = p * PANEL
        s_lo = start // LANES * LANES
        w_hi = (start + PANEL + LANES - 1) // LANES * LANES
        s, w = upper[p][:, s_lo:], inverse[p][:, :w_hi]
        columns = [
            jnp.broadcast_to(s[:, start - s_lo + t:start - s_lo + t + 1], (PANEL, LANES))
            for t in range(PANEL)
        ]
        pivots = jnp.zeros((PANEL, LANES), jnp.float32)
        for t in range(PANEL):
            column = columns[t]
            pivot_inv = 1.0 / column[t:t + 1, :]
            pivots = jnp.where(row_id == t, column, pivots)
            if t == PANEL - 1:
                break
            below = jnp.where(row_id > t, column, 0.0)
            for j in range(t + 1, PANEL):
                columns[j] = columns[j] - below * (column[j:j + 1, :] * pivot_inv)
            ratio = below * pivot_inv
            s = s - widen(ratio, s.shape[1]) * s[t:t + 1, :]
            w = w - widen(ratio, w.shape[1]) * w[t:t + 1, :]
        root = lax.rsqrt(pivots)
        s = s * widen(root, s.shape[1])
        w = w * widen(root, w.shape[1])
        inverse_ref[start:start + PANEL, :w_hi] = w
        if w_hi < k:
            inverse_ref[start:start + PANEL, w_hi:] = jnp.zeros((PANEL, k - w_hi), jnp.float32)
        if p == panels - 1:
            break
        st = s.T
        for lo, hi in ((p + 1, p + 2), (p + 2, panels)):
            if lo >= hi:
                continue
            left = st[lo * PANEL - s_lo:hi * PANEL - s_lo, :]
            s_lo2 = lo * PANEL // LANES * LANES
            ds = jnp.dot(left, s[:, s_lo2 - s_lo:], precision=HI, preferred_element_type=jnp.float32)
            dw = jnp.dot(left, w, precision=HI, preferred_element_type=jnp.float32)
            for m in range(lo, hi):
                o = (m - lo) * PANEL
                a = upper[m][:, s_lo2:] - ds[o:o + PANEL, :]
                upper[m] = a if s_lo2 == 0 else jnp.concatenate([upper[m][:, :s_lo2], a], 1)
                b = inverse[m][:, :w_hi] - dw[o:o + PANEL, :]
                inverse[m] = b if w_hi == k else jnp.concatenate([b, inverse[m][:, w_hi:]], 1)
    inv = inverse_ref[...]
    nt = (((1,), (1,)), ((), ()))
    orbitals_ref[...] = lax.dot_general(y_ref[...], inv, nt, precision=HI, preferred_element_type=jnp.float32)
    half = jnp.dot(inv, cross, precision=HI, preferred_element_type=jnp.float32)
    full = lax.dot_general(half, inv, nt, precision=HI, preferred_element_type=jnp.float32)
    projected_ref[...] = full * (0.5 * scale)

def finish(packed, diagonal, y, total_rows):
    k = packed.shape[0]
    f32 = jnp.float32
    return pl.pallas_call(
        functools.partial(finish_kernel, total_rows),
        out_shape=(jax.ShapeDtypeStruct(y.shape, f32), jax.ShapeDtypeStruct((k, k), f32)),
        in_specs=[pl.BlockSpec(memory_space=pltpu.VMEM)] * 3,
        out_specs=(pl.BlockSpec(memory_space=pltpu.VMEM),) * 2,
        scratch_shapes=[pltpu.VMEM((k, k), f32)],
        compiler_params=pltpu.CompilerParams(vmem_limit_bytes=32 * 1024 * 1024),
        name="finish",
    )(packed, diagonal, y)


def shifted(x, axis, size, step):
    return lax.ppermute(x, axis, [(i, (i + step) % size) for i in range(size)])


def exchanged(x, axis, size, bit):
    return lax.ppermute(x, axis, [(i, i ^ bit) for i in range(size)])


def core_swap(x, rows):
    return exchanged(x, "row", rows, 1)


def chip_shifted(x, rows, step):
    return lax.ppermute(x, "row", [(i, (i + 2 * step) % rows) for i in range(rows)])


def pack_kernel(col_ref, blocks_ref, places_ref, *piece_refs):
    cols = len(piece_refs)
    for s, piece in enumerate(piece_refs):
        owner = lax.rem(col_ref[0] + s, cols)
        piece[:, : BS * BS] = blocks_ref[owner]
        piece[:, BS * BS :] = places_ref[owner]


def pack(col, blocks, places):
    cols, height, _ = blocks.shape
    shape = jax.ShapeDtypeStruct((height, BS * BS + LANES), jnp.bfloat16)
    return pl.pallas_call(
        pack_kernel,
        out_shape=(shape,) * cols,
        in_specs=[SMEM, VMEM, VMEM],
        out_specs=(VMEM,) * cols,
        name="pack",
    )(col, blocks, places)


def unflatten(flat_ref, square_ref, groups):
    lower = lax.broadcasted_iota(jnp.int32, (groups, LANES), 1) < BS
    for h in range(BS * BS // LANES):
        even = flat_ref[:groups, h * LANES : (h + 1) * LANES]
        odd = flat_ref[groups:, h * LANES : (h + 1) * LANES]
        first = jnp.where(lower, even, pltpu.roll(odd, BS, 1))
        second = jnp.where(lower, pltpu.roll(even, BS, 1), odd)
        square_ref[pl.ds(2 * h, groups, stride=BS), :] = first
        square_ref[pl.ds(2 * h + 1, groups, stride=BS), :] = second


def mirror_kernel(key_ref, blocks_ref, near_ref, far_ref, flat_ref, square_ref):
    height = near_ref.shape[1]
    groups = square_ref.shape[0] // BS
    places = lax.broadcasted_iota(jnp.int32, (2 * groups, key_ref.shape[1]), 0)
    chosen = (places == key_ref[...]).astype(jnp.float32).astype(jnp.bfloat16)
    flat_ref[...] = jnp.dot(chosen, blocks_ref[...], preferred_element_type=jnp.float32)
    unflatten(flat_ref, square_ref, groups)
    devices = square_ref.shape[0] // height
    for d in range(devices):
        out = near_ref if d < devices // 2 else far_ref
        at = d % (devices // 2) * LANES
        square = square_ref[d * height : (d + 1) * height, :]
        out[at : at + LANES, :] = square.T.astype(jnp.bfloat16)


def mirror(key, blocks, rows, row_blocks):
    half = (rows // 2 * PB * BS, row_blocks * BS)
    groups = rows * row_blocks
    return pl.pallas_call(
        mirror_kernel,
        out_shape=(jax.ShapeDtypeStruct(half, jnp.bfloat16),) * 2,
        in_specs=[VMEM, VMEM],
        out_specs=(VMEM, VMEM),
        scratch_shapes=[
            pltpu.VMEM((2 * groups, BS * BS), jnp.float32),
            pltpu.VMEM((groups * BS, LANES), jnp.float32),
        ],
        compiler_params=pltpu.CompilerParams(vmem_limit_bytes=40 * 1024 * 1024),
        cost_estimate=pl.CostEstimate(
            flops=4 * groups * blocks.size, bytes_accessed=3 * blocks.size, transcendentals=0
        ),
        name="mirror",
    )(key, blocks)


def direct_kernel(rows, slots, *refs):
    cols = len(refs) - 3 - rows // 2
    piece_refs, onsite_ref = refs[:cols], refs[cols]
    out_refs, (flat_ref, square_ref) = refs[cols + 1 : -2], refs[-2:]
    row_blocks = cols * PB
    groups = rows * row_blocks
    total = jnp.zeros((2 * groups, BS * BS), jnp.float32)
    for s, piece in enumerate(piece_refs):
        height = piece.shape[0]
        place = piece[0:1, BS * BS : BS * BS + height].astype(jnp.float32).astype(jnp.int32)
        block = lax.broadcasted_iota(jnp.int32, (1, height), 1) // slots
        key = place % 2 * groups + place // 2 * row_blocks + s * PB + block
        key = jnp.where(place < 0, -1, key)
        ids = lax.broadcasted_iota(jnp.int32, (2 * groups, height), 0)
        chosen = (ids == key).astype(jnp.float32).astype(jnp.bfloat16)
        total += jnp.dot(chosen, piece[:, : BS * BS], preferred_element_type=jnp.float32)
    flat_ref[...] = total
    for p in range(PB):
        at = p * groups + p
        flat_ref[at : at + 1, :] += onsite_ref[p : p + 1, :].astype(jnp.float32)
    unflatten(flat_ref, square_ref, groups)
    for chip, out in enumerate(out_refs):
        for g in range(2 * cols):
            at = (chip * 2 * cols + g) * LANES
            out[:, g * LANES : (g + 1) * LANES] = square_ref[at : at + LANES, :].astype(
                jnp.bfloat16
            )


def direct_rows(pieces, onsite, rows, slots):
    cols = len(pieces)
    groups = rows * cols * PB
    shape = jax.ShapeDtypeStruct((PB * BS, 2 * cols * LANES), jnp.bfloat16)
    return pl.pallas_call(
        functools.partial(direct_kernel, rows, slots),
        out_shape=(shape,) * (rows // 2),
        in_specs=[VMEM] * (cols + 1),
        out_specs=(VMEM,) * (rows // 2),
        scratch_shapes=[
            pltpu.VMEM((2 * groups, BS * BS), jnp.float32),
            pltpu.VMEM((groups * BS, LANES), jnp.float32),
        ],
        compiler_params=pltpu.CompilerParams(vmem_limit_bytes=48 * 1024 * 1024),
        name="direct_rows",
    )(*pieces, onsite)


def local(orbitals_in, hblocks, block_cols, live_counts, onsite, cut_low, top_bound):
    rows = lax.axis_size("row")
    cols = lax.axis_size("col")
    chips = rows // 2
    row = lax.axis_index("row")
    col = lax.axis_index("col")
    chip, core = row // 2, row % 2
    row_blocks, slots, _ = hblocks.shape
    k = orbitals_in.shape[1]
    local_rows = PB * BS
    total_rows = rows * cols * local_rows
    near_rows = cols * local_rows

    live = jnp.arange(slots, dtype=jnp.int32)[None, :] < live_counts
    device, block = block_cols // PB, block_cols % PB
    apart = (device % 2) ^ core
    ahead = (device // 2 - chip) % chips
    places = jnp.where(live, (ahead * 2 + apart) * PB + block, -1).astype(jnp.bfloat16)
    places = places.reshape(cols, 1, PB * slots)
    places = jnp.pad(places, ((0, 0), (0, PB * slots - 1), (0, LANES - PB * slots)))
    block_row = jnp.arange(row_blocks, dtype=jnp.int32)[:, None]
    near_row = (col - block_row // PB) % cols * PB + block_row % PB
    behind = (chips - ahead) % chips
    groups = rows * row_blocks
    key = block * groups + (apart * chips + behind) * row_blocks + near_row
    key = jnp.where(live, key, -1).reshape(1, row_blocks * slots)

    pieces = pack(col[None], hblocks.reshape(cols, PB * slots, BS * BS), places)
    key, pieces = lax.optimization_barrier((key, pieces))
    pieces = [shifted(pieces[s], "col", cols, s) if s else pieces[s] for s in range(cols)]

    def gather_near(v):
        return jnp.concatenate([v] + [shifted(v, "col", cols, s) for s in range(1, cols)], 0)

    def gather_rows(v):
        near = gather_near(v)
        return near, core_swap(near, rows)

    near, far = mirror(key, hblocks.reshape(row_blocks * slots, BS * BS), rows, row_blocks)
    far = core_swap(far, rows)

    direct = direct_rows(pieces, onsite, rows, slots)
    first, direct = lax.optimization_barrier((orbitals_in.astype(jnp.bfloat16), direct))
    direct = [chip_shifted(direct[s], rows, s) if s else direct[s] for s in range(chips)]
    first_gathered = gather_rows(first)
    tile = jnp.concatenate([near, far], 1) + jnp.concatenate(direct, 0)
    tile_near, tile_far = tile[:, :near_rows], tile[:, near_rows:]

    def partial_product(gathered):
        near, far = gathered
        return jnp.dot(tile_near, near, preferred_element_type=jnp.float32) + jnp.dot(
            tile_far, far, preferred_element_type=jnp.float32
        )

    def apply(gathered):
        terms = partial_product(gathered).reshape(chips, local_rows, k)
        total = terms[0]
        for s in range(1, chips):
            total = total + chip_shifted(terms[s], rows, chips - s)
        return total

    centre = 0.5 * (top_bound[0] + cut_low[0])
    halfwidth = 0.5 * (top_bound[0] - cut_low[0])
    previous = orbitals_in
    current = (apply(first_gathered) - centre * orbitals_in) / halfwidth
    for degree in range(DEG - 1):
        gathered = gather_rows(current.astype(jnp.bfloat16))
        following = 2.0 * (apply(gathered) - centre * current) / halfwidth - previous
        previous, current = (current, following)

    rounded = current.astype(jnp.bfloat16)
    plane_rows = jnp.concatenate(
        [rounded] + [chip_shifted(rounded, rows, s) for s in range(1, chips)], 0
    )
    near, plane_rows = lax.optimization_barrier((gather_near(rounded), plane_rows))
    gathered = near, core_swap(near, rows)
    contract = (((0,), (0,)), ((), ()))
    gram_part = lax.dot_general(
        gathered[0], gathered[0], contract, preferred_element_type=jnp.float32
    ) / cols
    cross_part = lax.dot_general(
        plane_rows.astype(jnp.float32), partial_product(gathered), contract, precision=HI
    )

    share = k // rows
    cross_part = cross_part + cross_part.T
    ids = jnp.arange(k, dtype=jnp.int32)
    packed = jnp.where(ids[:, None] <= ids[None, :], gram_part, cross_part)
    diagonal = jnp.sum(jnp.where(ids[:, None] == ids[None, :], cross_part, 0.0), 0)
    diagonal = jnp.broadcast_to(diagonal, (rows, 8, k))
    total = jnp.concatenate([packed.reshape(rows, share, k), diagonal], 1)
    bits = [1 << b for b in range(rows.bit_length() - 1)]
    for bit in bits:
        upper = (row // bit) % 2 == 1
        total = total.reshape(total.shape[0] // 2, 2, share + 8, k)
        sent = jnp.where(upper, total[:, 0], total[:, 1])
        kept = jnp.where(upper, total[:, 1], total[:, 0])
        total = kept + exchanged(sent, "row", rows, bit)
    total = total[0]
    for bit in [1 << b for b in range(cols.bit_length() - 1)]:
        total = total + exchanged(total, "col", cols, bit)
    total = total[None]
    for bit in reversed(bits):
        upper = (row // bit) % 2 == 1
        other = exchanged(total, "row", rows, bit)
        pair = (jnp.where(upper, other, total), jnp.where(upper, total, other))
        total = jnp.stack(pair, 1).reshape(2 * total.shape[0], share + 8, k)
    packed = total[:, :share].reshape(k, k)
    return finish(packed, total[0, share : share + 1], current, total_rows)


def solution(mesh):
    placed = (
        P(("row", "col"), None),
        P("row", "col", None),
        P("row", "col"),
        P("row", "col"),
        P(("row", "col"), None),
        P(),
        P(),
    )
    return jax.shard_map(
        local, mesh=mesh, in_specs=placed, out_specs=(P(("row", "col"), None), P()), check_vma=False
    )
```

```python
import functools

import jax
import jax.numpy as jnp
from jax import lax
from jax.experimental import pallas as pl
from jax.experimental.pallas import tpu as pltpu
from jax.sharding import PartitionSpec as P

BS = 64
PB = 2
DEG = 3
LANES = 128
PANEL = 32
HI = lax.Precision.HIGHEST
VMEM = pl.BlockSpec(memory_space=pltpu.VMEM)
SMEM = pl.BlockSpec(memory_space=pltpu.SMEM)


def widen(x, width):
    return jnp.concatenate([x] * (width // LANES), 1) if width > LANES else x

def finish_kernel(total_rows, packed_ref, diagonal_ref, y_ref, orbitals_ref, projected_ref, inverse_ref):
    k = packed_ref.shape[0]
    panels = k // PANEL
    packed = packed_ref[...]
    flipped = packed.T
    above = lax.broadcasted_iota(jnp.int32, (k, k), 0) - lax.broadcasted_iota(jnp.int32, (k, k), 1)
    gram = jnp.where(above <= 0, packed, flipped)
    cross = jnp.where(above > 0, packed, jnp.where(above < 0, flipped, diagonal_ref[...]))
    row_id = lax.broadcasted_iota(jnp.int32, (PANEL, LANES), 0)
    scale = 1.0 / total_rows
    upper = [gram[m * PANEL:(m + 1) * PANEL, :] * scale for m in range(panels)]
    inverse = []
    for m in range(panels):
        r = lax.broadcasted_iota(jnp.int32, (PANEL, k), 0) + m * PANEL
        inverse.append((r == lax.broadcasted_iota(jnp.int32, (PANEL, k), 1)).astype(jnp.float32))
    for p in range(panels):
        start = p * PANEL
        s_lo = start // LANES * LANES
        w_hi = (start + PANEL + LANES - 1) // LANES * LANES
        s, w = upper[p][:, s_lo:], inverse[p][:, :w_hi]
        columns = [
            jnp.broadcast_to(s[:, start - s_lo + t:start - s_lo + t + 1], (PANEL, LANES))
            for t in range(PANEL)
        ]
        pivots = jnp.zeros((PANEL, LANES), jnp.float32)
        for t in range(PANEL):
            column = columns[t]
            pivot_inv = 1.0 / column[t:t + 1, :]
            pivots = jnp.where(row_id == t, column, pivots)
            if t == PANEL - 1:
                break
            below = jnp.where(row_id > t, column, 0.0)
            for j in range(t + 1, PANEL):
                columns[j] = columns[j] - below * (column[j:j + 1, :] * pivot_inv)
            ratio = below * pivot_inv
            s = s - widen(ratio, s.shape[1]) * s[t:t + 1, :]
            w = w - widen(ratio, w.shape[1]) * w[t:t + 1, :]
        root = lax.rsqrt(pivots)
        s = s * widen(root, s.shape[1])
        w = w * widen(root, w.shape[1])
        inverse_ref[start:start + PANEL, :w_hi] = w
        if w_hi < k:
            inverse_ref[start:start + PANEL, w_hi:] = jnp.zeros((PANEL, k - w_hi), jnp.float32)
        if p == panels - 1:
            break
        st = s.T
        for lo, hi in ((p + 1, p + 2), (p + 2, panels)):
            if lo >= hi:
                continue
            left = st[lo * PANEL - s_lo:hi * PANEL - s_lo, :]
            s_lo2 = lo * PANEL // LANES * LANES
            ds = jnp.dot(left, s[:, s_lo2 - s_lo:], precision=HI, preferred_element_type=jnp.float32)
            dw = jnp.dot(left, w, precision=HI, preferred_element_type=jnp.float32)
            for m in range(lo, hi):
                o = (m - lo) * PANEL
                a = upper[m][:, s_lo2:] - ds[o:o + PANEL, :]
                upper[m] = a if s_lo2 == 0 else jnp.concatenate([upper[m][:, :s_lo2], a], 1)
                b = inverse[m][:, :w_hi] - dw[o:o + PANEL, :]
                inverse[m] = b if w_hi == k else jnp.concatenate([b, inverse[m][:, w_hi:]], 1)
    inv = inverse_ref[...]
    nt = (((1,), (1,)), ((), ()))
    orbitals_ref[...] = lax.dot_general(y_ref[...], inv, nt, precision=HI, preferred_element_type=jnp.float32)
    half = jnp.dot(inv, cross, precision=HI, preferred_element_type=jnp.float32)
    full = lax.dot_general(half, inv, nt, precision=HI, preferred_element_type=jnp.float32)
    projected_ref[...] = full * (0.5 * scale)

def finish(packed, diagonal, y, total_rows):
    k = packed.shape[0]
    f32 = jnp.float32
    return pl.pallas_call(
        functools.partial(finish_kernel, total_rows),
        out_shape=(jax.ShapeDtypeStruct(y.shape, f32), jax.ShapeDtypeStruct((k, k), f32)),
        in_specs=[pl.BlockSpec(memory_space=pltpu.VMEM)] * 3,
        out_specs=(pl.BlockSpec(memory_space=pltpu.VMEM),) * 2,
        scratch_shapes=[pltpu.VMEM((k, k), f32)],
        compiler_params=pltpu.CompilerParams(vmem_limit_bytes=32 * 1024 * 1024),
        name="finish",
    )(packed, diagonal, y)


def exchanged(x, axis, size, apart):
    return lax.ppermute(x, axis, [(i, i ^ apart) for i in range(size)])


def core_swap(x, rows):
    return exchanged(x, "row", rows, 1)


def chip_swap(x, rows, apart):
    return exchanged(x, "row", rows, 2 * apart)


def by_distance(x, index):
    size = x.shape[0]
    bit = 1
    while bit < size:
        pairs = x.reshape(size // (2 * bit), 2, bit, *x.shape[1:])
        flipped = jnp.stack([pairs[:, 1], pairs[:, 0]], 1).reshape(x.shape)
        x = jnp.where((index // bit) % 2 == 1, flipped, x)
        bit *= 2
    return x


def pack_kernel(col_ref, blocks_ref, places_ref, *piece_refs):
    cols = len(piece_refs)
    for s, piece in enumerate(piece_refs):
        owner = jnp.bitwise_xor(col_ref[0], s)
        piece[:, : BS * BS] = blocks_ref[owner]
        piece[:, BS * BS :] = places_ref[owner]


def pack(col, blocks, places):
    cols, height, _ = blocks.shape
    shape = jax.ShapeDtypeStruct((height, BS * BS + LANES), jnp.bfloat16)
    return pl.pallas_call(
        pack_kernel,
        out_shape=(shape,) * cols,
        in_specs=[SMEM, VMEM, VMEM],
        out_specs=(VMEM,) * cols,
        name="pack",
    )(col, blocks, places)


def unflatten(flat_ref, square_ref, groups):
    lower = lax.broadcasted_iota(jnp.int32, (groups, LANES), 1) < BS
    for h in range(BS * BS // LANES):
        even = flat_ref[:groups, h * LANES : (h + 1) * LANES]
        odd = flat_ref[groups:, h * LANES : (h + 1) * LANES]
        first = jnp.where(lower, even, pltpu.roll(odd, BS, 1))
        second = jnp.where(lower, pltpu.roll(even, BS, 1), odd)
        square_ref[pl.ds(2 * h, groups, stride=BS), :] = first
        square_ref[pl.ds(2 * h + 1, groups, stride=BS), :] = second


def mirror_kernel(key_ref, blocks_ref, near_ref, far_ref, flat_ref, square_ref):
    height = near_ref.shape[1]
    groups = square_ref.shape[0] // BS
    places = lax.broadcasted_iota(jnp.int32, (2 * groups, key_ref.shape[1]), 0)
    chosen = (places == key_ref[...]).astype(jnp.float32).astype(jnp.bfloat16)
    flat_ref[...] = jnp.dot(chosen, blocks_ref[...], preferred_element_type=jnp.float32)
    unflatten(flat_ref, square_ref, groups)
    devices = square_ref.shape[0] // height
    for d in range(devices):
        out = near_ref if d < devices // 2 else far_ref
        at = d % (devices // 2) * LANES
        square = square_ref[d * height : (d + 1) * height, :]
        out[at : at + LANES, :] = square.T.astype(jnp.bfloat16)


def mirror(key, blocks, rows, row_blocks):
    half = (rows // 2 * PB * BS, row_blocks * BS)
    groups = rows * row_blocks
    return pl.pallas_call(
        mirror_kernel,
        out_shape=(jax.ShapeDtypeStruct(half, jnp.bfloat16),) * 2,
        in_specs=[VMEM, VMEM],
        out_specs=(VMEM, VMEM),
        scratch_shapes=[
            pltpu.VMEM((2 * groups, BS * BS), jnp.float32),
            pltpu.VMEM((groups * BS, LANES), jnp.float32),
        ],
        compiler_params=pltpu.CompilerParams(vmem_limit_bytes=40 * 1024 * 1024),
        cost_estimate=pl.CostEstimate(
            flops=4 * groups * blocks.size, bytes_accessed=3 * blocks.size, transcendentals=0
        ),
        name="mirror",
    )(key, blocks)


def direct_kernel(rows, slots, *refs):
    cols = len(refs) - 3 - rows // 2
    piece_refs, onsite_ref = refs[:cols], refs[cols]
    out_refs, (flat_ref, square_ref) = refs[cols + 1 : -2], refs[-2:]
    row_blocks = cols * PB
    groups = rows * row_blocks
    total = jnp.zeros((2 * groups, BS * BS), jnp.float32)
    for s, piece in enumerate(piece_refs):
        height = piece.shape[0]
        place = piece[0:1, BS * BS : BS * BS + height].astype(jnp.float32).astype(jnp.int32)
        block = lax.broadcasted_iota(jnp.int32, (1, height), 1) // slots
        key = place % 2 * groups + place // 2 * row_blocks + s * PB + block
        key = jnp.where(place < 0, -1, key)
        ids = lax.broadcasted_iota(jnp.int32, (2 * groups, height), 0)
        chosen = (ids == key).astype(jnp.float32).astype(jnp.bfloat16)
        total += jnp.dot(chosen, piece[:, : BS * BS], preferred_element_type=jnp.float32)
    flat_ref[...] = total
    for p in range(PB):
        at = p * groups + p
        flat_ref[at : at + 1, :] += onsite_ref[p : p + 1, :].astype(jnp.float32)
    unflatten(flat_ref, square_ref, groups)
    for chip, out in enumerate(out_refs):
        for g in range(2 * cols):
            at = (chip * 2 * cols + g) * LANES
            out[:, g * LANES : (g + 1) * LANES] = square_ref[at : at + LANES, :].astype(
                jnp.bfloat16
            )


def direct_rows(pieces, onsite, rows, slots):
    cols = len(pieces)
    groups = rows * cols * PB
    shape = jax.ShapeDtypeStruct((PB * BS, 2 * cols * LANES), jnp.bfloat16)
    return pl.pallas_call(
        functools.partial(direct_kernel, rows, slots),
        out_shape=(shape,) * (rows // 2),
        in_specs=[VMEM] * (cols + 1),
        out_specs=(VMEM,) * (rows // 2),
        scratch_shapes=[
            pltpu.VMEM((2 * groups, BS * BS), jnp.float32),
            pltpu.VMEM((groups * BS, LANES), jnp.float32),
        ],
        compiler_params=pltpu.CompilerParams(vmem_limit_bytes=48 * 1024 * 1024),
        name="direct_rows",
    )(*pieces, onsite)


def local(orbitals_in, hblocks, block_cols, live_counts, onsite, cut_low, top_bound):
    rows = lax.axis_size("row")
    cols = lax.axis_size("col")
    chips = rows // 2
    row = lax.axis_index("row")
    col = lax.axis_index("col")
    chip, core = row // 2, row % 2
    row_blocks, slots, _ = hblocks.shape
    k = orbitals_in.shape[1]
    local_rows = PB * BS
    total_rows = rows * cols * local_rows
    near_rows = cols * local_rows

    live = jnp.arange(slots, dtype=jnp.int32)[None, :] < live_counts
    device, block = block_cols // PB, block_cols % PB
    apart = (device % 2) ^ core
    distance = (device // 2) ^ chip
    places = jnp.where(live, (distance * 2 + apart) * PB + block, -1).astype(jnp.bfloat16)
    places = places.reshape(cols, 1, PB * slots)
    places = jnp.pad(places, ((0, 0), (0, PB * slots - 1), (0, LANES - PB * slots)))
    block_row = jnp.arange(row_blocks, dtype=jnp.int32)[:, None]
    near_row = (col ^ (block_row // PB)) * PB + block_row % PB
    groups = rows * row_blocks
    key = block * groups + (apart * chips + distance) * row_blocks + near_row
    key = jnp.where(live, key, -1).reshape(1, row_blocks * slots)

    pieces = pack(col[None], hblocks.reshape(cols, PB * slots, BS * BS), places)
    key, pieces = lax.optimization_barrier((key, pieces))
    pieces = [exchanged(pieces[s], "col", cols, s) if s else pieces[s] for s in range(cols)]

    def gather_near(v):
        return jnp.concatenate([v] + [exchanged(v, "col", cols, s) for s in range(1, cols)], 0)

    def gather_rows(v):
        near = gather_near(v)
        return near, core_swap(near, rows)

    near, far = mirror(key, hblocks.reshape(row_blocks * slots, BS * BS), rows, row_blocks)

    direct = direct_rows(pieces, onsite, rows, slots)
    far, direct = lax.optimization_barrier((far, direct))
    far = core_swap(far, rows)
    direct = [chip_swap(direct[s], rows, s) if s else direct[s] for s in range(chips)]
    first, far = lax.optimization_barrier((orbitals_in.astype(jnp.bfloat16), far))
    first_gathered = gather_rows(first)
    tile = jnp.concatenate([near, far], 1) + jnp.concatenate(direct, 0)
    tile_near, tile_far = tile[:, :near_rows], tile[:, near_rows:]

    def partial_product(gathered):
        near, far = gathered
        return jnp.dot(tile_near, near, preferred_element_type=jnp.float32) + jnp.dot(
            tile_far, far, preferred_element_type=jnp.float32
        )

    def apply(gathered):
        terms = partial_product(gathered).reshape(chips, local_rows, k)
        total = terms[0]
        for s in range(1, chips):
            total = total + chip_swap(terms[s], rows, s)
        return total

    centre = 0.5 * (top_bound[0] + cut_low[0])
    halfwidth = 0.5 * (top_bound[0] - cut_low[0])
    previous = orbitals_in
    current = (apply(first_gathered) - centre * orbitals_in) / halfwidth
    for degree in range(DEG - 1):
        gathered = gather_rows(current.astype(jnp.bfloat16))
        following = 2.0 * (apply(gathered) - centre * current) / halfwidth - previous
        previous, current = (current, following)

    rounded = current.astype(jnp.bfloat16)
    plane_rows = jnp.concatenate(
        [rounded] + [chip_swap(rounded, rows, s) for s in range(1, chips)], 0
    )
    near, plane_rows = lax.optimization_barrier((gather_near(rounded), plane_rows))
    gathered = near, core_swap(near, rows)
    contract = (((0,), (0,)), ((), ()))
    gram_part = lax.dot_general(
        gathered[0], gathered[0], contract, preferred_element_type=jnp.float32
    ) / cols
    cross_part = lax.dot_general(
        plane_rows.astype(jnp.float32), partial_product(gathered), contract, precision=HI
    )

    share = k // rows
    cross_part = cross_part + cross_part.T
    ids = jnp.arange(k, dtype=jnp.int32)
    packed = jnp.where(ids[:, None] <= ids[None, :], gram_part, cross_part)
    diagonal = jnp.sum(jnp.where(ids[:, None] == ids[None, :], cross_part, 0.0), 0)
    diagonal = jnp.broadcast_to(diagonal, (rows, 8, k))
    total = jnp.concatenate([packed.reshape(rows, share, k), diagonal], 1)
    total = total.reshape(chips, 2, share + 8, k)
    kept = jnp.where(core == 0, total[:, 0], total[:, 1])
    total = kept + core_swap(jnp.where(core == 0, total[:, 1], total[:, 0]), rows)
    total = by_distance(total, chip)
    total = sum([chip_swap(total[s], rows, s) for s in range(1, chips)], total[0])
    total = sum([exchanged(total, "col", cols, s) for s in range(1, cols)], total)
    total = jnp.stack([total] + [chip_swap(total, rows, s) for s in range(1, chips)])
    total = by_distance(total, chip)
    other = core_swap(total, rows)
    pair = (jnp.where(core == 0, total, other), jnp.where(core == 0, other, total))
    total = jnp.stack(pair, 1).reshape(rows, share + 8, k)
    packed = total[:, :share].reshape(k, k)
    return finish(packed, total[0, share : share + 1], current, total_rows)


def solution(mesh):
    placed = (
        P(("row", "col"), None),
        P("row", "col", None),
        P("row", "col"),
        P("row", "col"),
        P(("row", "col"), None),
        P(),
        P(),
    )
    return jax.shard_map(
        local, mesh=mesh, in_specs=placed, out_specs=(P(("row", "col"), None), P()), check_vma=False
    )
```

```python
import functools

import jax
import jax.numpy as jnp
from jax import lax
from jax.experimental import pallas as pl
from jax.experimental.pallas import tpu as pltpu
from jax.sharding import PartitionSpec as P

BS = 64
PB = 2
DEG = 3
LANES = 128
PANEL = 32
HI = lax.Precision.HIGHEST
VMEM = pl.BlockSpec(memory_space=pltpu.VMEM)
SMEM = pl.BlockSpec(memory_space=pltpu.SMEM)


def widen(x, width):
    return jnp.concatenate([x] * (width // LANES), 1) if width > LANES else x

def finish_kernel(total_rows, packed_ref, diagonal_ref, y_ref, orbitals_ref, projected_ref, inverse_ref):
    k = packed_ref.shape[0]
    panels = k // PANEL
    packed = packed_ref[...]
    flipped = packed.T
    above = lax.broadcasted_iota(jnp.int32, (k, k), 0) - lax.broadcasted_iota(jnp.int32, (k, k), 1)
    gram = jnp.where(above <= 0, packed, flipped)
    cross = jnp.where(above > 0, packed, jnp.where(above < 0, flipped, diagonal_ref[...]))
    row_id = lax.broadcasted_iota(jnp.int32, (PANEL, LANES), 0)
    scale = 1.0 / total_rows
    upper = [gram[m * PANEL:(m + 1) * PANEL, :] * scale for m in range(panels)]
    inverse = []
    for m in range(panels):
        r = lax.broadcasted_iota(jnp.int32, (PANEL, k), 0) + m * PANEL
        inverse.append((r == lax.broadcasted_iota(jnp.int32, (PANEL, k), 1)).astype(jnp.float32))
    for p in range(panels):
        start = p * PANEL
        s_lo = start // LANES * LANES
        w_hi = (start + PANEL + LANES - 1) // LANES * LANES
        s, w = upper[p][:, s_lo:], inverse[p][:, :w_hi]
        columns = [
            jnp.broadcast_to(s[:, start - s_lo + t:start - s_lo + t + 1], (PANEL, LANES))
            for t in range(PANEL)
        ]
        pivots = jnp.zeros((PANEL, LANES), jnp.float32)
        for t in range(PANEL):
            column = columns[t]
            pivot_inv = 1.0 / column[t:t + 1, :]
            pivots = jnp.where(row_id == t, column, pivots)
            if t == PANEL - 1:
                break
            below = jnp.where(row_id > t, column, 0.0)
            for j in range(t + 1, PANEL):
                columns[j] = columns[j] - below * (column[j:j + 1, :] * pivot_inv)
            ratio = below * pivot_inv
            s = s - widen(ratio, s.shape[1]) * s[t:t + 1, :]
            w = w - widen(ratio, w.shape[1]) * w[t:t + 1, :]
        root = lax.rsqrt(pivots)
        s = s * widen(root, s.shape[1])
        w = w * widen(root, w.shape[1])
        inverse_ref[start:start + PANEL, :w_hi] = w
        if w_hi < k:
            inverse_ref[start:start + PANEL, w_hi:] = jnp.zeros((PANEL, k - w_hi), jnp.float32)
        if p == panels - 1:
            break
        st = s.T
        for lo, hi in ((p + 1, p + 2), (p + 2, panels)):
            if lo >= hi:
                continue
            left = st[lo * PANEL - s_lo:hi * PANEL - s_lo, :]
            s_lo2 = lo * PANEL // LANES * LANES
            ds = jnp.dot(left, s[:, s_lo2 - s_lo:], precision=HI, preferred_element_type=jnp.float32)
            dw = jnp.dot(left, w, precision=HI, preferred_element_type=jnp.float32)
            for m in range(lo, hi):
                o = (m - lo) * PANEL
                a = upper[m][:, s_lo2:] - ds[o:o + PANEL, :]
                upper[m] = a if s_lo2 == 0 else jnp.concatenate([upper[m][:, :s_lo2], a], 1)
                b = inverse[m][:, :w_hi] - dw[o:o + PANEL, :]
                inverse[m] = b if w_hi == k else jnp.concatenate([b, inverse[m][:, w_hi:]], 1)
    inv = inverse_ref[...]
    nt = (((1,), (1,)), ((), ()))
    orbitals_ref[...] = lax.dot_general(y_ref[...], inv, nt, precision=HI, preferred_element_type=jnp.float32)
    half = jnp.dot(inv, cross, precision=HI, preferred_element_type=jnp.float32)
    full = lax.dot_general(half, inv, nt, precision=HI, preferred_element_type=jnp.float32)
    projected_ref[...] = full * (0.5 * scale)

def finish(packed, diagonal, y, total_rows):
    k = packed.shape[0]
    f32 = jnp.float32
    return pl.pallas_call(
        functools.partial(finish_kernel, total_rows),
        out_shape=(jax.ShapeDtypeStruct(y.shape, f32), jax.ShapeDtypeStruct((k, k), f32)),
        in_specs=[pl.BlockSpec(memory_space=pltpu.VMEM)] * 3,
        out_specs=(pl.BlockSpec(memory_space=pltpu.VMEM),) * 2,
        scratch_shapes=[pltpu.VMEM((k, k), f32)],
        compiler_params=pltpu.CompilerParams(vmem_limit_bytes=32 * 1024 * 1024),
        name="finish",
    )(packed, diagonal, y)


def exchanged(x, axis, size, apart):
    return lax.ppermute(x, axis, [(i, i ^ apart) for i in range(size)])


def shifted(x, axis, size, step):
    return lax.ppermute(x, axis, [(i, (i + step) % size) for i in range(size)])


def core_swap(x, rows):
    return exchanged(x, "row", rows, 1)


def chip_swap(x, rows, apart):
    return exchanged(x, "row", rows, 2 * apart)


def by_distance(x, index):
    size = x.shape[0]
    bit = 1
    while bit < size:
        pairs = x.reshape(size // (2 * bit), 2, bit, *x.shape[1:])
        flipped = jnp.stack([pairs[:, 1], pairs[:, 0]], 1).reshape(x.shape)
        x = jnp.where((index // bit) % 2 == 1, flipped, x)
        bit *= 2
    return x


def slot_places(here_ref, cols_ref, live_ref):
    columns = cols_ref[...]
    device, block = columns // PB, columns % PB
    apart = jnp.bitwise_xor(device % 2, here_ref[1])
    distance = jnp.bitwise_xor(device // 2, here_ref[0])
    slot = lax.broadcasted_iota(jnp.int32, columns.shape, 1)
    return jnp.where(slot < live_ref[...], (distance * 2 + apart) * PB + block, -1)


def spread(places, width, offset):
    height, slots = places.shape
    slot = lax.broadcasted_iota(jnp.int32, (slots, width), 0)
    lane = lax.broadcasted_iota(jnp.int32, (slots, width), 1)
    repeat = (lane % slots == slot).astype(jnp.float32).astype(jnp.bfloat16)
    copies = jnp.dot(
        (places + 1).astype(jnp.float32).astype(jnp.bfloat16),
        repeat,
        preferred_element_type=jnp.float32,
    )
    row = lax.broadcasted_iota(jnp.int32, (height, width), 0)
    lane = lax.broadcasted_iota(jnp.int32, (height, width), 1)
    return jnp.where(lane // slots == offset(row), copies, 0.0).astype(jnp.int32) - 1


def pack_kernel(here_ref, blocks_ref, cols_ref, live_ref, *piece_refs):
    cols = blocks_ref.shape[0]
    height = blocks_ref.shape[1]
    half = BS * BS // 2
    places = spread(slot_places(here_ref, cols_ref, live_ref), LANES, lambda row: row % PB)
    owner_of_row = lax.broadcasted_iota(jnp.int32, places.shape, 0) // PB
    for s in range(cols):
        owner = lax.rem(here_ref[2] + s, cols)
        mine = jnp.max(jnp.where(owner_of_row == owner, places, -1), 0, keepdims=True)
        mine = jnp.broadcast_to(mine.astype(jnp.float32), (height, LANES)).astype(jnp.bfloat16)
        for h in range(2):
            piece = piece_refs[h * cols + s]
            piece[:, :half] = blocks_ref[owner, :, h * half : (h + 1) * half]
            piece[:, half:] = mine


def pack(here, blocks, block_cols, live_counts):
    cols, height, _ = blocks.shape
    shape = jax.ShapeDtypeStruct((height, BS * BS // 2 + LANES), jnp.bfloat16)
    pieces = pl.pallas_call(
        pack_kernel,
        out_shape=(shape,) * (2 * cols),
        in_specs=[SMEM, VMEM, VMEM, VMEM],
        out_specs=(VMEM,) * (2 * cols),
        name="pack",
    )(here, blocks, block_cols, live_counts)
    return pieces[:cols], pieces[cols:]


def unflatten(flat_ref, square_ref, groups):
    height = flat_ref.shape[1] // BS
    lower = lax.broadcasted_iota(jnp.int32, (groups, LANES), 1) < BS
    for h in range(height // 2):
        even = flat_ref[:groups, h * LANES : (h + 1) * LANES]
        odd = flat_ref[groups:, h * LANES : (h + 1) * LANES]
        first = jnp.where(lower, even, pltpu.roll(odd, BS, 1))
        second = jnp.where(lower, pltpu.roll(even, BS, 1), odd)
        square_ref[pl.ds(2 * h, groups, stride=height), :] = first
        square_ref[pl.ds(2 * h + 1, groups, stride=height), :] = second


def mirror_kernel(
    here_ref, cols_ref, live_ref, blocks_ref, near_ref, far_ref, flat_ref, square_ref
):
    height = near_ref.shape[1]
    groups = square_ref.shape[0] // BS
    row_blocks, slots = cols_ref.shape
    chips = groups // row_blocks // 2
    width = row_blocks * slots
    places = slot_places(here_ref, cols_ref, live_ref)
    place = jnp.max(spread(places, width, lambda row: row), 0, keepdims=True)
    block_row = lax.broadcasted_iota(jnp.int32, (1, width), 1) // slots
    behind = here_ref[2] - block_row // PB
    behind = jnp.where(behind < 0, behind + row_blocks // PB, behind)
    device = place // PB
    key = place % PB * groups + (device % 2 * chips + device // 2) * row_blocks
    key = jnp.where(place < 0, -1, key + behind * PB + block_row % PB)
    ids = lax.broadcasted_iota(jnp.int32, (2 * groups, width), 0)
    chosen = (ids == key).astype(jnp.float32).astype(jnp.bfloat16)
    flat_ref[...] = jnp.dot(chosen, blocks_ref[...], preferred_element_type=jnp.float32)
    unflatten(flat_ref, square_ref, groups)
    devices = square_ref.shape[0] // height
    for d in range(devices):
        out = near_ref if d < devices // 2 else far_ref
        at = d % (devices // 2) * LANES
        square = square_ref[d * height : (d + 1) * height, :]
        out[at : at + LANES, :] = square.T.astype(jnp.bfloat16)


def mirror(here, block_cols, live_counts, blocks, rows):
    row_blocks = block_cols.shape[0]
    half = (rows // 2 * PB * BS, row_blocks * BS)
    groups = rows * row_blocks
    return pl.pallas_call(
        mirror_kernel,
        out_shape=(jax.ShapeDtypeStruct(half, jnp.bfloat16),) * 2,
        in_specs=[SMEM, VMEM, VMEM, VMEM],
        out_specs=(VMEM, VMEM),
        scratch_shapes=[
            pltpu.VMEM((2 * groups, BS * BS), jnp.float32),
            pltpu.VMEM((groups * BS, LANES), jnp.float32),
        ],
        compiler_params=pltpu.CompilerParams(vmem_limit_bytes=40 * 1024 * 1024),
        cost_estimate=pl.CostEstimate(
            flops=4 * groups * blocks.size, bytes_accessed=3 * blocks.size, transcendentals=0
        ),
        name="mirror",
    )(here, block_cols, live_counts, blocks)


def direct_kernel(rows, slots, half, *refs):
    cols = len(refs) - 3 - rows // 2
    piece_refs, onsite_ref = refs[:cols], refs[cols]
    out_refs, (flat_ref, square_ref) = refs[cols + 1 : -2], refs[-2:]
    row_blocks = cols * PB
    groups = rows * row_blocks
    width = BS * BS // 2
    height = PB * BS // 2
    total = jnp.zeros((2 * groups, width), jnp.float32)
    for s, piece in enumerate(piece_refs):
        count = piece.shape[0]
        place = piece[0:1, width : width + count].astype(jnp.float32).astype(jnp.int32)
        block = lax.broadcasted_iota(jnp.int32, (1, count), 1) // slots
        key = place % 2 * groups + place // 2 * row_blocks + s * PB + block
        key = jnp.where(place < 0, -1, key)
        ids = lax.broadcasted_iota(jnp.int32, (2 * groups, count), 0)
        chosen = (ids == key).astype(jnp.float32).astype(jnp.bfloat16)
        total += jnp.dot(chosen, piece[:, :width], preferred_element_type=jnp.float32)
    flat_ref[...] = total
    for p in range(PB):
        at = p * groups + p
        own = onsite_ref[p : p + 1, half * width : (half + 1) * width]
        flat_ref[at : at + 1, :] += own.astype(jnp.float32)
    unflatten(flat_ref, square_ref, groups)
    for chip, out in enumerate(out_refs):
        for g in range(2 * cols):
            at = (chip * 2 * cols + g) * height
            out[:, g * LANES : (g + 1) * LANES] = square_ref[at : at + height, :].astype(
                jnp.bfloat16
            )


def direct_rows(pieces, onsite, rows, slots, half):
    cols = len(pieces)
    groups = rows * cols * PB
    shape = jax.ShapeDtypeStruct((PB * BS // 2, 2 * cols * LANES), jnp.bfloat16)
    return pl.pallas_call(
        functools.partial(direct_kernel, rows, slots, half),
        out_shape=(shape,) * (rows // 2),
        in_specs=[VMEM] * (cols + 1),
        out_specs=(VMEM,) * (rows // 2),
        scratch_shapes=[
            pltpu.VMEM((2 * groups, BS * BS // 2), jnp.float32),
            pltpu.VMEM((groups * BS // 2, LANES), jnp.float32),
        ],
        compiler_params=pltpu.CompilerParams(vmem_limit_bytes=48 * 1024 * 1024),
        cost_estimate=pl.CostEstimate(
            flops=0, bytes_accessed=64 * cols * pieces[0].size, transcendentals=0
        ),
        name="direct_rows",
    )(*pieces, onsite)


def local(orbitals_in, hblocks, block_cols, live_counts, onsite, cut_low, top_bound):
    rows = lax.axis_size("row")
    cols = lax.axis_size("col")
    chips = rows // 2
    row = lax.axis_index("row")
    col = lax.axis_index("col")
    chip, core = row // 2, row % 2
    row_blocks, slots, _ = hblocks.shape
    k = orbitals_in.shape[1]
    local_rows = PB * BS
    total_rows = rows * cols * local_rows
    near_rows = cols * local_rows

    here = jnp.stack([chip, core, col])
    pieces = pack(here, hblocks.reshape(cols, PB * slots, BS * BS), block_cols, live_counts)
    block_cols, pieces = lax.optimization_barrier((block_cols, pieces))
    pieces = [
        [shifted(half[s], "col", cols, s) if s else half[s] for s in range(cols)]
        for half in pieces
    ]

    def gather_near(v):
        return jnp.concatenate([v] + [shifted(v, "col", cols, s) for s in range(1, cols)], 0)

    def gather_rows(v):
        near = gather_near(v)
        return near, core_swap(near, rows)

    blocks = hblocks.reshape(row_blocks * slots, BS * BS)
    near, far = mirror(here, block_cols, live_counts, blocks, rows)

    def across(dense):
        return [chip_swap(dense[s], rows, s) if s else dense[s] for s in range(chips)]

    direct = [direct_rows(pieces[h], onsite, rows, slots, h) for h in range(2)]
    direct[0] = across(direct[0])
    far, direct = lax.optimization_barrier((far, direct))
    far = core_swap(far, rows)
    direct[1] = across(direct[1])
    first, far = lax.optimization_barrier((orbitals_in.astype(jnp.bfloat16), far))
    first_gathered = gather_rows(first)
    direct = jnp.stack([jnp.stack(half).reshape(chips, PB, BS // 2, -1) for half in direct], 2)
    tile = jnp.concatenate([near, far], 1) + direct.reshape(chips * local_rows, -1)
    tile_near, tile_far = tile[:, :near_rows], tile[:, near_rows:]

    def partial_product(gathered):
        near, far = gathered
        return jnp.dot(tile_near, near, preferred_element_type=jnp.float32) + jnp.dot(
            tile_far, far, preferred_element_type=jnp.float32
        )

    def apply(gathered):
        terms = partial_product(gathered).reshape(chips, local_rows, k)
        total = terms[0]
        for s in range(1, chips):
            total = total + chip_swap(terms[s], rows, s)
        return total

    centre = 0.5 * (top_bound[0] + cut_low[0])
    halfwidth = 0.5 * (top_bound[0] - cut_low[0])
    previous = orbitals_in
    current = (apply(first_gathered) - centre * orbitals_in) / halfwidth
    for degree in range(DEG - 1):
        gathered = gather_rows(current.astype(jnp.bfloat16))
        following = 2.0 * (apply(gathered) - centre * current) / halfwidth - previous
        previous, current = (current, following)

    rounded = current.astype(jnp.bfloat16)
    plane_rows = jnp.concatenate(
        [rounded] + [chip_swap(rounded, rows, s) for s in range(1, chips)], 0
    )
    near, plane_rows = lax.optimization_barrier((gather_near(rounded), plane_rows))
    gathered = near, core_swap(near, rows)
    contract = (((0,), (0,)), ((), ()))
    gram_part = lax.dot_general(
        gathered[0], gathered[0], contract, preferred_element_type=jnp.float32
    ) / cols
    cross_part = lax.dot_general(
        plane_rows.astype(jnp.float32), partial_product(gathered), contract, precision=HI
    )

    share = k // rows
    cross_part = cross_part + cross_part.T
    ids = jnp.arange(k, dtype=jnp.int32)
    packed = jnp.where(ids[:, None] <= ids[None, :], gram_part, cross_part)
    diagonal = jnp.sum(jnp.where(ids[:, None] == ids[None, :], cross_part, 0.0), 0)
    diagonal = jnp.broadcast_to(diagonal, (rows, 8, k))
    total = jnp.concatenate([packed.reshape(rows, share, k), diagonal], 1)
    total = total.reshape(chips, 2, share + 8, k)
    kept = jnp.where(core == 0, total[:, 0], total[:, 1])
    total = kept + core_swap(jnp.where(core == 0, total[:, 1], total[:, 0]), rows)
    total = by_distance(total, chip)
    total = sum([chip_swap(total[s], rows, s) for s in range(1, chips)], total[0])
    total = sum([shifted(total, "col", cols, s) for s in range(1, cols)], total)
    total = jnp.stack([total] + [chip_swap(total, rows, s) for s in range(1, chips)])
    total = by_distance(total, chip)
    other = core_swap(total, rows)
    pair = (jnp.where(core == 0, total, other), jnp.where(core == 0, other, total))
    total = jnp.stack(pair, 1).reshape(rows, share + 8, k)
    packed = total[:, :share].reshape(k, k)
    return finish(packed, total[0, share : share + 1], current, total_rows)


def solution(mesh):
    placed = (
        P(("row", "col"), None),
        P("row", "col", None),
        P("row", "col"),
        P("row", "col"),
        P(("row", "col"), None),
        P(),
        P(),
    )
    return jax.shard_map(
        local, mesh=mesh, in_specs=placed, out_specs=(P(("row", "col"), None), P()), check_vma=False
    )
```

```python
import functools

import jax
import jax.numpy as jnp
from jax import lax
from jax.experimental import pallas as pl
from jax.experimental.pallas import tpu as pltpu
from jax.sharding import PartitionSpec as P

BS = 64
PB = 2
DEG = 3
LANES = 128
PANEL = 32
HI = lax.Precision.HIGHEST
VMEM = pl.BlockSpec(memory_space=pltpu.VMEM)
SMEM = pl.BlockSpec(memory_space=pltpu.SMEM)


def widen(x, width):
    return jnp.concatenate([x] * (width // LANES), 1) if width > LANES else x

def reciprocal(x):
    return pl.reciprocal(x, approx=True)


def finish_kernel(total_rows, packed_ref, diagonal_ref, y_ref, orbitals_ref, projected_ref, inverse_ref):
    k = packed_ref.shape[0]
    panels = k // PANEL
    packed = packed_ref[...]
    flipped = packed.T
    above = lax.broadcasted_iota(jnp.int32, (k, k), 0) - lax.broadcasted_iota(jnp.int32, (k, k), 1)
    gram = jnp.where(above <= 0, packed, flipped)
    cross = jnp.where(above > 0, packed, jnp.where(above < 0, flipped, diagonal_ref[...]))
    row_id = lax.broadcasted_iota(jnp.int32, (PANEL, LANES), 0)
    scale = 1.0 / total_rows
    upper = [gram[m * PANEL:(m + 1) * PANEL, :] * scale for m in range(panels)]
    inverse = []
    for m in range(panels):
        r = lax.broadcasted_iota(jnp.int32, (PANEL, k), 0) + m * PANEL
        inverse.append((r == lax.broadcasted_iota(jnp.int32, (PANEL, k), 1)).astype(jnp.float32))
    for p in range(panels):
        start = p * PANEL
        s_lo = start // LANES * LANES
        w_hi = (start + PANEL + LANES - 1) // LANES * LANES
        s, w = upper[p][:, s_lo:], inverse[p][:, :w_hi]
        columns = [
            jnp.broadcast_to(s[:, start - s_lo + t:start - s_lo + t + 1], (PANEL, LANES))
            for t in range(PANEL)
        ]
        pivots = jnp.zeros((PANEL, LANES), jnp.float32)
        for t in range(0, PANEL, 2):
            one, two = columns[t], columns[t + 1]
            a, b, d = one[t:t + 1, :], one[t + 1:t + 2, :], two[t + 1:t + 2, :]
            det = a * d - b * b
            det_inv = reciprocal(det)
            a_inv = reciprocal(a)
            pivots = jnp.where(row_id == t, a, pivots)
            pivots = jnp.where(row_id == t + 1, det * a_inv, pivots)
            one_below = jnp.where(row_id > t + 1, one, 0.0)
            two_below = jnp.where(row_id > t + 1, two, 0.0)
            for j in range(t + 2, PANEL):
                p1, p2 = one[j:j + 1, :], two[j:j + 1, :]
                columns[j] = (
                    columns[j]
                    - one_below * ((d * p1 - b * p2) * det_inv)
                    - two_below * ((a * p2 - b * p1) * det_inv)
                )
            first = (d * one_below - b * two_below) * det_inv
            first = jnp.where(row_id == t + 1, b * a_inv, first)
            second = (a * two_below - b * one_below) * det_inv
            s = (
                s
                - widen(first, s.shape[1]) * s[t:t + 1, :]
                - widen(second, s.shape[1]) * s[t + 1:t + 2, :]
            )
            w = (
                w
                - widen(first, w.shape[1]) * w[t:t + 1, :]
                - widen(second, w.shape[1]) * w[t + 1:t + 2, :]
            )
        root = lax.rsqrt(pivots)
        s = s * widen(root, s.shape[1])
        w = w * widen(root, w.shape[1])
        inverse_ref[start:start + PANEL, :w_hi] = w
        if w_hi < k:
            inverse_ref[start:start + PANEL, w_hi:] = jnp.zeros((PANEL, k - w_hi), jnp.float32)
        if p == panels - 1:
            break
        st = s.T
        for lo, hi in ((p + 1, p + 2), (p + 2, panels)):
            if lo >= hi:
                continue
            left = st[lo * PANEL - s_lo:hi * PANEL - s_lo, :]
            s_lo2 = lo * PANEL // LANES * LANES
            ds = jnp.dot(left, s[:, s_lo2 - s_lo:], precision=HI, preferred_element_type=jnp.float32)
            dw = jnp.dot(left, w, precision=HI, preferred_element_type=jnp.float32)
            for m in range(lo, hi):
                o = (m - lo) * PANEL
                a = upper[m][:, s_lo2:] - ds[o:o + PANEL, :]
                upper[m] = a if s_lo2 == 0 else jnp.concatenate([upper[m][:, :s_lo2], a], 1)
                b = inverse[m][:, :w_hi] - dw[o:o + PANEL, :]
                inverse[m] = b if w_hi == k else jnp.concatenate([b, inverse[m][:, w_hi:]], 1)
    inv = inverse_ref[...]
    nt = (((1,), (1,)), ((), ()))
    orbitals_ref[...] = lax.dot_general(y_ref[...], inv, nt, precision=HI, preferred_element_type=jnp.float32)
    half = jnp.dot(inv, cross, precision=HI, preferred_element_type=jnp.float32)
    full = lax.dot_general(half, inv, nt, precision=HI, preferred_element_type=jnp.float32)
    projected_ref[...] = full * (0.5 * scale)

def finish(packed, diagonal, y, total_rows):
    k = packed.shape[0]
    f32 = jnp.float32
    return pl.pallas_call(
        functools.partial(finish_kernel, total_rows),
        out_shape=(jax.ShapeDtypeStruct(y.shape, f32), jax.ShapeDtypeStruct((k, k), f32)),
        in_specs=[pl.BlockSpec(memory_space=pltpu.VMEM)] * 3,
        out_specs=(pl.BlockSpec(memory_space=pltpu.VMEM),) * 2,
        scratch_shapes=[pltpu.VMEM((k, k), f32)],
        compiler_params=pltpu.CompilerParams(vmem_limit_bytes=32 * 1024 * 1024),
        name="finish",
    )(packed, diagonal, y)


def exchanged(x, axis, size, apart):
    return lax.ppermute(x, axis, [(i, i ^ apart) for i in range(size)])


def shifted(x, axis, size, step):
    return lax.ppermute(x, axis, [(i, (i + step) % size) for i in range(size)])


def core_swap(x, rows):
    return exchanged(x, "row", rows, 1)


def chip_swap(x, rows, apart):
    return exchanged(x, "row", rows, 2 * apart)


def by_distance(x, index):
    size = x.shape[0]
    bit = 1
    while bit < size:
        pairs = x.reshape(size // (2 * bit), 2, bit, *x.shape[1:])
        flipped = jnp.stack([pairs[:, 1], pairs[:, 0]], 1).reshape(x.shape)
        x = jnp.where((index // bit) % 2 == 1, flipped, x)
        bit *= 2
    return x


def pack_kernel(col_ref, blocks_ref, places_ref, *piece_refs):
    cols = len(piece_refs)
    for s, piece in enumerate(piece_refs):
        owner = lax.rem(col_ref[0] + s, cols)
        piece[:, : BS * BS] = blocks_ref[owner]
        piece[:, BS * BS :] = places_ref[owner]


def pack(col, blocks, places):
    cols, height, _ = blocks.shape
    shape = jax.ShapeDtypeStruct((height, BS * BS + LANES), jnp.bfloat16)
    return pl.pallas_call(
        pack_kernel,
        out_shape=(shape,) * cols,
        in_specs=[SMEM, VMEM, VMEM],
        out_specs=(VMEM,) * cols,
        name="pack",
    )(col, blocks, places)


def unflatten(flat_ref, square_ref, groups):
    lower = lax.broadcasted_iota(jnp.int32, (groups, LANES), 1) < BS
    for h in range(BS * BS // LANES):
        even = flat_ref[:groups, h * LANES : (h + 1) * LANES]
        odd = flat_ref[groups:, h * LANES : (h + 1) * LANES]
        first = jnp.where(lower, even, pltpu.roll(odd, BS, 1))
        second = jnp.where(lower, pltpu.roll(even, BS, 1), odd)
        square_ref[pl.ds(2 * h, groups, stride=BS), :] = first
        square_ref[pl.ds(2 * h + 1, groups, stride=BS), :] = second


def mirror_kernel(key_ref, blocks_ref, onsite_ref, near_ref, far_ref, flat_ref, square_ref):
    height = near_ref.shape[1]
    groups = square_ref.shape[0] // BS
    places = lax.broadcasted_iota(jnp.int32, (2 * groups, key_ref.shape[1]), 0)
    chosen = (places == key_ref[...]).astype(jnp.float32).astype(jnp.bfloat16)
    flat_ref[...] = jnp.dot(chosen, blocks_ref[...], preferred_element_type=jnp.float32)
    for p in range(PB):
        at = p * groups + p
        flat_ref[at : at + 1, :] += onsite_ref[p : p + 1, :].astype(jnp.float32)
    unflatten(flat_ref, square_ref, groups)
    devices = square_ref.shape[0] // height
    for d in range(devices):
        out = near_ref if d < devices // 2 else far_ref
        at = d % (devices // 2) * LANES
        square = square_ref[d * height : (d + 1) * height, :]
        out[at : at + LANES, :] = square.T.astype(jnp.bfloat16)


def mirror(key, blocks, onsite, rows, row_blocks):
    half = (rows // 2 * PB * BS, row_blocks * BS)
    groups = rows * row_blocks
    return pl.pallas_call(
        mirror_kernel,
        out_shape=(jax.ShapeDtypeStruct(half, jnp.bfloat16),) * 2,
        in_specs=[VMEM, VMEM, VMEM],
        out_specs=(VMEM, VMEM),
        scratch_shapes=[
            pltpu.VMEM((2 * groups, BS * BS), jnp.float32),
            pltpu.VMEM((groups * BS, LANES), jnp.float32),
        ],
        compiler_params=pltpu.CompilerParams(vmem_limit_bytes=40 * 1024 * 1024),
        cost_estimate=pl.CostEstimate(
            flops=4 * groups * blocks.size, bytes_accessed=3 * blocks.size, transcendentals=0
        ),
        name="mirror",
    )(key, blocks, onsite)


def direct_kernel(rows, slots, *refs):
    cols = len(refs) - 2 - rows // 2
    piece_refs, out_refs, (flat_ref, square_ref) = refs[:cols], refs[cols:-2], refs[-2:]
    row_blocks = cols * PB
    groups = rows * row_blocks
    total = jnp.zeros((2 * groups, BS * BS), jnp.float32)
    for s, piece in enumerate(piece_refs):
        height = piece.shape[0]
        place = piece[0:1, BS * BS : BS * BS + height].astype(jnp.float32).astype(jnp.int32)
        block = lax.broadcasted_iota(jnp.int32, (1, height), 1) // slots
        key = place % 2 * groups + place // 2 * row_blocks + s * PB + block
        key = jnp.where(place < 0, -1, key)
        ids = lax.broadcasted_iota(jnp.int32, (2 * groups, height), 0)
        chosen = (ids == key).astype(jnp.float32).astype(jnp.bfloat16)
        total += jnp.dot(chosen, piece[:, : BS * BS], preferred_element_type=jnp.float32)
    flat_ref[...] = total
    unflatten(flat_ref, square_ref, groups)
    for chip, out in enumerate(out_refs):
        for g in range(2 * cols):
            at = (chip * 2 * cols + g) * LANES
            out[:, g * LANES : (g + 1) * LANES] = square_ref[at : at + LANES, :].astype(
                jnp.bfloat16
            )


def direct_rows(pieces, rows, slots):
    cols = len(pieces)
    groups = rows * cols * PB
    shape = jax.ShapeDtypeStruct((PB * BS, 2 * cols * LANES), jnp.bfloat16)
    return pl.pallas_call(
        functools.partial(direct_kernel, rows, slots),
        out_shape=(shape,) * (rows // 2),
        in_specs=[VMEM] * cols,
        out_specs=(VMEM,) * (rows // 2),
        scratch_shapes=[
            pltpu.VMEM((2 * groups, BS * BS), jnp.float32),
            pltpu.VMEM((groups * BS, LANES), jnp.float32),
        ],
        compiler_params=pltpu.CompilerParams(vmem_limit_bytes=48 * 1024 * 1024),
        name="direct_rows",
    )(*pieces)


def local(orbitals_in, hblocks, block_cols, live_counts, onsite, cut_low, top_bound):
    rows = lax.axis_size("row")
    cols = lax.axis_size("col")
    chips = rows // 2
    row = lax.axis_index("row")
    col = lax.axis_index("col")
    chip, core = row // 2, row % 2
    row_blocks, slots, _ = hblocks.shape
    k = orbitals_in.shape[1]
    local_rows = PB * BS
    total_rows = rows * cols * local_rows
    near_rows = cols * local_rows

    live = jnp.arange(slots, dtype=jnp.int32)[None, :] < live_counts
    device, block = block_cols // PB, block_cols % PB
    apart = (device % 2) ^ core
    distance = (device // 2) ^ chip
    places = jnp.where(live, (distance * 2 + apart) * PB + block, -1).astype(jnp.bfloat16)
    places = places.reshape(cols, 1, PB * slots)
    places = jnp.pad(places, ((0, 0), (0, PB * slots - 1), (0, LANES - PB * slots)))
    block_row = jnp.arange(row_blocks, dtype=jnp.int32)[:, None]
    near_row = (col - block_row // PB) % cols * PB + block_row % PB
    groups = rows * row_blocks
    key = block * groups + (apart * chips + distance) * row_blocks + near_row
    key = jnp.where(live, key, -1).reshape(1, row_blocks * slots)

    pieces = pack(col[None], hblocks.reshape(cols, PB * slots, BS * BS), places)
    key, pieces = lax.optimization_barrier((key, pieces))
    pieces = [shifted(pieces[s], "col", cols, s) if s else pieces[s] for s in range(cols)]

    def gather_near(v):
        return jnp.concatenate([v] + [shifted(v, "col", cols, s) for s in range(1, cols)], 0)

    def gather_rows(v):
        near = gather_near(v)
        return near, core_swap(near, rows)

    def dot(a, b):
        return jnp.dot(a, b, preferred_element_type=jnp.float32)

    near, far = mirror(
        key, hblocks.reshape(row_blocks * slots, BS * BS), onsite, rows, row_blocks
    )

    direct = direct_rows(pieces, rows, slots)
    far, direct = lax.optimization_barrier((far, direct))
    far = core_swap(far, rows)
    direct = [chip_swap(direct[s], rows, s) if s else direct[s] for s in range(chips)]
    first, far = lax.optimization_barrier((orbitals_in.astype(jnp.bfloat16), far))
    first_gathered = gather_rows(first)
    tile = jnp.concatenate([near, far], 1) + jnp.concatenate(direct, 0)
    tile_near, tile_far = tile[:, :near_rows], tile[:, near_rows:]

    def partial_product(gathered):
        near, far = gathered
        first, far = lax.optimization_barrier((dot(tile_near, near), far))
        return first + dot(tile_far, far)

    def apply(gathered):
        terms = partial_product(gathered).reshape(chips, local_rows, k)
        total = terms[0]
        for s in range(1, chips):
            total = total + chip_swap(terms[s], rows, s)
        return total

    centre = 0.5 * (top_bound[0] + cut_low[0])
    halfwidth = 0.5 * (top_bound[0] - cut_low[0])
    previous = orbitals_in
    current = (apply(first_gathered) - centre * orbitals_in) / halfwidth
    for degree in range(DEG - 1):
        gathered = gather_rows(current.astype(jnp.bfloat16))
        following = 2.0 * (apply(gathered) - centre * current) / halfwidth - previous
        previous, current = (current, following)

    rounded = current.astype(jnp.bfloat16)
    plane_rows = jnp.concatenate(
        [rounded] + [chip_swap(rounded, rows, s) for s in range(1, chips)], 0
    )
    near, plane_rows = lax.optimization_barrier((gather_near(rounded), plane_rows))
    gathered = near, core_swap(near, rows)
    contract = (((0,), (0,)), ((), ()))
    gram_part = lax.dot_general(
        gathered[0], gathered[0], contract, preferred_element_type=jnp.float32
    ) / cols
    cross_part = lax.dot_general(
        plane_rows.astype(jnp.float32), partial_product(gathered), contract, precision=HI
    )

    share = k // rows
    cross_part = cross_part + cross_part.T
    ids = jnp.arange(k, dtype=jnp.int32)
    packed = jnp.where(ids[:, None] <= ids[None, :], gram_part, cross_part)
    diagonal = jnp.sum(jnp.where(ids[:, None] == ids[None, :], cross_part, 0.0), 0)
    diagonal = jnp.broadcast_to(diagonal, (rows, 8, k))
    total = jnp.concatenate([packed.reshape(rows, share, k), diagonal], 1)
    total = total.reshape(chips, 2, share + 8, k)
    kept = jnp.where(core == 0, total[:, 0], total[:, 1])
    total = kept + core_swap(jnp.where(core == 0, total[:, 1], total[:, 0]), rows)
    total = by_distance(total, chip)
    total = sum([chip_swap(total[s], rows, s) for s in range(1, chips)], total[0])
    total = sum([shifted(total, "col", cols, s) for s in range(1, cols)], total)
    total = jnp.stack([total] + [chip_swap(total, rows, s) for s in range(1, chips)])
    total = by_distance(total, chip)
    other = core_swap(total, rows)
    pair = (jnp.where(core == 0, total, other), jnp.where(core == 0, other, total))
    total = jnp.stack(pair, 1).reshape(rows, share + 8, k)
    packed = total[:, :share].reshape(k, k)
    return finish(packed, total[0, share : share + 1], current, total_rows)


def solution(mesh):
    placed = (
        P(("row", "col"), None),
        P("row", "col", None),
        P("row", "col"),
        P("row", "col"),
        P(("row", "col"), None),
        P(),
        P(),
    )
    return jax.shard_map(
        local, mesh=mesh, in_specs=placed, out_specs=(P(("row", "col"), None), P()), check_vma=False
    )
```

```python
import functools

import jax
import jax.numpy as jnp
from jax import lax
from jax.experimental import pallas as pl
from jax.experimental.pallas import tpu as pltpu
from jax.sharding import PartitionSpec as P

BS = 64
PB = 2
DEG = 3
LANES = 128
PANEL = 32
HI = lax.Precision.HIGHEST
VMEM = pl.BlockSpec(memory_space=pltpu.VMEM)
SMEM = pl.BlockSpec(memory_space=pltpu.SMEM)


def widen(x, width):
    return jnp.concatenate([x] * (width // LANES), 1) if width > LANES else x

def reciprocal(x):
    return pl.reciprocal(x, approx=True)


def finish_kernel(total_rows, packed_ref, diagonal_ref, y_ref, orbitals_ref, projected_ref, inverse_ref):
    k = packed_ref.shape[0]
    panels = k // PANEL
    packed = packed_ref[...]
    flipped = packed.T
    above = lax.broadcasted_iota(jnp.int32, (k, k), 0) - lax.broadcasted_iota(jnp.int32, (k, k), 1)
    gram = jnp.where(above <= 0, packed, flipped)
    cross = jnp.where(above > 0, packed, jnp.where(above < 0, flipped, diagonal_ref[...]))
    row_id = lax.broadcasted_iota(jnp.int32, (PANEL, LANES), 0)
    scale = 1.0 / total_rows
    upper = [gram[m * PANEL:(m + 1) * PANEL, :] * scale for m in range(panels)]
    inverse = []
    for m in range(panels):
        r = lax.broadcasted_iota(jnp.int32, (PANEL, k), 0) + m * PANEL
        inverse.append((r == lax.broadcasted_iota(jnp.int32, (PANEL, k), 1)).astype(jnp.float32))
    for p in range(panels):
        start = p * PANEL
        s_lo = start // LANES * LANES
        w_hi = (start + PANEL + LANES - 1) // LANES * LANES
        s, w = upper[p][:, s_lo:], inverse[p][:, :w_hi]
        columns = [
            jnp.broadcast_to(s[:, start - s_lo + t:start - s_lo + t + 1], (PANEL, LANES))
            for t in range(PANEL)
        ]
        s_done, w_done = [], []
        for base in range(0, PANEL, 8):
            ids = row_id[: PANEL - base]
            pivots = jnp.zeros((8, LANES), jnp.float32)
            for t in range(base, base + 8, 2):
                at = t - base
                one, two = columns[t], columns[t + 1]
                a, b, d = one[at:at + 1, :], one[at + 1:at + 2, :], two[at + 1:at + 2, :]
                det = a * d - b * b
                det_inv = reciprocal(det)
                a_inv = reciprocal(a)
                pivots = jnp.where(ids[:8] == at, a, pivots)
                pivots = jnp.where(ids[:8] == at + 1, det * a_inv, pivots)
                below = ids > at + 1
                one_below = jnp.where(below, one, 0.0)
                two_below = jnp.where(below, two, 0.0)
                first = (d * one - b * two) * det_inv
                second = (a * two - b * one) * det_inv
                for j in range(t + 2, PANEL):
                    r = j - base
                    if j < t + 4:
                        p1, p2 = one[r:r + 1, :], two[r:r + 1, :]
                        m1, m2 = (d * p1 - b * p2) * det_inv, (a * p2 - b * p1) * det_inv
                    else:
                        m1, m2 = first[r:r + 1, :], second[r:r + 1, :]
                    columns[j] = columns[j] - (one_below * m1 + two_below * m2)
                first = jnp.where(below, first, jnp.where(ids == at + 1, b * a_inv, 0.0))
                second = jnp.where(below, second, 0.0)
                s = s - (
                    widen(first, s.shape[1]) * s[at:at + 1, :]
                    + widen(second, s.shape[1]) * s[at + 1:at + 2, :]
                )
                w = w - (
                    widen(first, w.shape[1]) * w[at:at + 1, :]
                    + widen(second, w.shape[1]) * w[at + 1:at + 2, :]
                )
            root = lax.rsqrt(pivots)
            s_done.append(s[:8] * widen(root, s.shape[1]))
            w_done.append(w[:8] * widen(root, w.shape[1]))
            s, w = s[8:], w[8:]
            columns = [c[8:] for c in columns]
        s = jnp.concatenate(s_done, 0)
        w = jnp.concatenate(w_done, 0)
        inverse_ref[start:start + PANEL, :w_hi] = w
        if w_hi < k:
            inverse_ref[start:start + PANEL, w_hi:] = jnp.zeros((PANEL, k - w_hi), jnp.float32)
        if p == panels - 1:
            break
        st = s.T
        for lo, hi in ((p + 1, p + 2), (p + 2, panels)):
            if lo >= hi:
                continue
            left = st[lo * PANEL - s_lo:hi * PANEL - s_lo, :]
            s_lo2 = lo * PANEL // LANES * LANES
            ds = jnp.dot(left, s[:, s_lo2 - s_lo:], precision=HI, preferred_element_type=jnp.float32)
            dw = jnp.dot(left, w, precision=HI, preferred_element_type=jnp.float32)
            for m in range(lo, hi):
                o = (m - lo) * PANEL
                a = upper[m][:, s_lo2:] - ds[o:o + PANEL, :]
                upper[m] = a if s_lo2 == 0 else jnp.concatenate([upper[m][:, :s_lo2], a], 1)
                b = inverse[m][:, :w_hi] - dw[o:o + PANEL, :]
                inverse[m] = b if w_hi == k else jnp.concatenate([b, inverse[m][:, w_hi:]], 1)
    inv = inverse_ref[...]
    nt = (((1,), (1,)), ((), ()))
    orbitals_ref[...] = lax.dot_general(y_ref[...], inv, nt, precision=HI, preferred_element_type=jnp.float32)
    half = jnp.dot(inv, cross, precision=HI, preferred_element_type=jnp.float32)
    full = lax.dot_general(half, inv, nt, precision=HI, preferred_element_type=jnp.float32)
    projected_ref[...] = full * (0.5 * scale)

def finish(packed, diagonal, y, total_rows):
    k = packed.shape[0]
    f32 = jnp.float32
    return pl.pallas_call(
        functools.partial(finish_kernel, total_rows),
        out_shape=(jax.ShapeDtypeStruct(y.shape, f32), jax.ShapeDtypeStruct((k, k), f32)),
        in_specs=[pl.BlockSpec(memory_space=pltpu.VMEM)] * 3,
        out_specs=(pl.BlockSpec(memory_space=pltpu.VMEM),) * 2,
        scratch_shapes=[pltpu.VMEM((k, k), f32)],
        compiler_params=pltpu.CompilerParams(vmem_limit_bytes=32 * 1024 * 1024),
        name="finish",
    )(packed, diagonal, y)


def exchanged(x, axis, size, apart):
    return lax.ppermute(x, axis, [(i, i ^ apart) for i in range(size)])


def shifted(x, axis, size, step):
    return lax.ppermute(x, axis, [(i, (i + step) % size) for i in range(size)])


def core_swap(x, rows):
    return exchanged(x, "row", rows, 1)


def chip_swap(x, rows, apart):
    return exchanged(x, "row", rows, 2 * apart)


def by_distance(x, index):
    size = x.shape[0]
    bit = 1
    while bit < size:
        pairs = x.reshape(size // (2 * bit), 2, bit, *x.shape[1:])
        flipped = jnp.stack([pairs[:, 1], pairs[:, 0]], 1).reshape(x.shape)
        x = jnp.where((index // bit) % 2 == 1, flipped, x)
        bit *= 2
    return x


def places_of(places_ref, owner):
    ids = lax.broadcasted_iota(jnp.int32, places_ref.shape, 0)
    return jnp.sum(jnp.where(ids == owner, places_ref[...], 0.0), 0, keepdims=True)


def pack_kernel(col_ref, blocks_ref, places_ref, *piece_refs):
    cols = len(piece_refs) + 1
    for s, piece in enumerate(piece_refs, 1):
        owner = lax.rem(col_ref[0] + s, cols)
        piece[:, : BS * BS] = blocks_ref[owner]
        count = places_ref.shape[1]
        row = jnp.broadcast_to(places_of(places_ref, owner), (piece.shape[0], count))
        piece[:, BS * BS : BS * BS + count] = row.astype(jnp.bfloat16)


def pack(col, blocks, places):
    cols, height, _ = blocks.shape
    shape = jax.ShapeDtypeStruct((height, BS * BS + LANES), jnp.bfloat16)
    return pl.pallas_call(
        pack_kernel,
        out_shape=(shape,) * (cols - 1),
        in_specs=[SMEM, VMEM, VMEM],
        out_specs=(VMEM,) * (cols - 1),
        name="pack",
    )(col, blocks, places)


def unflatten(flat_ref, square_ref, groups):
    lower = lax.broadcasted_iota(jnp.int32, (groups, LANES), 1) < BS
    for h in range(BS * BS // LANES):
        even = flat_ref[:groups, h * LANES : (h + 1) * LANES]
        odd = flat_ref[groups:, h * LANES : (h + 1) * LANES]
        first = jnp.where(lower, even, pltpu.roll(odd, BS, 1))
        second = jnp.where(lower, pltpu.roll(even, BS, 1), odd)
        square_ref[pl.ds(2 * h, groups, stride=BS), :] = first
        square_ref[pl.ds(2 * h + 1, groups, stride=BS), :] = second


def mirror_kernel(key_ref, blocks_ref, onsite_ref, near_ref, far_ref, flat_ref, square_ref):
    height = near_ref.shape[1]
    groups = square_ref.shape[0] // BS
    places = lax.broadcasted_iota(jnp.int32, (2 * groups, key_ref.shape[1]), 0)
    chosen = (places == key_ref[...]).astype(jnp.float32).astype(jnp.bfloat16)
    flat_ref[...] = jnp.dot(chosen, blocks_ref[...], preferred_element_type=jnp.float32)
    for p in range(PB):
        at = p * groups + p
        flat_ref[at : at + 1, :] += onsite_ref[p : p + 1, :].astype(jnp.float32)
    unflatten(flat_ref, square_ref, groups)
    devices = square_ref.shape[0] // height
    for d in range(devices):
        out = near_ref if d < devices // 2 else far_ref
        at = d % (devices // 2) * LANES
        square = square_ref[d * height : (d + 1) * height, :]
        out[at : at + LANES, :] = square.T.astype(jnp.bfloat16)


def mirror(key, blocks, onsite, rows, row_blocks):
    half = (rows // 2 * PB * BS, row_blocks * BS)
    groups = rows * row_blocks
    return pl.pallas_call(
        mirror_kernel,
        out_shape=(jax.ShapeDtypeStruct(half, jnp.bfloat16),) * 2,
        in_specs=[VMEM, VMEM, VMEM],
        out_specs=(VMEM, VMEM),
        scratch_shapes=[
            pltpu.VMEM((2 * groups, BS * BS), jnp.float32),
            pltpu.VMEM((groups * BS, LANES), jnp.float32),
        ],
        compiler_params=pltpu.CompilerParams(vmem_limit_bytes=40 * 1024 * 1024),
        cost_estimate=pl.CostEstimate(
            flops=4 * groups * blocks.size, bytes_accessed=3 * blocks.size, transcendentals=0
        ),
        name="mirror",
    )(key, blocks, onsite)


def direct_kernel(rows, slots, col_ref, blocks_ref, places_ref, *refs):
    cols = blocks_ref.shape[0]
    piece_refs, out_refs = refs[: cols - 1], refs[cols - 1 : -2]
    flat_ref, square_ref = refs[-2:]
    row_blocks = cols * PB
    groups = rows * row_blocks
    total = jnp.zeros((2 * groups, BS * BS), jnp.float32)
    height = blocks_ref.shape[1]
    for s in range(cols):
        if s == 0:
            place, blocks = places_of(places_ref, col_ref[0]), blocks_ref[col_ref[0]]
        else:
            piece = piece_refs[s - 1]
            place = piece[0:1, BS * BS : BS * BS + height].astype(jnp.float32)
            blocks = piece[:, : BS * BS]
        place = place.astype(jnp.int32)
        block = lax.broadcasted_iota(jnp.int32, (1, height), 1) // slots
        key = place % 2 * groups + place // 2 * row_blocks + s * PB + block
        key = jnp.where(place < 0, -1, key)
        ids = lax.broadcasted_iota(jnp.int32, (2 * groups, height), 0)
        chosen = (ids == key).astype(jnp.float32).astype(jnp.bfloat16)
        total += jnp.dot(chosen, blocks, preferred_element_type=jnp.float32)
    flat_ref[...] = total
    unflatten(flat_ref, square_ref, groups)
    for chip, out in enumerate(out_refs):
        for g in range(2 * cols):
            at = (chip * 2 * cols + g) * LANES
            out[:, g * LANES : (g + 1) * LANES] = square_ref[at : at + LANES, :].astype(
                jnp.bfloat16
            )


def direct_rows(col, blocks, places, pieces, rows, slots):
    cols = blocks.shape[0]
    groups = rows * cols * PB
    shape = jax.ShapeDtypeStruct((PB * BS, 2 * cols * LANES), jnp.bfloat16)
    return pl.pallas_call(
        functools.partial(direct_kernel, rows, slots),
        out_shape=(shape,) * (rows // 2),
        in_specs=[SMEM] + [VMEM] * (cols + 1),
        out_specs=(VMEM,) * (rows // 2),
        scratch_shapes=[
            pltpu.VMEM((2 * groups, BS * BS), jnp.float32),
            pltpu.VMEM((groups * BS, LANES), jnp.float32),
        ],
        compiler_params=pltpu.CompilerParams(vmem_limit_bytes=48 * 1024 * 1024),
        name="direct_rows",
    )(col, blocks, places, *pieces)


def local(orbitals_in, hblocks, block_cols, live_counts, onsite, cut_low, top_bound):
    rows = lax.axis_size("row")
    cols = lax.axis_size("col")
    chips = rows // 2
    row = lax.axis_index("row")
    col = lax.axis_index("col")
    chip, core = row // 2, row % 2
    row_blocks, slots, _ = hblocks.shape
    k = orbitals_in.shape[1]
    local_rows = PB * BS
    total_rows = rows * cols * local_rows
    near_rows = cols * local_rows

    live = jnp.arange(slots, dtype=jnp.int32)[None, :] < live_counts
    device, block = block_cols // PB, block_cols % PB
    apart = (device % 2) ^ core
    distance = (device // 2) ^ chip
    places = jnp.where(live, (distance * 2 + apart) * PB + block, -1).astype(jnp.float32)
    places = places.reshape(cols, PB * slots)
    block_row = jnp.arange(row_blocks, dtype=jnp.int32)[:, None]
    near_row = (col - block_row // PB) % cols * PB + block_row % PB
    groups = rows * row_blocks
    key = block * groups + (apart * chips + distance) * row_blocks + near_row
    key = jnp.where(live, key, -1).reshape(1, row_blocks * slots)

    by_owner = hblocks.reshape(cols, PB * slots, BS * BS)
    pieces = pack(col[None], by_owner, places)
    key, pieces = lax.optimization_barrier((key, pieces))
    pieces = [shifted(piece, "col", cols, s) for s, piece in enumerate(pieces, 1)]

    def gather_near(v):
        return jnp.concatenate([v] + [shifted(v, "col", cols, s) for s in range(1, cols)], 0)

    def gather_rows(v):
        near = gather_near(v)
        return near, core_swap(near, rows)

    def dot(a, b):
        return jnp.dot(a, b, preferred_element_type=jnp.float32)

    near, far = mirror(
        key, hblocks.reshape(row_blocks * slots, BS * BS), onsite, rows, row_blocks
    )

    direct = direct_rows(col[None], by_owner, places, pieces, rows, slots)
    far, direct = lax.optimization_barrier((far, direct))
    far = core_swap(far, rows)
    direct = [chip_swap(direct[s], rows, s) if s else direct[s] for s in range(chips)]
    first, far = lax.optimization_barrier((orbitals_in.astype(jnp.bfloat16), far))
    first_gathered = gather_rows(first)
    tile = jnp.concatenate([near, far], 1) + jnp.concatenate(direct, 0)
    tile_near, tile_far = tile[:, :near_rows], tile[:, near_rows:]

    def partial_product(gathered):
        near, far = gathered
        first, far = lax.optimization_barrier((dot(tile_near, near), far))
        return first + dot(tile_far, far)

    def apply(gathered):
        terms = partial_product(gathered).reshape(chips, local_rows, k)
        total = terms[0]
        for s in range(1, chips):
            total = total + chip_swap(terms[s], rows, s)
        return total

    centre = 0.5 * (top_bound[0] + cut_low[0])
    halfwidth = 0.5 * (top_bound[0] - cut_low[0])
    previous = orbitals_in
    current = (apply(first_gathered) - centre * orbitals_in) / halfwidth
    for degree in range(DEG - 1):
        gathered = gather_rows(current.astype(jnp.bfloat16))
        following = 2.0 * (apply(gathered) - centre * current) / halfwidth - previous
        previous, current = (current, following)

    rounded = current.astype(jnp.bfloat16)
    plane_rows = jnp.concatenate(
        [rounded] + [chip_swap(rounded, rows, s) for s in range(1, chips)], 0
    )
    near, plane_rows = lax.optimization_barrier((gather_near(rounded), plane_rows))
    gathered = near, core_swap(near, rows)
    contract = (((0,), (0,)), ((), ()))
    gram_part = lax.dot_general(
        gathered[0], gathered[0], contract, preferred_element_type=jnp.float32
    ) / cols
    cross_part = lax.dot_general(
        plane_rows.astype(jnp.float32), partial_product(gathered), contract, precision=HI
    )

    share = k // rows
    cross_part = cross_part + cross_part.T
    ids = jnp.arange(k, dtype=jnp.int32)
    packed = jnp.where(ids[:, None] <= ids[None, :], gram_part, cross_part)
    diagonal = jnp.sum(jnp.where(ids[:, None] == ids[None, :], cross_part, 0.0), 0)
    diagonal = jnp.broadcast_to(diagonal, (rows, 8, k))
    total = jnp.concatenate([packed.reshape(rows, share, k), diagonal], 1)
    total = total.reshape(chips, 2, share + 8, k)
    kept = jnp.where(core == 0, total[:, 0], total[:, 1])
    total = kept + core_swap(jnp.where(core == 0, total[:, 1], total[:, 0]), rows)
    total = by_distance(total, chip)
    total = sum([chip_swap(total[s], rows, s) for s in range(1, chips)], total[0])
    total = sum([shifted(total, "col", cols, s) for s in range(1, cols)], total)
    total = jnp.stack([total] + [chip_swap(total, rows, s) for s in range(1, chips)])
    total = by_distance(total, chip)
    other = core_swap(total, rows)
    pair = (jnp.where(core == 0, total, other), jnp.where(core == 0, other, total))
    total = jnp.stack(pair, 1).reshape(rows, share + 8, k)
    packed = total[:, :share].reshape(k, k)
    return finish(packed, total[0, share : share + 1], current, total_rows)


def solution(mesh):
    placed = (
        P(("row", "col"), None),
        P("row", "col", None),
        P("row", "col"),
        P("row", "col"),
        P(("row", "col"), None),
        P(),
        P(),
    )
    return jax.shard_map(
        local, mesh=mesh, in_specs=placed, out_specs=(P(("row", "col"), None), P()), check_vma=False
    )
```

```python
import functools

import jax
import jax.numpy as jnp
from jax import lax
from jax.experimental import pallas as pl
from jax.experimental.pallas import tpu as pltpu
from jax.sharding import PartitionSpec as P

BS = 64
PB = 2
DEG = 3
LANES = 128
PANEL = 32
HI = lax.Precision.HIGHEST
VMEM = pl.BlockSpec(memory_space=pltpu.VMEM)
SMEM = pl.BlockSpec(memory_space=pltpu.SMEM)


def widen(x, width):
    return jnp.concatenate([x] * (width // LANES), 1) if width > LANES else x

def reciprocal(x):
    return pl.reciprocal(x, approx=True)


def finish_kernel(total_rows, gram_ref, cross_ref, y_ref, orbitals_ref, projected_ref, inverse_ref):
    k = gram_ref.shape[0]
    panels = k // PANEL
    row_id = lax.broadcasted_iota(jnp.int32, (PANEL, LANES), 0)
    scale = 1.0 / total_rows
    upper = [gram_ref[m * PANEL:(m + 1) * PANEL, :] * scale for m in range(panels)]
    inverse = []
    for m in range(panels):
        r = lax.broadcasted_iota(jnp.int32, (PANEL, k), 0) + m * PANEL
        inverse.append((r == lax.broadcasted_iota(jnp.int32, (PANEL, k), 1)).astype(jnp.float32))
    for p in range(panels):
        start = p * PANEL
        s_lo = start // LANES * LANES
        w_hi = (start + PANEL + LANES - 1) // LANES * LANES
        s, w = upper[p][:, s_lo:], inverse[p][:, :w_hi]
        columns = [
            jnp.broadcast_to(s[:, start - s_lo + t:start - s_lo + t + 1], (PANEL, LANES))
            for t in range(PANEL)
        ]
        s_done, w_done = [], []
        for base in range(0, PANEL, 8):
            ids = row_id[: PANEL - base]
            pivots = jnp.zeros((8, LANES), jnp.float32)
            for t in range(base, base + 8, 2):
                at = t - base
                one, two = columns[t], columns[t + 1]
                a, b, d = one[at:at + 1, :], one[at + 1:at + 2, :], two[at + 1:at + 2, :]
                det = a * d - b * b
                det_inv = reciprocal(det)
                a_inv = reciprocal(a)
                pivots = jnp.where(ids[:8] == at, a, pivots)
                pivots = jnp.where(ids[:8] == at + 1, det * a_inv, pivots)
                below = ids > at + 1
                one_below = jnp.where(below, one, 0.0)
                two_below = jnp.where(below, two, 0.0)
                first = (d * one - b * two) * det_inv
                second = (a * two - b * one) * det_inv
                for j in range(t + 2, PANEL):
                    r = j - base
                    if j < t + 4:
                        p1, p2 = one[r:r + 1, :], two[r:r + 1, :]
                        m1, m2 = (d * p1 - b * p2) * det_inv, (a * p2 - b * p1) * det_inv
                    else:
                        m1, m2 = first[r:r + 1, :], second[r:r + 1, :]
                    columns[j] = columns[j] - (one_below * m1 + two_below * m2)
                first = jnp.where(below, first, jnp.where(ids == at + 1, b * a_inv, 0.0))
                second = jnp.where(below, second, 0.0)
                s = s - (
                    widen(first, s.shape[1]) * s[at:at + 1, :]
                    + widen(second, s.shape[1]) * s[at + 1:at + 2, :]
                )
                w = w - (
                    widen(first, w.shape[1]) * w[at:at + 1, :]
                    + widen(second, w.shape[1]) * w[at + 1:at + 2, :]
                )
            root = lax.rsqrt(pivots)
            s_done.append(s[:8] * widen(root, s.shape[1]))
            w_done.append(w[:8] * widen(root, w.shape[1]))
            s, w = s[8:], w[8:]
            columns = [c[8:] for c in columns]
        s = jnp.concatenate(s_done, 0)
        w = jnp.concatenate(w_done, 0)
        inverse_ref[start:start + PANEL, :w_hi] = w
        if w_hi < k:
            inverse_ref[start:start + PANEL, w_hi:] = jnp.zeros((PANEL, k - w_hi), jnp.float32)
        if p == panels - 1:
            break
        st = s.T
        for lo, hi in ((p + 1, p + 2), (p + 2, panels)):
            if lo >= hi:
                continue
            left = st[lo * PANEL - s_lo:hi * PANEL - s_lo, :]
            s_lo2 = lo * PANEL // LANES * LANES
            ds = jnp.dot(left, s[:, s_lo2 - s_lo:], precision=HI, preferred_element_type=jnp.float32)
            dw = jnp.dot(left, w, precision=HI, preferred_element_type=jnp.float32)
            for m in range(lo, hi):
                o = (m - lo) * PANEL
                a = upper[m][:, s_lo2:] - ds[o:o + PANEL, :]
                upper[m] = a if s_lo2 == 0 else jnp.concatenate([upper[m][:, :s_lo2], a], 1)
                b = inverse[m][:, :w_hi] - dw[o:o + PANEL, :]
                inverse[m] = b if w_hi == k else jnp.concatenate([b, inverse[m][:, w_hi:]], 1)
    inv = inverse_ref[...]
    nt = (((1,), (1,)), ((), ()))
    orbitals_ref[...] = lax.dot_general(y_ref[...], inv, nt, precision=HI, preferred_element_type=jnp.float32)
    half = jnp.dot(inv, cross_ref[...], precision=HI, preferred_element_type=jnp.float32)
    full = lax.dot_general(half, inv, nt, precision=HI, preferred_element_type=jnp.float32)
    projected_ref[...] = (full + full.T) * (0.5 * scale)

def finish(gram, cross, y, total_rows):
    k = gram.shape[0]
    f32 = jnp.float32
    return pl.pallas_call(
        functools.partial(finish_kernel, total_rows),
        out_shape=(jax.ShapeDtypeStruct(y.shape, f32), jax.ShapeDtypeStruct((k, k), f32)),
        in_specs=[pl.BlockSpec(memory_space=pltpu.VMEM)] * 3,
        out_specs=(pl.BlockSpec(memory_space=pltpu.VMEM),) * 2,
        scratch_shapes=[pltpu.VMEM((k, k), f32)],
        compiler_params=pltpu.CompilerParams(vmem_limit_bytes=32 * 1024 * 1024),
        name="finish",
    )(gram, cross, y)


def exchanged(x, axis, size, apart):
    return lax.ppermute(x, axis, [(i, i ^ apart) for i in range(size)])


def shifted(x, axis, size, step):
    return lax.ppermute(x, axis, [(i, (i + step) % size) for i in range(size)])


def core_swap(x, rows):
    return exchanged(x, "row", rows, 1)


def chip_swap(x, rows, apart):
    return exchanged(x, "row", rows, 2 * apart)


def by_distance(x, index):
    size = x.shape[0]
    bit = 1
    while bit < size:
        pairs = x.reshape(size // (2 * bit), 2, bit, *x.shape[1:])
        flipped = jnp.stack([pairs[:, 1], pairs[:, 0]], 1).reshape(x.shape)
        x = jnp.where((index // bit) % 2 == 1, flipped, x)
        bit *= 2
    return x


def places_of(places_ref, owner):
    ids = lax.broadcasted_iota(jnp.int32, places_ref.shape, 0)
    return jnp.sum(jnp.where(ids == owner, places_ref[...], 0.0), 0, keepdims=True)


def pack_kernel(col_ref, blocks_ref, places_ref, *piece_refs):
    cols = len(piece_refs) + 1
    for s, piece in enumerate(piece_refs, 1):
        owner = lax.rem(col_ref[0] + s, cols)
        piece[:, : BS * BS] = blocks_ref[owner]
        count = places_ref.shape[1]
        row = jnp.broadcast_to(places_of(places_ref, owner), (piece.shape[0], count))
        piece[:, BS * BS : BS * BS + count] = row.astype(jnp.bfloat16)


def pack(col, blocks, places):
    cols, height, _ = blocks.shape
    shape = jax.ShapeDtypeStruct((height, BS * BS + LANES), jnp.bfloat16)
    return pl.pallas_call(
        pack_kernel,
        out_shape=(shape,) * (cols - 1),
        in_specs=[SMEM, VMEM, VMEM],
        out_specs=(VMEM,) * (cols - 1),
        name="pack",
    )(col, blocks, places)


def unflatten(flat_ref, square_ref, groups):
    lower = lax.broadcasted_iota(jnp.int32, (groups, LANES), 1) < BS
    for h in range(BS * BS // LANES):
        even = flat_ref[:groups, h * LANES : (h + 1) * LANES]
        odd = flat_ref[groups:, h * LANES : (h + 1) * LANES]
        first = jnp.where(lower, even, pltpu.roll(odd, BS, 1))
        second = jnp.where(lower, pltpu.roll(even, BS, 1), odd)
        square_ref[pl.ds(2 * h, groups, stride=BS), :] = first
        square_ref[pl.ds(2 * h + 1, groups, stride=BS), :] = second


def mirror_kernel(key_ref, blocks_ref, onsite_ref, out_ref, flat_ref, square_ref):
    height = out_ref.shape[2]
    groups = square_ref.shape[0] // BS
    places = lax.broadcasted_iota(jnp.int32, (2 * groups, key_ref.shape[1]), 0)
    chosen = (places == key_ref[...]).astype(jnp.float32).astype(jnp.bfloat16)
    flat_ref[...] = jnp.dot(chosen, blocks_ref[...], preferred_element_type=jnp.float32)
    for p in range(PB):
        at = p * groups + p
        flat_ref[at : at + 1, :] += onsite_ref[p : p + 1, :].astype(jnp.float32)
    unflatten(flat_ref, square_ref, groups)
    devices = square_ref.shape[0] // height
    for d in range(devices):
        which, at = d // (devices // 2), d % (devices // 2) * LANES
        square = square_ref[d * height : (d + 1) * height, :]
        out_ref[which, at : at + LANES, :] = square.T.astype(jnp.bfloat16)


def mirror(key, blocks, onsite, rows, row_blocks):
    shape = (2, rows // 2 * PB * BS, row_blocks * BS)
    groups = rows * row_blocks
    return pl.pallas_call(
        mirror_kernel,
        out_shape=jax.ShapeDtypeStruct(shape, jnp.bfloat16),
        in_specs=[VMEM, VMEM, VMEM],
        out_specs=VMEM,
        scratch_shapes=[
            pltpu.VMEM((2 * groups, BS * BS), jnp.float32),
            pltpu.VMEM((groups * BS, LANES), jnp.float32),
        ],
        compiler_params=pltpu.CompilerParams(vmem_limit_bytes=40 * 1024 * 1024),
        cost_estimate=pl.CostEstimate(
            flops=4 * groups * blocks.size, bytes_accessed=3 * blocks.size, transcendentals=0
        ),
        name="mirror",
    )(key, blocks, onsite)


def direct_kernel(rows, slots, col_ref, blocks_ref, places_ref, *refs):
    cols = blocks_ref.shape[0]
    piece_refs, out_refs = refs[: cols - 1], refs[cols - 1 : -2]
    flat_ref, square_ref = refs[-2:]
    row_blocks = cols * PB
    groups = rows * row_blocks
    total = jnp.zeros((2 * groups, BS * BS), jnp.float32)
    height = blocks_ref.shape[1]
    for s in range(cols):
        if s == 0:
            place, blocks = places_of(places_ref, col_ref[0]), blocks_ref[col_ref[0]]
        else:
            piece = piece_refs[s - 1]
            place = piece[0:1, BS * BS : BS * BS + height].astype(jnp.float32)
            blocks = piece[:, : BS * BS]
        place = place.astype(jnp.int32)
        block = lax.broadcasted_iota(jnp.int32, (1, height), 1) // slots
        key = place % 2 * groups + place // 2 * row_blocks + s * PB + block
        key = jnp.where(place < 0, -1, key)
        ids = lax.broadcasted_iota(jnp.int32, (2 * groups, height), 0)
        chosen = (ids == key).astype(jnp.float32).astype(jnp.bfloat16)
        total += jnp.dot(chosen, blocks, preferred_element_type=jnp.float32)
    flat_ref[...] = total
    unflatten(flat_ref, square_ref, groups)
    for chip, out in enumerate(out_refs):
        for g in range(2 * cols):
            at = (chip * 2 * cols + g) * LANES
            lane = (g % cols * 2 + g // cols) * LANES
            out[:, lane : lane + LANES] = square_ref[at : at + LANES, :].astype(jnp.bfloat16)


def direct_rows(col, blocks, places, pieces, rows, slots):
    cols = blocks.shape[0]
    groups = rows * cols * PB
    shape = jax.ShapeDtypeStruct((PB * BS, 2 * cols * LANES), jnp.bfloat16)
    return pl.pallas_call(
        functools.partial(direct_kernel, rows, slots),
        out_shape=(shape,) * (rows // 2),
        in_specs=[SMEM] + [VMEM] * (cols + 1),
        out_specs=(VMEM,) * (rows // 2),
        scratch_shapes=[
            pltpu.VMEM((2 * groups, BS * BS), jnp.float32),
            pltpu.VMEM((groups * BS, LANES), jnp.float32),
        ],
        compiler_params=pltpu.CompilerParams(vmem_limit_bytes=48 * 1024 * 1024),
        name="direct_rows",
    )(col, blocks, places, *pieces)


def assemble_kernel(mirrored, mirrored_other, *refs):
    chips = (len(refs) - 1) // 2
    tile = refs[-1]
    size = PB * BS
    cols = mirrored.shape[2] // size
    for chip in range(chips):
        for j in range(2):
            sources = mirrored.at[j], mirrored_other.at[1 - j]
            direct = refs[j * chips + chip]
            rows = slice(chip * size, (chip + 1) * size)
            out_rows = slice((2 * chip + j) * size, (2 * chip + j + 1) * size)
            for s in range(cols):
                for i in range(2):
                    taken = (2 * s + (i ^ j)) * size
                    lane = (2 * s + i) * size
                    tile[out_rows, lane : lane + size] = (
                        sources[i][rows, s * size : (s + 1) * size]
                        + direct[:, taken : taken + size]
                    )


def assemble(mirrored, mirrored_other, direct, direct_other):
    _, height, width = mirrored.shape
    args = (mirrored, mirrored_other, *direct, *direct_other)
    return pl.pallas_call(
        assemble_kernel,
        out_shape=jax.ShapeDtypeStruct((2 * height, 2 * width), jnp.bfloat16),
        in_specs=[VMEM] * len(args),
        out_specs=VMEM,
        compiler_params=pltpu.CompilerParams(vmem_limit_bytes=40 * 1024 * 1024),
        name="assemble",
    )(*args)


def local(orbitals_in, hblocks, block_cols, live_counts, onsite, cut_low, top_bound):
    rows = lax.axis_size("row")
    cols = lax.axis_size("col")
    chips = rows // 2
    row = lax.axis_index("row")
    col = lax.axis_index("col")
    chip, core = row // 2, row % 2
    row_blocks, slots, _ = hblocks.shape
    k = orbitals_in.shape[1]
    local_rows = PB * BS
    total_rows = rows * cols * local_rows

    live = jnp.arange(slots, dtype=jnp.int32)[None, :] < live_counts
    device, block = block_cols // PB, block_cols % PB
    apart = (device % 2) ^ core
    distance = (device // 2) ^ chip
    places = jnp.where(live, (distance * 2 + apart) * PB + block, -1).astype(jnp.float32)
    places = places.reshape(cols, PB * slots)
    block_row = jnp.arange(row_blocks, dtype=jnp.int32)[:, None]
    near_row = (col - block_row // PB) % cols * PB + block_row % PB
    groups = rows * row_blocks
    key = block * groups + (apart * chips + distance) * row_blocks + near_row
    key = jnp.where(live, key, -1).reshape(1, row_blocks * slots)

    half = k // 2
    first_core = core == 0

    def halves(x):
        low, high = x[:, :half], x[:, half:]
        return jnp.where(first_core, low, high), jnp.where(first_core, high, low)

    def joined(own, other, axis):
        ordered = jnp.concatenate([own, other], axis), jnp.concatenate([other, own], axis)
        return jnp.where(first_core, *ordered)

    own, other = halves(orbitals_in)
    start = jnp.concatenate([own, core_swap(other, rows)], 0)

    by_owner = hblocks.reshape(cols, PB * slots, BS * BS)
    pieces = pack(col[None], by_owner, places)
    key, pieces, start = lax.optimization_barrier((key, pieces, start))
    pieces = [shifted(piece, "col", cols, s) for s, piece in enumerate(pieces, 1)]

    def gather(v):
        return jnp.concatenate([v] + [shifted(v, "col", cols, s) for s in range(1, cols)], 0)

    def plane_gather(v):
        return jnp.concatenate([v] + [chip_swap(v, rows, s) for s in range(1, chips)], 0)

    def from_other_core(v):
        blocks = core_swap(v, rows).reshape(-1, 2, local_rows, half)
        return jnp.stack([blocks[:, 1], blocks[:, 0]], 1).reshape(v.shape)

    mirrored = mirror(
        key, hblocks.reshape(row_blocks * slots, BS * BS), onsite, rows, row_blocks
    )

    direct = direct_rows(col[None], by_owner, places, pieces, rows, slots)
    mirrored, direct = lax.optimization_barrier((mirrored, direct))
    mirrored_other = core_swap(mirrored, rows)
    direct = [chip_swap(direct[s], rows, s) if s else direct[s] for s in range(chips)]
    first, mirrored_other = lax.optimization_barrier(
        (start.astype(jnp.bfloat16), mirrored_other)
    )
    first_gathered, direct = lax.optimization_barrier((gather(first), direct))
    direct_other = [core_swap(rows_of_chip, rows) for rows_of_chip in direct]

    tile = assemble(mirrored, mirrored_other, direct, direct_other)

    def partial_product(gathered):
        return jnp.dot(tile, gathered, preferred_element_type=jnp.float32)

    def apply(gathered):
        terms = partial_product(gathered).reshape(chips, 2 * local_rows, half)
        total = terms[0]
        for s in range(1, chips):
            total = total + chip_swap(terms[s], rows, s)
        return total

    centre = 0.5 * (top_bound[0] + cut_low[0])
    halfwidth = 0.5 * (top_bound[0] - cut_low[0])
    previous = start
    current = (apply(first_gathered) - centre * start) / halfwidth
    for degree in range(DEG - 1):
        gathered = gather(current.astype(jnp.bfloat16))
        following = 2.0 * (apply(gathered) - centre * current) / halfwidth - previous
        previous, current = (current, following)

    rounded = current.astype(jnp.bfloat16)
    plane_rows = plane_gather(rounded)
    gathered, plane_rows = lax.optimization_barrier((gather(rounded), plane_rows))
    gathered_other = from_other_core(gathered)
    plane_other = from_other_core(plane_rows)
    filtered = joined(current[:local_rows], core_swap(current[local_rows:], rows), 1)
    contract = (((0,), (0,)), ((), ()))

    def gram_rows(g):
        return lax.dot_general(g, gathered, contract, preferred_element_type=jnp.float32)

    image = partial_product(gathered)

    def cross_rows(g):
        return lax.dot_general(g.astype(jnp.float32), image, contract, precision=HI)

    gram_part = jnp.concatenate([gram_rows(gathered), gram_rows(gathered_other)], 0)
    cross_part = jnp.concatenate([cross_rows(plane_rows), cross_rows(plane_other)], 0)
    share = k // chips
    parts = [x.reshape(chips, share, half) for x in (gram_part, cross_part)]
    parts = by_distance(jnp.stack(parts, 1), chip)
    total = sum([chip_swap(parts[s], rows, s) for s in range(1, chips)], parts[0])
    cross_share = sum([shifted(total[1], "col", cols, s) for s in range(1, cols)], total[1])
    total = jnp.stack([total[0], cross_share])
    total = jnp.stack([total] + [chip_swap(total, rows, s) for s in range(1, chips)])
    total = by_distance(total, chip).swapaxes(0, 1).reshape(2, k, half)
    total = joined(total[:, :half], total[:, half:], 1)
    total = joined(total, core_swap(total, rows), 2)
    return finish(total[0], total[1], filtered, total_rows)


def solution(mesh):
    placed = (
        P(("row", "col"), None),
        P("row", "col", None),
        P("row", "col"),
        P("row", "col"),
        P(("row", "col"), None),
        P(),
        P(),
    )
    return jax.shard_map(
        local, mesh=mesh, in_specs=placed, out_specs=(P(("row", "col"), None), P()), check_vma=False
    )
```

```python
import functools

import jax
import jax.numpy as jnp
from jax import lax
from jax.experimental import pallas as pl
from jax.experimental.pallas import tpu as pltpu
from jax.sharding import PartitionSpec as P

BS = 64
PB = 2
DEG = 3
LANES = 128
PANEL = 32
HI = lax.Precision.HIGHEST
VMEM = pl.BlockSpec(memory_space=pltpu.VMEM)
SMEM = pl.BlockSpec(memory_space=pltpu.SMEM)


def widen(x, width):
    return jnp.concatenate([x] * (width // LANES), 1) if width > LANES else x

def reciprocal(x):
    return pl.reciprocal(x, approx=True)


def finish_kernel(total_rows, gram_ref, cross_ref, y_ref, orbitals_ref, projected_ref, inverse_ref):
    k = gram_ref.shape[0]
    panels = k // PANEL
    row_id = lax.broadcasted_iota(jnp.int32, (PANEL, LANES), 0)
    scale = 1.0 / total_rows
    upper = [gram_ref[m * PANEL:(m + 1) * PANEL, :] * scale for m in range(panels)]
    inverse = []
    for m in range(panels):
        r = lax.broadcasted_iota(jnp.int32, (PANEL, k), 0) + m * PANEL
        inverse.append((r == lax.broadcasted_iota(jnp.int32, (PANEL, k), 1)).astype(jnp.float32))
    for p in range(panels):
        start = p * PANEL
        s_lo = start // LANES * LANES
        w_hi = (start + PANEL + LANES - 1) // LANES * LANES
        s, w = upper[p][:, s_lo:], inverse[p][:, :w_hi]
        columns = [
            jnp.broadcast_to(s[:, start - s_lo + t:start - s_lo + t + 1], (PANEL, LANES))
            for t in range(PANEL)
        ]
        s_done, w_done = [], []
        for base in range(0, PANEL, 8):
            ids = row_id[: PANEL - base]
            pivots = jnp.zeros((8, LANES), jnp.float32)
            for t in range(base, base + 8, 2):
                at = t - base
                one, two = columns[t], columns[t + 1]
                a, b, d = one[at:at + 1, :], one[at + 1:at + 2, :], two[at + 1:at + 2, :]
                det = a * d - b * b
                det_inv = reciprocal(det)
                a_inv = reciprocal(a)
                pivots = jnp.where(ids[:8] == at, a, pivots)
                pivots = jnp.where(ids[:8] == at + 1, det * a_inv, pivots)
                below = ids > at + 1
                one_below = jnp.where(below, one, 0.0)
                two_below = jnp.where(below, two, 0.0)
                first = (d * one - b * two) * det_inv
                second = (a * two - b * one) * det_inv
                for j in range(t + 2, PANEL):
                    r = j - base
                    if j < t + 4:
                        p1, p2 = one[r:r + 1, :], two[r:r + 1, :]
                        m1, m2 = (d * p1 - b * p2) * det_inv, (a * p2 - b * p1) * det_inv
                    else:
                        m1, m2 = first[r:r + 1, :], second[r:r + 1, :]
                    columns[j] = columns[j] - (one_below * m1 + two_below * m2)
                first = jnp.where(below, first, jnp.where(ids == at + 1, b * a_inv, 0.0))
                second = jnp.where(below, second, 0.0)
                s = s - (
                    widen(first, s.shape[1]) * s[at:at + 1, :]
                    + widen(second, s.shape[1]) * s[at + 1:at + 2, :]
                )
                w = w - (
                    widen(first, w.shape[1]) * w[at:at + 1, :]
                    + widen(second, w.shape[1]) * w[at + 1:at + 2, :]
                )
            root = lax.rsqrt(pivots)
            s_done.append(s[:8] * widen(root, s.shape[1]))
            w_done.append(w[:8] * widen(root, w.shape[1]))
            s, w = s[8:], w[8:]
            columns = [c[8:] for c in columns]
        s = jnp.concatenate(s_done, 0)
        w = jnp.concatenate(w_done, 0)
        inverse_ref[start:start + PANEL, :w_hi] = w
        if w_hi < k:
            inverse_ref[start:start + PANEL, w_hi:] = jnp.zeros((PANEL, k - w_hi), jnp.float32)
        if p == panels - 1:
            break
        st = s.T
        for lo, hi in ((p + 1, p + 2), (p + 2, panels)):
            if lo >= hi:
                continue
            left = st[lo * PANEL - s_lo:hi * PANEL - s_lo, :]
            s_lo2 = lo * PANEL // LANES * LANES
            ds = jnp.dot(left, s[:, s_lo2 - s_lo:], precision=HI, preferred_element_type=jnp.float32)
            dw = jnp.dot(left, w, precision=HI, preferred_element_type=jnp.float32)
            for m in range(lo, hi):
                o = (m - lo) * PANEL
                a = upper[m][:, s_lo2:] - ds[o:o + PANEL, :]
                upper[m] = a if s_lo2 == 0 else jnp.concatenate([upper[m][:, :s_lo2], a], 1)
                b = inverse[m][:, :w_hi] - dw[o:o + PANEL, :]
                inverse[m] = b if w_hi == k else jnp.concatenate([b, inverse[m][:, w_hi:]], 1)
    inv = inverse_ref[...]
    nt = (((1,), (1,)), ((), ()))
    orbitals_ref[...] = lax.dot_general(y_ref[...], inv, nt, precision=HI, preferred_element_type=jnp.float32)
    half = jnp.dot(inv, cross_ref[...], precision=HI, preferred_element_type=jnp.float32)
    full = lax.dot_general(half, inv, nt, precision=HI, preferred_element_type=jnp.float32)
    projected_ref[...] = (full + full.T) * (0.5 * scale)

def finish(gram, cross, y, total_rows):
    k = gram.shape[0]
    f32 = jnp.float32
    return pl.pallas_call(
        functools.partial(finish_kernel, total_rows),
        out_shape=(jax.ShapeDtypeStruct(y.shape, f32), jax.ShapeDtypeStruct((k, k), f32)),
        in_specs=[pl.BlockSpec(memory_space=pltpu.VMEM)] * 3,
        out_specs=(pl.BlockSpec(memory_space=pltpu.VMEM),) * 2,
        scratch_shapes=[pltpu.VMEM((k, k), f32)],
        compiler_params=pltpu.CompilerParams(vmem_limit_bytes=32 * 1024 * 1024),
        name="finish",
    )(gram, cross, y)


def exchanged(x, axis, size, apart):
    return lax.ppermute(x, axis, [(i, i ^ apart) for i in range(size)])


def shifted(x, axis, size, step):
    return lax.ppermute(x, axis, [(i, (i + step) % size) for i in range(size)])


def core_swap(x, rows):
    return exchanged(x, "row", rows, 1)


def chip_swap(x, rows, apart):
    return exchanged(x, "row", rows, 2 * apart)


def by_distance(x, index):
    size = x.shape[0]
    bit = 1
    while bit < size:
        pairs = x.reshape(size // (2 * bit), 2, bit, *x.shape[1:])
        flipped = jnp.stack([pairs[:, 1], pairs[:, 0]], 1).reshape(x.shape)
        x = jnp.where((index // bit) % 2 == 1, flipped, x)
        bit *= 2
    return x


def places_of(places_ref, owner):
    ids = lax.broadcasted_iota(jnp.int32, places_ref.shape, 0)
    return jnp.sum(jnp.where(ids == owner, places_ref[...], 0.0), 0, keepdims=True)


def pack_kernel(col_ref, blocks_ref, places_ref, *piece_refs):
    cols = len(piece_refs) + 1
    for s, piece in enumerate(piece_refs, 1):
        owner = lax.rem(col_ref[0] + s, cols)
        piece[:, : BS * BS] = blocks_ref[owner]
        count = places_ref.shape[1]
        row = jnp.broadcast_to(places_of(places_ref, owner), (piece.shape[0], count))
        piece[:, BS * BS : BS * BS + count] = row.astype(jnp.bfloat16)


def pack(col, blocks, places):
    cols, height, _ = blocks.shape
    shape = jax.ShapeDtypeStruct((height, BS * BS + LANES), jnp.bfloat16)
    return pl.pallas_call(
        pack_kernel,
        out_shape=(shape,) * (cols - 1),
        in_specs=[SMEM, VMEM, VMEM],
        out_specs=(VMEM,) * (cols - 1),
        name="pack",
    )(col, blocks, places)


def unflatten(flat_ref, square_ref, groups):
    lower = lax.broadcasted_iota(jnp.int32, (groups, LANES), 1) < BS
    for h in range(BS * BS // LANES):
        even = flat_ref[:groups, h * LANES : (h + 1) * LANES]
        odd = flat_ref[groups:, h * LANES : (h + 1) * LANES]
        first = jnp.where(lower, even, pltpu.roll(odd, BS, 1))
        second = jnp.where(lower, pltpu.roll(even, BS, 1), odd)
        square_ref[pl.ds(2 * h, groups, stride=BS), :] = first
        square_ref[pl.ds(2 * h + 1, groups, stride=BS), :] = second


def mirror_kernel(key_ref, blocks_ref, onsite_ref, out_ref, flat_ref, square_ref):
    height = out_ref.shape[2]
    groups = square_ref.shape[0] // BS
    places = lax.broadcasted_iota(jnp.int32, (2 * groups, key_ref.shape[1]), 0)
    chosen = (places == key_ref[...]).astype(jnp.float32).astype(jnp.bfloat16)
    flat_ref[...] = jnp.dot(chosen, blocks_ref[...], preferred_element_type=jnp.float32)
    for p in range(PB):
        at = p * groups + p
        flat_ref[at : at + 1, :] += onsite_ref[p : p + 1, :].astype(jnp.float32)
    unflatten(flat_ref, square_ref, groups)
    devices = square_ref.shape[0] // height
    for d in range(devices):
        which, at = d // (devices // 2), d % (devices // 2) * LANES
        square = square_ref[d * height : (d + 1) * height, :]
        out_ref[which, at : at + LANES, :] = square.T.astype(jnp.bfloat16)


def mirror(key, blocks, onsite, rows, row_blocks):
    shape = (2, rows // 2 * PB * BS, row_blocks * BS)
    groups = rows * row_blocks
    return pl.pallas_call(
        mirror_kernel,
        out_shape=jax.ShapeDtypeStruct(shape, jnp.bfloat16),
        in_specs=[VMEM, VMEM, VMEM],
        out_specs=VMEM,
        scratch_shapes=[
            pltpu.VMEM((2 * groups, BS * BS), jnp.float32),
            pltpu.VMEM((groups * BS, LANES), jnp.float32),
        ],
        compiler_params=pltpu.CompilerParams(vmem_limit_bytes=40 * 1024 * 1024),
        cost_estimate=pl.CostEstimate(
            flops=4 * groups * blocks.size, bytes_accessed=3 * blocks.size, transcendentals=0
        ),
        name="mirror",
    )(key, blocks, onsite)


def direct_kernel(rows, slots, col_ref, blocks_ref, places_ref, *refs):
    cols = blocks_ref.shape[0]
    piece_refs, out_refs = refs[: cols - 1], refs[cols - 1 : -2]
    flat_ref, square_ref = refs[-2:]
    row_blocks = cols * PB
    groups = rows * row_blocks
    total = jnp.zeros((2 * groups, BS * BS), jnp.float32)
    height = blocks_ref.shape[1]
    for s in range(cols):
        if s == 0:
            place, blocks = places_of(places_ref, col_ref[0]), blocks_ref[col_ref[0]]
        else:
            piece = piece_refs[s - 1]
            place = piece[0:1, BS * BS : BS * BS + height].astype(jnp.float32)
            blocks = piece[:, : BS * BS]
        place = place.astype(jnp.int32)
        block = lax.broadcasted_iota(jnp.int32, (1, height), 1) // slots
        key = place % 2 * groups + place // 2 * row_blocks + s * PB + block
        key = jnp.where(place < 0, -1, key)
        ids = lax.broadcasted_iota(jnp.int32, (2 * groups, height), 0)
        chosen = (ids == key).astype(jnp.float32).astype(jnp.bfloat16)
        total += jnp.dot(chosen, blocks, preferred_element_type=jnp.float32)
    flat_ref[...] = total
    unflatten(flat_ref, square_ref, groups)
    for chip, out in enumerate(out_refs):
        for g in range(2 * cols):
            at = (chip * 2 * cols + g) * LANES
            lane = (g % cols * 2 + g // cols) * LANES
            out[:, lane : lane + LANES] = square_ref[at : at + LANES, :].astype(jnp.bfloat16)


def direct_rows(col, blocks, places, pieces, rows, slots):
    cols = blocks.shape[0]
    groups = rows * cols * PB
    shape = jax.ShapeDtypeStruct((PB * BS, 2 * cols * LANES), jnp.bfloat16)
    return pl.pallas_call(
        functools.partial(direct_kernel, rows, slots),
        out_shape=(shape,) * (rows // 2),
        in_specs=[SMEM] + [VMEM] * (cols + 1),
        out_specs=(VMEM,) * (rows // 2),
        scratch_shapes=[
            pltpu.VMEM((2 * groups, BS * BS), jnp.float32),
            pltpu.VMEM((groups * BS, LANES), jnp.float32),
        ],
        compiler_params=pltpu.CompilerParams(vmem_limit_bytes=48 * 1024 * 1024),
        name="direct_rows",
    )(col, blocks, places, *pieces)


def assemble_kernel(mirrored, mirrored_other, *refs):
    chips = (len(refs) - 1) // 2
    tile = refs[-1]
    size = PB * BS
    cols = mirrored.shape[2] // size
    for chip in range(chips):
        for j in range(2):
            sources = mirrored.at[j], mirrored_other.at[1 - j]
            direct = refs[j * chips + chip]
            rows = slice(chip * size, (chip + 1) * size)
            out_rows = slice((2 * chip + j) * size, (2 * chip + j + 1) * size)
            for s in range(cols):
                for i in range(2):
                    taken = (2 * s + (i ^ j)) * size
                    lane = (2 * s + i) * size
                    tile[out_rows, lane : lane + size] = (
                        sources[i][rows, s * size : (s + 1) * size]
                        + direct[:, taken : taken + size]
                    )


def assemble(mirrored, mirrored_other, direct, direct_other):
    _, height, width = mirrored.shape
    args = (mirrored, mirrored_other, *direct, *direct_other)
    return pl.pallas_call(
        assemble_kernel,
        out_shape=jax.ShapeDtypeStruct((2 * height, 2 * width), jnp.bfloat16),
        in_specs=[VMEM] * len(args),
        out_specs=VMEM,
        compiler_params=pltpu.CompilerParams(vmem_limit_bytes=40 * 1024 * 1024),
        name="assemble",
    )(*args)


def local(orbitals_in, hblocks, block_cols, live_counts, onsite, cut_low, top_bound):
    rows = lax.axis_size("row")
    cols = lax.axis_size("col")
    chips = rows // 2
    row = lax.axis_index("row")
    col = lax.axis_index("col")
    chip, core = row // 2, row % 2
    row_blocks, slots, _ = hblocks.shape
    k = orbitals_in.shape[1]
    local_rows = PB * BS
    total_rows = rows * cols * local_rows

    live = jnp.arange(slots, dtype=jnp.int32)[None, :] < live_counts
    device, block = block_cols // PB, block_cols % PB
    apart = (device % 2) ^ core
    distance = (device // 2) ^ chip
    places = jnp.where(live, (distance * 2 + apart) * PB + block, -1).astype(jnp.float32)
    places = places.reshape(cols, PB * slots)
    block_row = jnp.arange(row_blocks, dtype=jnp.int32)[:, None]
    near_row = (col - block_row // PB) % cols * PB + block_row % PB
    groups = rows * row_blocks
    key = block * groups + (apart * chips + distance) * row_blocks + near_row
    key = jnp.where(live, key, -1).reshape(1, row_blocks * slots)

    half = k // 2
    first_core = core == 0

    def halves(x):
        low, high = x[:, :half], x[:, half:]
        return jnp.where(first_core, low, high), jnp.where(first_core, high, low)

    def joined(own, other, axis):
        ordered = jnp.concatenate([own, other], axis), jnp.concatenate([other, own], axis)
        return jnp.where(first_core, *ordered)

    own, other = halves(orbitals_in)
    start = jnp.concatenate([own, core_swap(other, rows)], 0)

    by_owner = hblocks.reshape(cols, PB * slots, BS * BS)
    pieces = pack(col[None], by_owner, places)
    key, pieces, start = lax.optimization_barrier((key, pieces, start))
    pieces = [shifted(piece, "col", cols, s) for s, piece in enumerate(pieces, 1)]

    def gather(v):
        return jnp.concatenate([v] + [shifted(v, "col", cols, s) for s in range(1, cols)], 0)

    def plane_gather(v):
        return jnp.concatenate([v] + [chip_swap(v, rows, s) for s in range(1, chips)], 0)

    def from_other_core(v):
        blocks = core_swap(v, rows).reshape(-1, 2, local_rows, half)
        return jnp.stack([blocks[:, 1], blocks[:, 0]], 1).reshape(v.shape)

    mirrored = mirror(
        key, hblocks.reshape(row_blocks * slots, BS * BS), onsite, rows, row_blocks
    )

    direct = direct_rows(col[None], by_owner, places, pieces, rows, slots)
    mirrored, direct = lax.optimization_barrier((mirrored, direct))
    mirrored_other = core_swap(mirrored, rows)
    direct = [chip_swap(direct[s], rows, s) if s else direct[s] for s in range(chips)]
    first, mirrored_other = lax.optimization_barrier(
        (start.astype(jnp.bfloat16), mirrored_other)
    )
    def last_piece(v, of_core):
        return lax.ppermute(
            v,
            ("row", "col"),
            [
                (r * cols + i, r * cols + (i + cols - 1) % cols)
                for r in range(of_core, rows, 2)
                for i in range(cols)
            ],
        )

    early = [shifted(first, "col", cols, s) for s in range(1, cols - 1)] + [last_piece(first, 0)]
    early, direct = lax.optimization_barrier((early, direct))
    direct_other = [core_swap(rows_of_chip, rows) for rows_of_chip in direct]

    tile = assemble(mirrored, mirrored_other, direct, direct_other)

    tile, first = lax.optimization_barrier((tile, first))
    last = jnp.where(first_core, early[-1], last_piece(first, 1))
    first_gathered = jnp.concatenate([first] + early[:-1] + [last], 0)

    def partial_product(gathered):
        return jnp.dot(tile, gathered, preferred_element_type=jnp.float32)

    def apply(gathered):
        terms = partial_product(gathered).reshape(chips, 2 * local_rows, half)
        total = terms[0]
        for s in range(1, chips):
            total = total + chip_swap(terms[s], rows, s)
        return total

    centre = 0.5 * (top_bound[0] + cut_low[0])
    halfwidth = 0.5 * (top_bound[0] - cut_low[0])
    previous = start
    current = (apply(first_gathered) - centre * start) / halfwidth
    for degree in range(DEG - 1):
        gathered = gather(current.astype(jnp.bfloat16))
        following = 2.0 * (apply(gathered) - centre * current) / halfwidth - previous
        previous, current = (current, following)

    rounded = current.astype(jnp.bfloat16)
    plane_rows = plane_gather(rounded)
    gathered, plane_rows = lax.optimization_barrier((gather(rounded), plane_rows))
    gathered_other = from_other_core(gathered)
    plane_other = from_other_core(plane_rows)
    filtered = joined(current[:local_rows], core_swap(current[local_rows:], rows), 1)
    contract = (((0,), (0,)), ((), ()))

    def gram_rows(g):
        return lax.dot_general(g, gathered, contract, preferred_element_type=jnp.float32)

    image = partial_product(gathered)

    def cross_rows(g):
        return lax.dot_general(g.astype(jnp.float32), image, contract, precision=HI)

    gram_part = jnp.concatenate([gram_rows(gathered), gram_rows(gathered_other)], 0)
    cross_part = jnp.concatenate([cross_rows(plane_rows), cross_rows(plane_other)], 0)
    share = k // chips
    parts = [x.reshape(chips, share, half) for x in (gram_part, cross_part)]
    parts = by_distance(jnp.stack(parts, 1), chip)
    total = sum([chip_swap(parts[s], rows, s) for s in range(1, chips)], parts[0])
    cross_share = sum([shifted(total[1], "col", cols, s) for s in range(1, cols)], total[1])
    total = jnp.stack([total[0], cross_share])
    total = jnp.stack([total] + [chip_swap(total, rows, s) for s in range(1, chips)])
    total = by_distance(total, chip).swapaxes(0, 1).reshape(2, k, half)
    total = joined(total[:, :half], total[:, half:], 1)
    total = joined(total, core_swap(total, rows), 2)
    return finish(total[0], total[1], filtered, total_rows)


def solution(mesh):
    placed = (
        P(("row", "col"), None),
        P("row", "col", None),
        P("row", "col"),
        P("row", "col"),
        P(("row", "col"), None),
        P(),
        P(),
    )
    return jax.shard_map(
        local, mesh=mesh, in_specs=placed, out_specs=(P(("row", "col"), None), P()), check_vma=False
    )
```

```python
import functools

import jax
import jax.numpy as jnp
from jax import lax
from jax.experimental import pallas as pl
from jax.experimental.pallas import tpu as pltpu
from jax.sharding import PartitionSpec as P

BS = 64
PB = 2
DEG = 3
LANES = 128
PANEL = 32
HI = lax.Precision.HIGHEST
VMEM = pl.BlockSpec(memory_space=pltpu.VMEM)
SMEM = pl.BlockSpec(memory_space=pltpu.SMEM)


def widen(x, width):
    return jnp.concatenate([x] * (width // LANES), 1) if width > LANES else x

def reciprocal(x):
    return pl.reciprocal(x, approx=True)


def factor_kernel(total_rows, gram_ref, y_ref, orbitals_ref, inverse_ref):
    k = gram_ref.shape[0]
    panels = k // PANEL
    row_id = lax.broadcasted_iota(jnp.int32, (PANEL, LANES), 0)
    scale = 1.0 / total_rows
    upper = [gram_ref[m * PANEL:(m + 1) * PANEL, :] * scale for m in range(panels)]
    inverse = []
    for m in range(panels):
        r = lax.broadcasted_iota(jnp.int32, (PANEL, k), 0) + m * PANEL
        inverse.append((r == lax.broadcasted_iota(jnp.int32, (PANEL, k), 1)).astype(jnp.float32))
    for p in range(panels):
        start = p * PANEL
        s_lo = start // LANES * LANES
        w_hi = (start + PANEL + LANES - 1) // LANES * LANES
        s, w = upper[p][:, s_lo:], inverse[p][:, :w_hi]
        columns = [
            jnp.broadcast_to(s[:, start - s_lo + t:start - s_lo + t + 1], (PANEL, LANES))
            for t in range(PANEL)
        ]
        s_done, w_done = [], []
        for base in range(0, PANEL, 8):
            ids = row_id[: PANEL - base]
            pivots = jnp.zeros((8, LANES), jnp.float32)
            for t in range(base, base + 8, 2):
                at = t - base
                one, two = columns[t], columns[t + 1]
                a, b, d = one[at:at + 1, :], one[at + 1:at + 2, :], two[at + 1:at + 2, :]
                det = a * d - b * b
                det_inv = reciprocal(det)
                a_inv = reciprocal(a)
                pivots = jnp.where(ids[:8] == at, a, pivots)
                pivots = jnp.where(ids[:8] == at + 1, det * a_inv, pivots)
                below = ids > at + 1
                one_below = jnp.where(below, one, 0.0)
                two_below = jnp.where(below, two, 0.0)
                first = (d * one - b * two) * det_inv
                second = (a * two - b * one) * det_inv
                for j in range(t + 2, PANEL):
                    r = j - base
                    if j < t + 4:
                        p1, p2 = one[r:r + 1, :], two[r:r + 1, :]
                        m1, m2 = (d * p1 - b * p2) * det_inv, (a * p2 - b * p1) * det_inv
                    else:
                        m1, m2 = first[r:r + 1, :], second[r:r + 1, :]
                    columns[j] = columns[j] - (one_below * m1 + two_below * m2)
                first = jnp.where(below, first, jnp.where(ids == at + 1, b * a_inv, 0.0))
                second = jnp.where(below, second, 0.0)
                s = s - (
                    widen(first, s.shape[1]) * s[at:at + 1, :]
                    + widen(second, s.shape[1]) * s[at + 1:at + 2, :]
                )
                w = w - (
                    widen(first, w.shape[1]) * w[at:at + 1, :]
                    + widen(second, w.shape[1]) * w[at + 1:at + 2, :]
                )
            root = lax.rsqrt(pivots)
            s_done.append(s[:8] * widen(root, s.shape[1]))
            w_done.append(w[:8] * widen(root, w.shape[1]))
            s, w = s[8:], w[8:]
            columns = [c[8:] for c in columns]
        s = jnp.concatenate(s_done, 0)
        w = jnp.concatenate(w_done, 0)
        inverse_ref[start:start + PANEL, :w_hi] = w
        if w_hi < k:
            inverse_ref[start:start + PANEL, w_hi:] = jnp.zeros((PANEL, k - w_hi), jnp.float32)
        if p == panels - 1:
            break
        st = s.T
        for lo, hi in ((p + 1, p + 2), (p + 2, panels)):
            if lo >= hi:
                continue
            left = st[lo * PANEL - s_lo:hi * PANEL - s_lo, :]
            s_lo2 = lo * PANEL // LANES * LANES
            ds = jnp.dot(left, s[:, s_lo2 - s_lo:], precision=HI, preferred_element_type=jnp.float32)
            dw = jnp.dot(left, w, precision=HI, preferred_element_type=jnp.float32)
            for m in range(lo, hi):
                o = (m - lo) * PANEL
                a = upper[m][:, s_lo2:] - ds[o:o + PANEL, :]
                upper[m] = a if s_lo2 == 0 else jnp.concatenate([upper[m][:, :s_lo2], a], 1)
                b = inverse[m][:, :w_hi] - dw[o:o + PANEL, :]
                inverse[m] = b if w_hi == k else jnp.concatenate([b, inverse[m][:, w_hi:]], 1)
    inv = inverse_ref[...]
    nt = (((1,), (1,)), ((), ()))
    orbitals_ref[...] = lax.dot_general(y_ref[...], inv, nt, precision=HI, preferred_element_type=jnp.float32)


def project_kernel(total_rows, inverse_ref, cross_ref, projected_ref):
    inv = inverse_ref[...]
    nt = (((1,), (1,)), ((), ()))
    half = jnp.dot(inv, cross_ref[...], precision=HI, preferred_element_type=jnp.float32)
    full = lax.dot_general(half, inv, nt, precision=HI, preferred_element_type=jnp.float32)
    projected_ref[...] = (full + full.T) * (0.5 / total_rows)


def factorize(gram, y, total_rows):
    k = gram.shape[0]
    f32 = jnp.float32
    return pl.pallas_call(
        functools.partial(factor_kernel, total_rows),
        out_shape=(jax.ShapeDtypeStruct(y.shape, f32), jax.ShapeDtypeStruct((k, k), f32)),
        in_specs=[VMEM] * 2,
        out_specs=(VMEM,) * 2,
        compiler_params=pltpu.CompilerParams(vmem_limit_bytes=32 * 1024 * 1024),
        cost_estimate=pl.CostEstimate(
            flops=0, bytes_accessed=80 * gram.size, transcendentals=0
        ),
        name="factorize",
    )(gram, y)


def project(inverse, cross, total_rows):
    return pl.pallas_call(
        functools.partial(project_kernel, total_rows),
        out_shape=jax.ShapeDtypeStruct(cross.shape, jnp.float32),
        in_specs=[VMEM] * 2,
        out_specs=VMEM,
        compiler_params=pltpu.CompilerParams(vmem_limit_bytes=32 * 1024 * 1024),
        name="project",
    )(inverse, cross)


def exchanged(x, axis, size, apart):
    return lax.ppermute(x, axis, [(i, i ^ apart) for i in range(size)])


def shifted(x, axis, size, step):
    return lax.ppermute(x, axis, [(i, (i + step) % size) for i in range(size)])


def core_swap(x, rows):
    return exchanged(x, "row", rows, 1)


def chip_swap(x, rows, apart):
    return exchanged(x, "row", rows, 2 * apart)


def by_distance(x, index):
    size = x.shape[0]
    bit = 1
    while bit < size:
        pairs = x.reshape(size // (2 * bit), 2, bit, *x.shape[1:])
        flipped = jnp.stack([pairs[:, 1], pairs[:, 0]], 1).reshape(x.shape)
        x = jnp.where((index // bit) % 2 == 1, flipped, x)
        bit *= 2
    return x


def places_of(places_ref, owner):
    ids = lax.broadcasted_iota(jnp.int32, places_ref.shape, 0)
    return jnp.sum(jnp.where(ids == owner, places_ref[...], 0.0), 0, keepdims=True)


def pack_kernel(col_ref, blocks_ref, places_ref, *piece_refs):
    cols = len(piece_refs) + 1
    for s, piece in enumerate(piece_refs, 1):
        owner = lax.rem(col_ref[0] + s, cols)
        piece[:, : BS * BS] = blocks_ref[owner]
        count = places_ref.shape[1]
        row = jnp.broadcast_to(places_of(places_ref, owner), (piece.shape[0], count))
        piece[:, BS * BS : BS * BS + count] = row.astype(jnp.bfloat16)


def pack(col, blocks, places):
    cols, height, _ = blocks.shape
    shape = jax.ShapeDtypeStruct((height, BS * BS + LANES), jnp.bfloat16)
    return pl.pallas_call(
        pack_kernel,
        out_shape=(shape,) * (cols - 1),
        in_specs=[SMEM, VMEM, VMEM],
        out_specs=(VMEM,) * (cols - 1),
        name="pack",
    )(col, blocks, places)


def unflatten(flat_ref, square_ref, groups):
    lower = lax.broadcasted_iota(jnp.int32, (groups, LANES), 1) < BS
    for h in range(BS * BS // LANES):
        even = flat_ref[:groups, h * LANES : (h + 1) * LANES]
        odd = flat_ref[groups:, h * LANES : (h + 1) * LANES]
        first = jnp.where(lower, even, pltpu.roll(odd, BS, 1))
        second = jnp.where(lower, pltpu.roll(even, BS, 1), odd)
        square_ref[pl.ds(2 * h, groups, stride=BS), :] = first
        square_ref[pl.ds(2 * h + 1, groups, stride=BS), :] = second


def mirror_kernel(key_ref, blocks_ref, onsite_ref, out_ref, flat_ref, square_ref):
    height = out_ref.shape[2]
    groups = square_ref.shape[0] // BS
    places = lax.broadcasted_iota(jnp.int32, (2 * groups, key_ref.shape[1]), 0)
    chosen = (places == key_ref[...]).astype(jnp.float32).astype(jnp.bfloat16)
    flat_ref[...] = jnp.dot(chosen, blocks_ref[...], preferred_element_type=jnp.float32)
    for p in range(PB):
        at = p * groups + p
        flat_ref[at : at + 1, :] += onsite_ref[p : p + 1, :].astype(jnp.float32)
    unflatten(flat_ref, square_ref, groups)
    devices = square_ref.shape[0] // height
    for d in range(devices):
        which, at = d // (devices // 2), d % (devices // 2) * LANES
        square = square_ref[d * height : (d + 1) * height, :]
        out_ref[which, at : at + LANES, :] = square.T.astype(jnp.bfloat16)


def mirror(key, blocks, onsite, rows, row_blocks):
    shape = (2, rows // 2 * PB * BS, row_blocks * BS)
    groups = rows * row_blocks
    return pl.pallas_call(
        mirror_kernel,
        out_shape=jax.ShapeDtypeStruct(shape, jnp.bfloat16),
        in_specs=[VMEM, VMEM, VMEM],
        out_specs=VMEM,
        scratch_shapes=[
            pltpu.VMEM((2 * groups, BS * BS), jnp.float32),
            pltpu.VMEM((groups * BS, LANES), jnp.float32),
        ],
        compiler_params=pltpu.CompilerParams(vmem_limit_bytes=40 * 1024 * 1024),
        cost_estimate=pl.CostEstimate(
            flops=4 * groups * blocks.size, bytes_accessed=3 * blocks.size, transcendentals=0
        ),
        name="mirror",
    )(key, blocks, onsite)


def direct_kernel(rows, slots, col_ref, blocks_ref, places_ref, *refs):
    cols = blocks_ref.shape[0]
    piece_refs, out_refs = refs[: cols - 1], refs[cols - 1 : -2]
    flat_ref, square_ref = refs[-2:]
    row_blocks = cols * PB
    groups = rows * row_blocks
    total = jnp.zeros((2 * groups, BS * BS), jnp.float32)
    height = blocks_ref.shape[1]
    for s in range(cols):
        if s == 0:
            place, blocks = places_of(places_ref, col_ref[0]), blocks_ref[col_ref[0]]
        else:
            piece = piece_refs[s - 1]
            place = piece[0:1, BS * BS : BS * BS + height].astype(jnp.float32)
            blocks = piece[:, : BS * BS]
        place = place.astype(jnp.int32)
        block = lax.broadcasted_iota(jnp.int32, (1, height), 1) // slots
        key = place % 2 * groups + place // 2 * row_blocks + s * PB + block
        key = jnp.where(place < 0, -1, key)
        ids = lax.broadcasted_iota(jnp.int32, (2 * groups, height), 0)
        chosen = (ids == key).astype(jnp.float32).astype(jnp.bfloat16)
        total += jnp.dot(chosen, blocks, preferred_element_type=jnp.float32)
    flat_ref[...] = total
    unflatten(flat_ref, square_ref, groups)
    for chip, out in enumerate(out_refs):
        for g in range(2 * cols):
            at = (chip * 2 * cols + g) * LANES
            lane = (g % cols * 2 + g // cols) * LANES
            out[:, lane : lane + LANES] = square_ref[at : at + LANES, :].astype(jnp.bfloat16)


def direct_rows(col, blocks, places, pieces, rows, slots):
    cols = blocks.shape[0]
    groups = rows * cols * PB
    shape = jax.ShapeDtypeStruct((PB * BS, 2 * cols * LANES), jnp.bfloat16)
    return pl.pallas_call(
        functools.partial(direct_kernel, rows, slots),
        out_shape=(shape,) * (rows // 2),
        in_specs=[SMEM] + [VMEM] * (cols + 1),
        out_specs=(VMEM,) * (rows // 2),
        scratch_shapes=[
            pltpu.VMEM((2 * groups, BS * BS), jnp.float32),
            pltpu.VMEM((groups * BS, LANES), jnp.float32),
        ],
        compiler_params=pltpu.CompilerParams(vmem_limit_bytes=48 * 1024 * 1024),
        name="direct_rows",
    )(col, blocks, places, *pieces)


def assemble_kernel(mirrored, mirrored_other, *refs):
    chips = (len(refs) - 1) // 2
    tile = refs[-1]
    size = PB * BS
    cols = mirrored.shape[2] // size
    for chip in range(chips):
        for j in range(2):
            sources = mirrored.at[j], mirrored_other.at[1 - j]
            direct = refs[j * chips + chip]
            rows = slice(chip * size, (chip + 1) * size)
            out_rows = slice((2 * chip + j) * size, (2 * chip + j + 1) * size)
            for s in range(cols):
                for i in range(2):
                    taken = (2 * s + (i ^ j)) * size
                    lane = (2 * s + i) * size
                    tile[out_rows, lane : lane + size] = (
                        sources[i][rows, s * size : (s + 1) * size]
                        + direct[:, taken : taken + size]
                    )


def assemble(mirrored, mirrored_other, direct, direct_other):
    _, height, width = mirrored.shape
    args = (mirrored, mirrored_other, *direct, *direct_other)
    return pl.pallas_call(
        assemble_kernel,
        out_shape=jax.ShapeDtypeStruct((2 * height, 2 * width), jnp.bfloat16),
        in_specs=[VMEM] * len(args),
        out_specs=VMEM,
        compiler_params=pltpu.CompilerParams(vmem_limit_bytes=40 * 1024 * 1024),
        name="assemble",
    )(*args)


def local(orbitals_in, hblocks, block_cols, live_counts, onsite, cut_low, top_bound):
    rows = lax.axis_size("row")
    cols = lax.axis_size("col")
    chips = rows // 2
    row = lax.axis_index("row")
    col = lax.axis_index("col")
    chip, core = row // 2, row % 2
    row_blocks, slots, _ = hblocks.shape
    k = orbitals_in.shape[1]
    local_rows = PB * BS
    total_rows = rows * cols * local_rows

    live = jnp.arange(slots, dtype=jnp.int32)[None, :] < live_counts
    device, block = block_cols // PB, block_cols % PB
    apart = (device % 2) ^ core
    distance = (device // 2) ^ chip
    places = jnp.where(live, (distance * 2 + apart) * PB + block, -1).astype(jnp.float32)
    places = places.reshape(cols, PB * slots)
    block_row = jnp.arange(row_blocks, dtype=jnp.int32)[:, None]
    near_row = (col - block_row // PB) % cols * PB + block_row % PB
    groups = rows * row_blocks
    key = block * groups + (apart * chips + distance) * row_blocks + near_row
    key = jnp.where(live, key, -1).reshape(1, row_blocks * slots)

    half = k // 2
    first_core = core == 0

    def halves(x):
        low, high = x[:, :half], x[:, half:]
        return jnp.where(first_core, low, high), jnp.where(first_core, high, low)

    def joined(own, other, axis):
        ordered = jnp.concatenate([own, other], axis), jnp.concatenate([other, own], axis)
        return jnp.where(first_core, *ordered)

    own, other = halves(orbitals_in)

    by_owner = hblocks.reshape(cols, PB * slots, BS * BS)
    pieces = pack(col[None], by_owner, places)
    key, pieces, other = lax.optimization_barrier((key, pieces, other))
    start = jnp.concatenate([own, core_swap(other, rows)], 0)
    pieces = [shifted(piece, "col", cols, s) for s, piece in enumerate(pieces, 1)]
    pieces, start = lax.optimization_barrier((pieces, start))

    def gather(v):
        return jnp.concatenate([v] + [shifted(v, "col", cols, s) for s in range(1, cols)], 0)

    def plane_gather(v):
        return jnp.concatenate([v] + [chip_swap(v, rows, s) for s in range(1, chips)], 0)

    def from_other_core(v):
        blocks = core_swap(v, rows).reshape(-1, 2, local_rows, half)
        return jnp.stack([blocks[:, 1], blocks[:, 0]], 1).reshape(v.shape)

    mirrored = mirror(
        key, hblocks.reshape(row_blocks * slots, BS * BS), onsite, rows, row_blocks
    )

    direct = direct_rows(col[None], by_owner, places, pieces, rows, slots)
    mirrored, direct = lax.optimization_barrier((mirrored, direct))
    mirrored_other = core_swap(mirrored, rows)
    direct = [chip_swap(direct[s], rows, s) if s else direct[s] for s in range(chips)]
    first, mirrored_other = lax.optimization_barrier(
        (start.astype(jnp.bfloat16), mirrored_other)
    )
    first_gathered, direct = lax.optimization_barrier((gather(first), direct))
    direct_other = [core_swap(rows_of_chip, rows) for rows_of_chip in direct]

    tile = assemble(mirrored, mirrored_other, direct, direct_other)

    def partial_product(gathered):
        return jnp.dot(tile, gathered, preferred_element_type=jnp.float32)

    def apply(gathered):
        terms = partial_product(gathered).reshape(chips, 2 * local_rows, half)
        total = terms[0]
        for s in range(1, chips):
            total = total + chip_swap(terms[s], rows, s)
        return total

    centre = 0.5 * (top_bound[0] + cut_low[0])
    halfwidth = 0.5 * (top_bound[0] - cut_low[0])
    previous = start
    current = (apply(first_gathered) - centre * start) / halfwidth
    for degree in range(DEG - 1):
        gathered = gather(current.astype(jnp.bfloat16))
        following = 2.0 * (apply(gathered) - centre * current) / halfwidth - previous
        previous, current = (current, following)

    rounded = current.astype(jnp.bfloat16)
    plane_rows = plane_gather(rounded)
    gathered, plane_rows = lax.optimization_barrier((gather(rounded), plane_rows))
    gathered_other = from_other_core(gathered)
    plane_other = from_other_core(plane_rows)
    filtered = joined(current[:local_rows], core_swap(current[local_rows:], rows), 1)
    contract = (((0,), (0,)), ((), ()))

    def gram_rows(g):
        return lax.dot_general(g, gathered, contract, preferred_element_type=jnp.float32)

    image = partial_product(gathered)

    def cross_rows(g):
        return lax.dot_general(g.astype(jnp.float32), image, contract, precision=HI)

    gram_part = jnp.concatenate([gram_rows(gathered), gram_rows(gathered_other)], 0)
    cross_part = jnp.concatenate([cross_rows(plane_rows), cross_rows(plane_other)], 0)
    share = k // chips
    parts = [x.reshape(chips, share, half) for x in (gram_part, cross_part)]
    parts = by_distance(jnp.stack(parts, 1), chip)
    total = sum([chip_swap(parts[s], rows, s) for s in range(1, chips)], parts[0])

    def chip_shares(x):
        return [x] + [chip_swap(x, rows, s) for s in range(1, chips)]

    def whole(shares):
        x = by_distance(jnp.stack(shares), chip).reshape(k, half)
        x = joined(x[:half], x[half:], 0)
        return joined(x, core_swap(x, rows), 1)

    cross_share = sum([shifted(total[1], "col", cols, s) for s in range(1, cols)], total[1])
    orbitals, inverse = factorize(whole(chip_shares(total[0])), filtered, total_rows)
    inverse, shares = lax.optimization_barrier((inverse, chip_shares(cross_share)))
    return orbitals, project(inverse, whole(shares), total_rows)


def solution(mesh):
    placed = (
        P(("row", "col"), None),
        P("row", "col", None),
        P("row", "col"),
        P("row", "col"),
        P(("row", "col"), None),
        P(),
        P(),
    )
    return jax.shard_map(
        local, mesh=mesh, in_specs=placed, out_specs=(P(("row", "col"), None), P()), check_vma=False
    )
```

```python
import functools

import jax
import jax.numpy as jnp
from jax import lax
from jax.experimental import pallas as pl
from jax.experimental.pallas import tpu as pltpu
from jax.sharding import PartitionSpec as P

BS = 64
PB = 2
DEG = 3
LANES = 128
PANEL = 32
HI = lax.Precision.HIGHEST
VMEM = pl.BlockSpec(memory_space=pltpu.VMEM)
SMEM = pl.BlockSpec(memory_space=pltpu.SMEM)


def widen(x, width):
    return jnp.concatenate([x] * (width // LANES), 1) if width > LANES else x

def reciprocal(x):
    return pl.reciprocal(x, approx=True)


def factor_kernel(total_rows, gram_ref, y_ref, orbitals_ref, inverse_ref):
    k = gram_ref.shape[0]
    panels = k // PANEL
    row_id = lax.broadcasted_iota(jnp.int32, (PANEL, LANES), 0)
    scale = 1.0 / total_rows
    upper = [gram_ref[m * PANEL:(m + 1) * PANEL, :] * scale for m in range(panels)]
    inverse = []
    for m in range(panels):
        r = lax.broadcasted_iota(jnp.int32, (PANEL, k), 0) + m * PANEL
        inverse.append((r == lax.broadcasted_iota(jnp.int32, (PANEL, k), 1)).astype(jnp.float32))
    for p in range(panels):
        start = p * PANEL
        s_lo = start // LANES * LANES
        w_hi = (start + PANEL + LANES - 1) // LANES * LANES
        s, w = upper[p][:, s_lo:], inverse[p][:, :w_hi]
        columns = [
            jnp.broadcast_to(s[:, start - s_lo + t:start - s_lo + t + 1], (PANEL, LANES))
            for t in range(PANEL)
        ]
        s_done, w_done = [], []
        for base in range(0, PANEL, 8):
            ids = row_id[: PANEL - base]
            pivots = jnp.zeros((8, LANES), jnp.float32)
            for t in range(base, base + 8, 2):
                at = t - base
                one, two = columns[t], columns[t + 1]
                a, b, d = one[at:at + 1, :], one[at + 1:at + 2, :], two[at + 1:at + 2, :]
                det = a * d - b * b
                det_inv = reciprocal(det)
                a_inv = reciprocal(a)
                pivots = jnp.where(ids[:8] == at, a, pivots)
                pivots = jnp.where(ids[:8] == at + 1, det * a_inv, pivots)
                below = ids > at + 1
                one_below = jnp.where(below, one, 0.0)
                two_below = jnp.where(below, two, 0.0)
                first = (d * one - b * two) * det_inv
                second = (a * two - b * one) * det_inv
                for j in range(t + 2, PANEL):
                    r = j - base
                    if j < t + 4:
                        p1, p2 = one[r:r + 1, :], two[r:r + 1, :]
                        m1, m2 = (d * p1 - b * p2) * det_inv, (a * p2 - b * p1) * det_inv
                    else:
                        m1, m2 = first[r:r + 1, :], second[r:r + 1, :]
                    columns[j] = columns[j] - (one_below * m1 + two_below * m2)
                first = jnp.where(below, first, jnp.where(ids == at + 1, b * a_inv, 0.0))
                second = jnp.where(below, second, 0.0)
                s = s - (
                    widen(first, s.shape[1]) * s[at:at + 1, :]
                    + widen(second, s.shape[1]) * s[at + 1:at + 2, :]
                )
                w = w - (
                    widen(first, w.shape[1]) * w[at:at + 1, :]
                    + widen(second, w.shape[1]) * w[at + 1:at + 2, :]
                )
            root = lax.rsqrt(pivots)
            s_done.append(s[:8] * widen(root, s.shape[1]))
            w_done.append(w[:8] * widen(root, w.shape[1]))
            s, w = s[8:], w[8:]
            columns = [c[8:] for c in columns]
        s = jnp.concatenate(s_done, 0)
        w = jnp.concatenate(w_done, 0)
        inverse_ref[start:start + PANEL, :w_hi] = w
        if w_hi < k:
            inverse_ref[start:start + PANEL, w_hi:] = jnp.zeros((PANEL, k - w_hi), jnp.float32)
        if p == panels - 1:
            break
        st = s.T
        for lo, hi in ((p + 1, p + 2), (p + 2, panels)):
            if lo >= hi:
                continue
            left = st[lo * PANEL - s_lo:hi * PANEL - s_lo, :]
            s_lo2 = lo * PANEL // LANES * LANES
            ds = jnp.dot(left, s[:, s_lo2 - s_lo:], precision=HI, preferred_element_type=jnp.float32)
            dw = jnp.dot(left, w, precision=HI, preferred_element_type=jnp.float32)
            for m in range(lo, hi):
                o = (m - lo) * PANEL
                a = upper[m][:, s_lo2:] - ds[o:o + PANEL, :]
                upper[m] = a if s_lo2 == 0 else jnp.concatenate([upper[m][:, :s_lo2], a], 1)
                b = inverse[m][:, :w_hi] - dw[o:o + PANEL, :]
                inverse[m] = b if w_hi == k else jnp.concatenate([b, inverse[m][:, w_hi:]], 1)
    inv = inverse_ref[...]
    nt = (((1,), (1,)), ((), ()))
    orbitals_ref[...] = lax.dot_general(y_ref[...], inv, nt, precision=HI, preferred_element_type=jnp.float32)


def project_kernel(total_rows, inverse_ref, cross_ref, projected_ref):
    inv = inverse_ref[...]
    nt = (((1,), (1,)), ((), ()))
    half = jnp.dot(inv, cross_ref[...], precision=HI, preferred_element_type=jnp.float32)
    full = lax.dot_general(half, inv, nt, precision=HI, preferred_element_type=jnp.float32)
    projected_ref[...] = (full + full.T) * (0.5 / total_rows)


def factorize(gram, y, total_rows):
    k = gram.shape[0]
    f32 = jnp.float32
    return pl.pallas_call(
        functools.partial(factor_kernel, total_rows),
        out_shape=(jax.ShapeDtypeStruct(y.shape, f32), jax.ShapeDtypeStruct((k, k), f32)),
        in_specs=[VMEM] * 2,
        out_specs=(VMEM,) * 2,
        compiler_params=pltpu.CompilerParams(vmem_limit_bytes=32 * 1024 * 1024),
        cost_estimate=pl.CostEstimate(
            flops=0, bytes_accessed=80 * gram.size, transcendentals=0
        ),
        name="factorize",
    )(gram, y)


def project(inverse, cross, total_rows):
    return pl.pallas_call(
        functools.partial(project_kernel, total_rows),
        out_shape=jax.ShapeDtypeStruct(cross.shape, jnp.float32),
        in_specs=[VMEM] * 2,
        out_specs=VMEM,
        compiler_params=pltpu.CompilerParams(vmem_limit_bytes=32 * 1024 * 1024),
        name="project",
    )(inverse, cross)


def exchanged(x, axis, size, apart):
    return lax.ppermute(x, axis, [(i, i ^ apart) for i in range(size)])


def shifted(x, axis, size, step):
    return lax.ppermute(x, axis, [(i, (i + step) % size) for i in range(size)])


def core_swap(x, rows):
    return exchanged(x, "row", rows, 1)


def chip_swap(x, rows, apart):
    return exchanged(x, "row", rows, 2 * apart)


def by_distance(x, index):
    size = x.shape[0]
    bit = 1
    while bit < size:
        pairs = x.reshape(size // (2 * bit), 2, bit, *x.shape[1:])
        flipped = jnp.stack([pairs[:, 1], pairs[:, 0]], 1).reshape(x.shape)
        x = jnp.where((index // bit) % 2 == 1, flipped, x)
        bit *= 2
    return x


def places_of(places_ref, owner):
    ids = lax.broadcasted_iota(jnp.int32, places_ref.shape, 0)
    return jnp.sum(jnp.where(ids == owner, places_ref[...], 0.0), 0, keepdims=True)


def pack_kernel(col_ref, blocks_ref, places_ref, *piece_refs):
    cols = len(piece_refs) + 1
    for s, piece in enumerate(piece_refs, 1):
        owner = lax.rem(col_ref[0] + s, cols)
        piece[:, : BS * BS] = blocks_ref[owner]
        count = places_ref.shape[1]
        row = jnp.broadcast_to(places_of(places_ref, owner), (piece.shape[0], count))
        piece[:, BS * BS : BS * BS + count] = row.astype(jnp.bfloat16)


def pack(col, blocks, places):
    cols, height, _ = blocks.shape
    shape = jax.ShapeDtypeStruct((height, BS * BS + LANES), jnp.bfloat16)
    return pl.pallas_call(
        pack_kernel,
        out_shape=(shape,) * (cols - 1),
        in_specs=[SMEM, VMEM, VMEM],
        out_specs=(VMEM,) * (cols - 1),
        name="pack",
    )(col, blocks, places)


def unflatten(flat_ref, square_ref, groups):
    lower = lax.broadcasted_iota(jnp.int32, (groups, LANES), 1) < BS
    for h in range(BS * BS // LANES):
        even = flat_ref[:groups, h * LANES : (h + 1) * LANES]
        odd = flat_ref[groups:, h * LANES : (h + 1) * LANES]
        first = jnp.where(lower, even, pltpu.roll(odd, BS, 1))
        second = jnp.where(lower, pltpu.roll(even, BS, 1), odd)
        square_ref[pl.ds(2 * h, groups, stride=BS), :] = first
        square_ref[pl.ds(2 * h + 1, groups, stride=BS), :] = second


def mirror_kernel(key_ref, blocks_ref, onsite_ref, out_ref, flat_ref, square_ref):
    height = out_ref.shape[2]
    groups = square_ref.shape[0] // BS
    places = lax.broadcasted_iota(jnp.int32, (2 * groups, key_ref.shape[1]), 0)
    chosen = (places == key_ref[...]).astype(jnp.float32).astype(jnp.bfloat16)
    flat_ref[...] = jnp.dot(chosen, blocks_ref[...], preferred_element_type=jnp.float32)
    for p in range(PB):
        at = p * groups + p
        flat_ref[at : at + 1, :] += onsite_ref[p : p + 1, :].astype(jnp.float32)
    unflatten(flat_ref, square_ref, groups)
    devices = square_ref.shape[0] // height
    for d in range(devices):
        which, at = d // (devices // 2), d % (devices // 2) * LANES
        square = square_ref[d * height : (d + 1) * height, :]
        out_ref[which, at : at + LANES, :] = square.T.astype(jnp.bfloat16)


def mirror(key, blocks, onsite, rows, row_blocks):
    shape = (2, rows // 2 * PB * BS, row_blocks * BS)
    groups = rows * row_blocks
    return pl.pallas_call(
        mirror_kernel,
        out_shape=jax.ShapeDtypeStruct(shape, jnp.bfloat16),
        in_specs=[VMEM, VMEM, VMEM],
        out_specs=VMEM,
        scratch_shapes=[
            pltpu.VMEM((2 * groups, BS * BS), jnp.float32),
            pltpu.VMEM((groups * BS, LANES), jnp.float32),
        ],
        compiler_params=pltpu.CompilerParams(vmem_limit_bytes=40 * 1024 * 1024),
        cost_estimate=pl.CostEstimate(
            flops=4 * groups * blocks.size, bytes_accessed=3 * blocks.size, transcendentals=0
        ),
        name="mirror",
    )(key, blocks, onsite)


def direct_kernel(rows, slots, col_ref, blocks_ref, places_ref, *refs):
    cols = blocks_ref.shape[0]
    piece_refs, out_refs = refs[: cols - 1], refs[cols - 1 : -2]
    flat_ref, square_ref = refs[-2:]
    row_blocks = cols * PB
    groups = rows * row_blocks
    total = jnp.zeros((2 * groups, BS * BS), jnp.float32)
    height = blocks_ref.shape[1]
    for s in range(cols):
        if s == 0:
            place, blocks = places_of(places_ref, col_ref[0]), blocks_ref[col_ref[0]]
        else:
            piece = piece_refs[s - 1]
            place = piece[0:1, BS * BS : BS * BS + height].astype(jnp.float32)
            blocks = piece[:, : BS * BS]
        place = place.astype(jnp.int32)
        block = lax.broadcasted_iota(jnp.int32, (1, height), 1) // slots
        key = place % 2 * groups + place // 2 * row_blocks + s * PB + block
        key = jnp.where(place < 0, -1, key)
        ids = lax.broadcasted_iota(jnp.int32, (2 * groups, height), 0)
        chosen = (ids == key).astype(jnp.float32).astype(jnp.bfloat16)
        total += jnp.dot(chosen, blocks, preferred_element_type=jnp.float32)
    flat_ref[...] = total
    unflatten(flat_ref, square_ref, groups)
    for chip, out in enumerate(out_refs):
        for g in range(2 * cols):
            at = (chip * 2 * cols + g) * LANES
            lane = (g % cols * 2 + g // cols) * LANES
            out[:, lane : lane + LANES] = square_ref[at : at + LANES, :].astype(jnp.bfloat16)


def direct_rows(col, blocks, places, pieces, rows, slots):
    cols = blocks.shape[0]
    groups = rows * cols * PB
    shape = jax.ShapeDtypeStruct((PB * BS, 2 * cols * LANES), jnp.bfloat16)
    return pl.pallas_call(
        functools.partial(direct_kernel, rows, slots),
        out_shape=(shape,) * (rows // 2),
        in_specs=[SMEM] + [VMEM] * (cols + 1),
        out_specs=(VMEM,) * (rows // 2),
        scratch_shapes=[
            pltpu.VMEM((2 * groups, BS * BS), jnp.float32),
            pltpu.VMEM((groups * BS, LANES), jnp.float32),
        ],
        compiler_params=pltpu.CompilerParams(vmem_limit_bytes=48 * 1024 * 1024),
        name="direct_rows",
    )(col, blocks, places, *pieces)


def assemble_kernel(mirrored, mirrored_other, *refs):
    chips = (len(refs) - 1) // 2
    tile = refs[-1]
    size = PB * BS
    cols = mirrored.shape[2] // size
    for chip in range(chips):
        for j in range(2):
            sources = mirrored.at[j], mirrored_other.at[1 - j]
            direct = refs[j * chips + chip]
            rows = slice(chip * size, (chip + 1) * size)
            out_rows = slice((2 * chip + j) * size, (2 * chip + j + 1) * size)
            for s in range(cols):
                for i in range(2):
                    taken = (2 * s + (i ^ j)) * size
                    lane = (2 * s + i) * size
                    tile[out_rows, lane : lane + size] = (
                        sources[i][rows, s * size : (s + 1) * size]
                        + direct[:, taken : taken + size]
                    )


def assemble(mirrored, mirrored_other, direct, direct_other):
    _, height, width = mirrored.shape
    args = (mirrored, mirrored_other, *direct, *direct_other)
    return pl.pallas_call(
        assemble_kernel,
        out_shape=jax.ShapeDtypeStruct((2 * height, 2 * width), jnp.bfloat16),
        in_specs=[VMEM] * len(args),
        out_specs=VMEM,
        compiler_params=pltpu.CompilerParams(vmem_limit_bytes=40 * 1024 * 1024),
        name="assemble",
    )(*args)


def local(orbitals_in, hblocks, block_cols, live_counts, onsite, cut_low, top_bound):
    rows = lax.axis_size("row")
    cols = lax.axis_size("col")
    chips = rows // 2
    row = lax.axis_index("row")
    col = lax.axis_index("col")
    chip, core = row // 2, row % 2
    row_blocks, slots, _ = hblocks.shape
    k = orbitals_in.shape[1]
    local_rows = PB * BS
    total_rows = rows * cols * local_rows

    live = jnp.arange(slots, dtype=jnp.int32)[None, :] < live_counts
    device, block = block_cols // PB, block_cols % PB
    apart = (device % 2) ^ core
    distance = (device // 2) ^ chip
    places = jnp.where(live, (distance * 2 + apart) * PB + block, -1).astype(jnp.float32)
    places = places.reshape(cols, PB * slots)
    block_row = jnp.arange(row_blocks, dtype=jnp.int32)[:, None]
    near_row = (col - block_row // PB) % cols * PB + block_row % PB
    groups = rows * row_blocks
    key = block * groups + (apart * chips + distance) * row_blocks + near_row
    key = jnp.where(live, key, -1).reshape(1, row_blocks * slots)

    half = k // 2
    first_core = core == 0

    def halves(x):
        low, high = x[:, :half], x[:, half:]
        return jnp.where(first_core, low, high), jnp.where(first_core, high, low)

    def joined(own, other, axis):
        ordered = jnp.concatenate([own, other], axis), jnp.concatenate([other, own], axis)
        return jnp.where(first_core, *ordered)

    by_owner = hblocks.reshape(cols, PB * slots, BS * BS)
    pieces = pack(col[None], by_owner, places)
    key, pieces, orbitals_in = lax.optimization_barrier((key, pieces, orbitals_in))
    own, other = halves(orbitals_in)
    start = jnp.concatenate([own, core_swap(other, rows)], 0)
    pieces = [shifted(piece, "col", cols, s) for s, piece in enumerate(pieces, 1)]
    mirrored = mirror(
        key, hblocks.reshape(row_blocks * slots, BS * BS), onsite, rows, row_blocks
    )

    pieces, start, mirrored = lax.optimization_barrier((pieces, start, mirrored))

    def gather(v):
        return jnp.concatenate([v] + [shifted(v, "col", cols, s) for s in range(1, cols)], 0)

    def plane_gather(v):
        return jnp.concatenate([v] + [chip_swap(v, rows, s) for s in range(1, chips)], 0)

    def from_other_core(v):
        blocks = core_swap(v, rows).reshape(-1, 2, local_rows, half)
        return jnp.stack([blocks[:, 1], blocks[:, 0]], 1).reshape(v.shape)

    direct = direct_rows(col[None], by_owner, places, pieces, rows, slots)
    first = start.astype(jnp.bfloat16)
    second = shifted(first, "col", cols, 1)
    mirrored, direct, second = lax.optimization_barrier((mirrored, direct, second))
    mirrored_other = core_swap(mirrored, rows)
    direct = [chip_swap(direct[s], rows, s) if s else direct[s] for s in range(chips)]
    first, mirrored_other = lax.optimization_barrier((first, mirrored_other))
    first_gathered = jnp.concatenate(
        [first, second] + [shifted(first, "col", cols, s) for s in range(2, cols)], 0
    )
    first_gathered, direct = lax.optimization_barrier((first_gathered, direct))
    direct_other = [core_swap(rows_of_chip, rows) for rows_of_chip in direct]

    tile = assemble(mirrored, mirrored_other, direct, direct_other)

    def partial_product(gathered):
        return jnp.dot(tile, gathered, preferred_element_type=jnp.float32)

    def apply(gathered):
        terms = partial_product(gathered).reshape(chips, 2 * local_rows, half)
        total = terms[0]
        for s in range(1, chips):
            total = total + chip_swap(terms[s], rows, s)
        return total

    centre = 0.5 * (top_bound[0] + cut_low[0])
    halfwidth = 0.5 * (top_bound[0] - cut_low[0])
    previous = start
    current = (apply(first_gathered) - centre * start) / halfwidth
    for degree in range(DEG - 1):
        gathered = gather(current.astype(jnp.bfloat16))
        following = 2.0 * (apply(gathered) - centre * current) / halfwidth - previous
        previous, current = (current, following)

    rounded = current.astype(jnp.bfloat16)
    plane_rows = plane_gather(rounded)
    gathered, plane_rows = lax.optimization_barrier((gather(rounded), plane_rows))
    gathered_other = from_other_core(gathered)
    plane_other = from_other_core(plane_rows)
    filtered = joined(current[:local_rows], core_swap(current[local_rows:], rows), 1)
    contract = (((0,), (0,)), ((), ()))

    def gram_rows(g):
        return lax.dot_general(g, gathered, contract, preferred_element_type=jnp.float32)

    image = partial_product(gathered)

    def cross_rows(g):
        return lax.dot_general(g.astype(jnp.float32), image, contract, precision=HI)

    gram_part = jnp.concatenate([gram_rows(gathered), gram_rows(gathered_other)], 0)
    cross_part = jnp.concatenate([cross_rows(plane_rows), cross_rows(plane_other)], 0)
    share = k // chips
    parts = [x.reshape(chips, share, half) for x in (gram_part, cross_part)]
    parts = by_distance(jnp.stack(parts, 1), chip)
    total = sum([chip_swap(parts[s], rows, s) for s in range(1, chips)], parts[0])

    def chip_shares(x):
        return [x] + [chip_swap(x, rows, s) for s in range(1, chips)]

    def whole(shares):
        x = by_distance(jnp.stack(shares), chip).reshape(k, half)
        x = joined(x[:half], x[half:], 0)
        return joined(x, core_swap(x, rows), 1)

    cross_share = sum([shifted(total[1], "col", cols, s) for s in range(1, cols)], total[1])
    orbitals, inverse = factorize(whole(chip_shares(total[0])), filtered, total_rows)
    inverse, shares = lax.optimization_barrier((inverse, chip_shares(cross_share)))
    return orbitals, project(inverse, whole(shares), total_rows)


def solution(mesh):
    placed = (
        P(("row", "col"), None),
        P("row", "col", None),
        P("row", "col"),
        P("row", "col"),
        P(("row", "col"), None),
        P(),
        P(),
    )
    return jax.shard_map(
        local, mesh=mesh, in_specs=placed, out_specs=(P(("row", "col"), None), P()), check_vma=False
    )
```

```python
import functools

import jax
import jax.numpy as jnp
from jax import lax
from jax.experimental import pallas as pl
from jax.experimental.pallas import tpu as pltpu
from jax.sharding import PartitionSpec as P

BS = 64
PB = 2
DEG = 3
LANES = 128
PANEL = 32
HI = lax.Precision.HIGHEST
VMEM = pl.BlockSpec(memory_space=pltpu.VMEM)
SMEM = pl.BlockSpec(memory_space=pltpu.SMEM)


def widen(x, width):
    return jnp.concatenate([x] * (width // LANES), 1) if width > LANES else x

def reciprocal(x):
    return pl.reciprocal(x, approx=True)


def factor_kernel(total_rows, gram_ref, y_ref, orbitals_ref, inverse_ref):
    k = gram_ref.shape[0]
    panels = k // PANEL
    row_id = lax.broadcasted_iota(jnp.int32, (PANEL, LANES), 0)
    scale = 1.0 / total_rows
    upper = [gram_ref[m * PANEL:(m + 1) * PANEL, :] * scale for m in range(panels)]
    inverse = []
    for m in range(panels):
        r = lax.broadcasted_iota(jnp.int32, (PANEL, k), 0) + m * PANEL
        inverse.append((r == lax.broadcasted_iota(jnp.int32, (PANEL, k), 1)).astype(jnp.float32))
    for p in range(panels):
        start = p * PANEL
        s_lo = start // LANES * LANES
        w_hi = (start + PANEL + LANES - 1) // LANES * LANES
        s, w = upper[p][:, s_lo:], inverse[p][:, :w_hi]
        columns = [
            jnp.broadcast_to(s[:, start - s_lo + t:start - s_lo + t + 1], (PANEL, LANES))
            for t in range(PANEL)
        ]
        s_done, w_done = [], []
        for base in range(0, PANEL, 8):
            ids = row_id[: PANEL - base]
            pivots = jnp.zeros((8, LANES), jnp.float32)
            for t in range(base, base + 8, 2):
                at = t - base
                one, two = columns[t], columns[t + 1]
                a, b, d = one[at:at + 1, :], one[at + 1:at + 2, :], two[at + 1:at + 2, :]
                det = a * d - b * b
                det_inv = reciprocal(det)
                a_inv = reciprocal(a)
                pivots = jnp.where(ids[:8] == at, a, pivots)
                pivots = jnp.where(ids[:8] == at + 1, det * a_inv, pivots)
                below = ids > at + 1
                one_below = jnp.where(below, one, 0.0)
                two_below = jnp.where(below, two, 0.0)
                first = (d * one - b * two) * det_inv
                second = (a * two - b * one) * det_inv
                for j in range(t + 2, PANEL):
                    r = j - base
                    if j < t + 4:
                        p1, p2 = one[r:r + 1, :], two[r:r + 1, :]
                        m1, m2 = (d * p1 - b * p2) * det_inv, (a * p2 - b * p1) * det_inv
                    else:
                        m1, m2 = first[r:r + 1, :], second[r:r + 1, :]
                    columns[j] = columns[j] - (one_below * m1 + two_below * m2)
                first = jnp.where(below, first, jnp.where(ids == at + 1, b * a_inv, 0.0))
                second = jnp.where(below, second, 0.0)
                s = s - (
                    widen(first, s.shape[1]) * s[at:at + 1, :]
                    + widen(second, s.shape[1]) * s[at + 1:at + 2, :]
                )
                w = w - (
                    widen(first, w.shape[1]) * w[at:at + 1, :]
                    + widen(second, w.shape[1]) * w[at + 1:at + 2, :]
                )
            root = lax.rsqrt(pivots)
            s_done.append(s[:8] * widen(root, s.shape[1]))
            w_done.append(w[:8] * widen(root, w.shape[1]))
            s, w = s[8:], w[8:]
            columns = [c[8:] for c in columns]
        s = jnp.concatenate(s_done, 0)
        w = jnp.concatenate(w_done, 0)
        inverse_ref[start:start + PANEL, :w_hi] = w
        if w_hi < k:
            inverse_ref[start:start + PANEL, w_hi:] = jnp.zeros((PANEL, k - w_hi), jnp.float32)
        if p == panels - 1:
            break
        st = s.T
        for lo, hi in ((p + 1, p + 2), (p + 2, panels)):
            if lo >= hi:
                continue
            left = st[lo * PANEL - s_lo:hi * PANEL - s_lo, :]
            s_lo2 = lo * PANEL // LANES * LANES
            ds = jnp.dot(left, s[:, s_lo2 - s_lo:], precision=HI, preferred_element_type=jnp.float32)
            dw = jnp.dot(left, w, precision=HI, preferred_element_type=jnp.float32)
            for m in range(lo, hi):
                o = (m - lo) * PANEL
                a = upper[m][:, s_lo2:] - ds[o:o + PANEL, :]
                upper[m] = a if s_lo2 == 0 else jnp.concatenate([upper[m][:, :s_lo2], a], 1)
                b = inverse[m][:, :w_hi] - dw[o:o + PANEL, :]
                inverse[m] = b if w_hi == k else jnp.concatenate([b, inverse[m][:, w_hi:]], 1)
    inv = inverse_ref[...]
    nt = (((1,), (1,)), ((), ()))
    orbitals_ref[...] = lax.dot_general(y_ref[...], inv, nt, precision=HI, preferred_element_type=jnp.float32)


def project_kernel(total_rows, inverse_ref, cross_ref, projected_ref):
    inv = inverse_ref[...]
    nt = (((1,), (1,)), ((), ()))
    half = jnp.dot(inv, cross_ref[...], precision=HI, preferred_element_type=jnp.float32)
    full = lax.dot_general(half, inv, nt, precision=HI, preferred_element_type=jnp.float32)
    projected_ref[...] = (full + full.T) * (0.5 / total_rows)


def factorize(gram, y, total_rows):
    k = gram.shape[0]
    f32 = jnp.float32
    return pl.pallas_call(
        functools.partial(factor_kernel, total_rows),
        out_shape=(jax.ShapeDtypeStruct(y.shape, f32), jax.ShapeDtypeStruct((k, k), f32)),
        in_specs=[VMEM] * 2,
        out_specs=(VMEM,) * 2,
        compiler_params=pltpu.CompilerParams(vmem_limit_bytes=32 * 1024 * 1024),
        cost_estimate=pl.CostEstimate(
            flops=0, bytes_accessed=80 * gram.size, transcendentals=0
        ),
        name="factorize",
    )(gram, y)


def project(inverse, cross, total_rows):
    return pl.pallas_call(
        functools.partial(project_kernel, total_rows),
        out_shape=jax.ShapeDtypeStruct(cross.shape, jnp.float32),
        in_specs=[VMEM] * 2,
        out_specs=VMEM,
        compiler_params=pltpu.CompilerParams(vmem_limit_bytes=32 * 1024 * 1024),
        name="project",
    )(inverse, cross)


def exchanged(x, axis, size, apart):
    return lax.ppermute(x, axis, [(i, i ^ apart) for i in range(size)])


def shifted(x, axis, size, step):
    return lax.ppermute(x, axis, [(i, (i + step) % size) for i in range(size)])


def core_swap(x, rows):
    return exchanged(x, "row", rows, 1)


def chip_swap(x, rows, apart):
    return exchanged(x, "row", rows, 2 * apart)


def by_distance(x, index):
    size = x.shape[0]
    bit = 1
    while bit < size:
        pairs = x.reshape(size // (2 * bit), 2, bit, *x.shape[1:])
        flipped = jnp.stack([pairs[:, 1], pairs[:, 0]], 1).reshape(x.shape)
        x = jnp.where((index // bit) % 2 == 1, flipped, x)
        bit *= 2
    return x


def places_of(places_ref, owner):
    height, slots = places_ref.shape
    width = PB * slots
    slot = lax.broadcasted_iota(jnp.int32, (slots, width), 0)
    lane = lax.broadcasted_iota(jnp.int32, (slots, width), 1)
    repeat = (lane % slots == slot).astype(jnp.float32)
    copies = jnp.dot(places_ref[...], repeat, precision=HI, preferred_element_type=jnp.float32)
    row = lax.broadcasted_iota(jnp.int32, (height, width), 0)
    block = lax.broadcasted_iota(jnp.int32, (height, width), 1) // slots
    taken = row == owner * PB + block
    return jnp.sum(jnp.where(taken, copies, 0.0), 0, keepdims=True)


def pack_kernel(col_ref, blocks_ref, places_ref, *piece_refs):
    cols = len(piece_refs) + 1
    for s, piece in enumerate(piece_refs, 1):
        owner = lax.rem(col_ref[0] + s, cols)
        piece[:, : BS * BS] = blocks_ref[owner]
        count = piece.shape[0]
        row = jnp.broadcast_to(places_of(places_ref, owner), (piece.shape[0], count))
        piece[:, BS * BS : BS * BS + count] = row.astype(jnp.bfloat16)


def pack(col, blocks, places):
    cols, height, _ = blocks.shape
    shape = jax.ShapeDtypeStruct((height, BS * BS + LANES), jnp.bfloat16)
    return pl.pallas_call(
        pack_kernel,
        out_shape=(shape,) * (cols - 1),
        in_specs=[SMEM, VMEM, VMEM],
        out_specs=(VMEM,) * (cols - 1),
        name="pack",
    )(col, blocks, places)


def unflatten(flat_ref, square_ref, groups):
    lower = lax.broadcasted_iota(jnp.int32, (groups, LANES), 1) < BS
    for h in range(BS * BS // LANES):
        even = flat_ref[:groups, h * LANES : (h + 1) * LANES]
        odd = flat_ref[groups:, h * LANES : (h + 1) * LANES]
        first = jnp.where(lower, even, pltpu.roll(odd, BS, 1))
        second = jnp.where(lower, pltpu.roll(even, BS, 1), odd)
        square_ref[pl.ds(2 * h, groups, stride=BS), :] = first
        square_ref[pl.ds(2 * h + 1, groups, stride=BS), :] = second


def mirror_kernel(key_ref, blocks_ref, onsite_ref, out_ref, flat_ref, square_ref):
    height = out_ref.shape[2]
    groups = square_ref.shape[0] // BS
    places = lax.broadcasted_iota(jnp.int32, (2 * groups, key_ref.shape[1]), 0)
    chosen = (places == key_ref[...]).astype(jnp.float32).astype(jnp.bfloat16)
    flat_ref[...] = jnp.dot(chosen, blocks_ref[...], preferred_element_type=jnp.float32)
    for p in range(PB):
        at = p * groups + p
        flat_ref[at : at + 1, :] += onsite_ref[p : p + 1, :].astype(jnp.float32)
    unflatten(flat_ref, square_ref, groups)
    devices = square_ref.shape[0] // height
    for d in range(devices):
        which, at = d // (devices // 2), d % (devices // 2) * LANES
        square = square_ref[d * height : (d + 1) * height, :]
        out_ref[which, at : at + LANES, :] = square.T.astype(jnp.bfloat16)


def mirror(key, blocks, onsite, rows, row_blocks):
    shape = (2, rows // 2 * PB * BS, row_blocks * BS)
    groups = rows * row_blocks
    return pl.pallas_call(
        mirror_kernel,
        out_shape=jax.ShapeDtypeStruct(shape, jnp.bfloat16),
        in_specs=[VMEM, VMEM, VMEM],
        out_specs=VMEM,
        scratch_shapes=[
            pltpu.VMEM((2 * groups, BS * BS), jnp.float32),
            pltpu.VMEM((groups * BS, LANES), jnp.float32),
        ],
        compiler_params=pltpu.CompilerParams(vmem_limit_bytes=40 * 1024 * 1024),
        cost_estimate=pl.CostEstimate(
            flops=4 * groups * blocks.size, bytes_accessed=3 * blocks.size, transcendentals=0
        ),
        name="mirror",
    )(key, blocks, onsite)


def direct_kernel(rows, slots, col_ref, blocks_ref, places_ref, *refs):
    cols = blocks_ref.shape[0]
    piece_refs, out_refs = refs[: cols - 1], refs[cols - 1 : -2]
    flat_ref, square_ref = refs[-2:]
    row_blocks = cols * PB
    groups = rows * row_blocks
    total = jnp.zeros((2 * groups, BS * BS), jnp.float32)
    height = blocks_ref.shape[1]
    for s in range(cols):
        if s == 0:
            place, blocks = places_of(places_ref, col_ref[0]), blocks_ref[col_ref[0]]
        else:
            piece = piece_refs[s - 1]
            place = piece[0:1, BS * BS : BS * BS + height].astype(jnp.float32)
            blocks = piece[:, : BS * BS]
        place = place.astype(jnp.int32)
        block = lax.broadcasted_iota(jnp.int32, (1, height), 1) // slots
        key = place % 2 * groups + place // 2 * row_blocks + s * PB + block
        key = jnp.where(place < 0, -1, key)
        ids = lax.broadcasted_iota(jnp.int32, (2 * groups, height), 0)
        chosen = (ids == key).astype(jnp.float32).astype(jnp.bfloat16)
        total += jnp.dot(chosen, blocks, preferred_element_type=jnp.float32)
    flat_ref[...] = total
    unflatten(flat_ref, square_ref, groups)
    for chip, out in enumerate(out_refs):
        for g in range(2 * cols):
            at = (chip * 2 * cols + g) * LANES
            lane = (g % cols * 2 + g // cols) * LANES
            out[:, lane : lane + LANES] = square_ref[at : at + LANES, :].astype(jnp.bfloat16)


def direct_rows(col, blocks, places, pieces, rows, slots):
    cols = blocks.shape[0]
    groups = rows * cols * PB
    shape = jax.ShapeDtypeStruct((PB * BS, 2 * cols * LANES), jnp.bfloat16)
    return pl.pallas_call(
        functools.partial(direct_kernel, rows, slots),
        out_shape=(shape,) * (rows // 2),
        in_specs=[SMEM] + [VMEM] * (cols + 1),
        out_specs=(VMEM,) * (rows // 2),
        scratch_shapes=[
            pltpu.VMEM((2 * groups, BS * BS), jnp.float32),
            pltpu.VMEM((groups * BS, LANES), jnp.float32),
        ],
        compiler_params=pltpu.CompilerParams(vmem_limit_bytes=48 * 1024 * 1024),
        name="direct_rows",
    )(col, blocks, places, *pieces)


def assemble_kernel(mirrored, mirrored_other, *refs):
    chips = (len(refs) - 1) // 2
    tile = refs[-1]
    size = PB * BS
    cols = mirrored.shape[2] // size
    for chip in range(chips):
        for j in range(2):
            sources = mirrored.at[j], mirrored_other.at[1 - j]
            direct = refs[j * chips + chip]
            rows = slice(chip * size, (chip + 1) * size)
            out_rows = slice((2 * chip + j) * size, (2 * chip + j + 1) * size)
            for s in range(cols):
                for i in range(2):
                    taken = (2 * s + (i ^ j)) * size
                    lane = (2 * s + i) * size
                    tile[out_rows, lane : lane + size] = (
                        sources[i][rows, s * size : (s + 1) * size]
                        + direct[:, taken : taken + size]
                    )


def assemble(mirrored, mirrored_other, direct, direct_other):
    _, height, width = mirrored.shape
    args = (mirrored, mirrored_other, *direct, *direct_other)
    return pl.pallas_call(
        assemble_kernel,
        out_shape=jax.ShapeDtypeStruct((2 * height, 2 * width), jnp.bfloat16),
        in_specs=[VMEM] * len(args),
        out_specs=VMEM,
        compiler_params=pltpu.CompilerParams(vmem_limit_bytes=40 * 1024 * 1024),
        name="assemble",
    )(*args)


def local(orbitals_in, hblocks, block_cols, live_counts, onsite, cut_low, top_bound):
    rows = lax.axis_size("row")
    cols = lax.axis_size("col")
    chips = rows // 2
    row = lax.axis_index("row")
    col = lax.axis_index("col")
    chip, core = row // 2, row % 2
    row_blocks, slots, _ = hblocks.shape
    k = orbitals_in.shape[1]
    local_rows = PB * BS
    total_rows = rows * cols * local_rows

    live = jnp.arange(slots, dtype=jnp.int32)[None, :] < live_counts
    device, block = block_cols // PB, block_cols % PB
    apart = (device % 2) ^ core
    distance = (device // 2) ^ chip
    places = jnp.where(live, (distance * 2 + apart) * PB + block, -1).astype(jnp.float32)
    block_row = jnp.arange(row_blocks, dtype=jnp.int32)[:, None]
    near_row = (col - block_row // PB) % cols * PB + block_row % PB
    groups = rows * row_blocks
    key = block * groups + (apart * chips + distance) * row_blocks + near_row
    key = jnp.where(live, key, -1).reshape(1, row_blocks * slots)

    half = k // 2
    first_core = core == 0

    def halves(x):
        low, high = x[:, :half], x[:, half:]
        return jnp.where(first_core, low, high), jnp.where(first_core, high, low)

    def joined(own, other, axis):
        ordered = jnp.concatenate([own, other], axis), jnp.concatenate([other, own], axis)
        return jnp.where(first_core, *ordered)

    own, other = halves(orbitals_in)

    by_owner = hblocks.reshape(cols, PB * slots, BS * BS)
    pieces = pack(col[None], by_owner, places)
    key, pieces, other = lax.optimization_barrier((key, pieces, other))
    start = jnp.concatenate([own, core_swap(other, rows)], 0)
    pieces = [shifted(piece, "col", cols, s) for s, piece in enumerate(pieces, 1)]
    pieces, start = lax.optimization_barrier((pieces, start))

    def gather(v):
        return jnp.concatenate([v] + [shifted(v, "col", cols, s) for s in range(1, cols)], 0)

    def plane_gather(v):
        return jnp.concatenate([v] + [chip_swap(v, rows, s) for s in range(1, chips)], 0)

    def from_other_core(v):
        blocks = core_swap(v, rows).reshape(-1, 2, local_rows, half)
        return jnp.stack([blocks[:, 1], blocks[:, 0]], 1).reshape(v.shape)

    mirrored = mirror(
        key, hblocks.reshape(row_blocks * slots, BS * BS), onsite, rows, row_blocks
    )

    direct = direct_rows(col[None], by_owner, places, pieces, rows, slots)
    mirrored, direct = lax.optimization_barrier((mirrored, direct))
    mirrored_other = core_swap(mirrored, rows)
    direct = [
        lax.ppermute(
            direct[s],
            "row",
            [(i, i ^ (2 * s)) for i in range(rows) if i ^ (2 * s) > i],
        )
        if s
        else direct[s]
        for s in range(chips)
    ]
    first, mirrored_other = lax.optimization_barrier(
        (start.astype(jnp.bfloat16), mirrored_other)
    )
    first_gathered, direct = lax.optimization_barrier((gather(first), direct))
    direct_other = [core_swap(rows_of_chip, rows) for rows_of_chip in direct]

    tile = assemble(mirrored, mirrored_other, direct, direct_other)

    def partial_product(gathered):
        return jnp.dot(tile, gathered, preferred_element_type=jnp.float32)

    def apply(gathered):
        terms = partial_product(gathered).reshape(chips, 2 * local_rows, half)
        total = terms[0]
        for s in range(1, chips):
            total = total + chip_swap(terms[s], rows, s)
        return total

    centre = 0.5 * (top_bound[0] + cut_low[0])
    halfwidth = 0.5 * (top_bound[0] - cut_low[0])
    previous = start
    current = (apply(first_gathered) - centre * start) / halfwidth
    for degree in range(DEG - 1):
        gathered = gather(current.astype(jnp.bfloat16))
        following = 2.0 * (apply(gathered) - centre * current) / halfwidth - previous
        previous, current = (current, following)

    rounded = current.astype(jnp.bfloat16)
    plane_rows = plane_gather(rounded)
    gathered, plane_rows = lax.optimization_barrier((gather(rounded), plane_rows))
    gathered_other = from_other_core(gathered)
    plane_other = from_other_core(plane_rows)
    filtered = joined(current[:local_rows], core_swap(current[local_rows:], rows), 1)
    contract = (((0,), (0,)), ((), ()))

    def gram_rows(g):
        return lax.dot_general(g, gathered, contract, preferred_element_type=jnp.float32)

    image = partial_product(gathered)

    def cross_rows(g):
        return lax.dot_general(g.astype(jnp.float32), image, contract, precision=HI)

    gram_part = jnp.concatenate([gram_rows(gathered), gram_rows(gathered_other)], 0)
    cross_part = jnp.concatenate([cross_rows(plane_rows), cross_rows(plane_other)], 0)
    share = k // chips
    parts = [x.reshape(chips, share, half) for x in (gram_part, cross_part)]
    parts = by_distance(jnp.stack(parts, 1), chip)
    total = sum([chip_swap(parts[s], rows, s) for s in range(1, chips)], parts[0])

    def chip_shares(x):
        return [x] + [chip_swap(x, rows, s) for s in range(1, chips)]

    def whole(shares):
        x = by_distance(jnp.stack(shares), chip).reshape(k, half)
        x = joined(x[:half], x[half:], 0)
        return joined(x, core_swap(x, rows), 1)

    cross_share = sum([shifted(total[1], "col", cols, s) for s in range(1, cols)], total[1])
    orbitals, inverse = factorize(whole(chip_shares(total[0])), filtered, total_rows)
    inverse, shares = lax.optimization_barrier((inverse, chip_shares(cross_share)))
    return orbitals, project(inverse, whole(shares), total_rows)


def solution(mesh):
    placed = (
        P(("row", "col"), None),
        P("row", "col", None),
        P("row", "col"),
        P("row", "col"),
        P(("row", "col"), None),
        P(),
        P(),
    )
    return jax.shard_map(
        local, mesh=mesh, in_specs=placed, out_specs=(P(("row", "col"), None), P()), check_vma=False
    )
```

```python
import functools

import jax
import jax.numpy as jnp
from jax import lax
from jax.experimental import pallas as pl
from jax.experimental.pallas import tpu as pltpu
from jax.sharding import PartitionSpec as P

BS = 64
PB = 2
DEG = 3
LANES = 128
PANEL = 32
HI = lax.Precision.HIGHEST
VMEM = pl.BlockSpec(memory_space=pltpu.VMEM)
SMEM = pl.BlockSpec(memory_space=pltpu.SMEM)


def widen(x, width):
    return jnp.concatenate([x] * (width // LANES), 1) if width > LANES else x

def reciprocal(x):
    return pl.reciprocal(x, approx=True)


def factor_kernel(total_rows, gram_ref, y_ref, orbitals_ref, inverse_ref):
    k = gram_ref.shape[0]
    panels = k // PANEL
    row_id = lax.broadcasted_iota(jnp.int32, (PANEL, LANES), 0)
    scale = 1.0 / total_rows
    upper = [gram_ref[m * PANEL:(m + 1) * PANEL, :] * scale for m in range(panels)]
    inverse = []
    for m in range(panels):
        r = lax.broadcasted_iota(jnp.int32, (PANEL, k), 0) + m * PANEL
        inverse.append((r == lax.broadcasted_iota(jnp.int32, (PANEL, k), 1)).astype(jnp.float32))
    for p in range(panels):
        start = p * PANEL
        s_lo = start // LANES * LANES
        w_hi = (start + PANEL + LANES - 1) // LANES * LANES
        s, w = upper[p][:, s_lo:], inverse[p][:, :w_hi]
        columns = [
            jnp.broadcast_to(s[:, start - s_lo + t:start - s_lo + t + 1], (PANEL, LANES))
            for t in range(PANEL)
        ]
        s_done, w_done = [], []
        for base in range(0, PANEL, 8):
            ids = row_id[: PANEL - base]
            pivots = jnp.zeros((8, LANES), jnp.float32)
            for t in range(base, base + 8, 2):
                at = t - base
                one, two = columns[t], columns[t + 1]
                a, b, d = one[at:at + 1, :], one[at + 1:at + 2, :], two[at + 1:at + 2, :]
                det = a * d - b * b
                det_inv = reciprocal(det)
                a_inv = reciprocal(a)
                pivots = jnp.where(ids[:8] == at, a, pivots)
                pivots = jnp.where(ids[:8] == at + 1, det * a_inv, pivots)
                below = ids > at + 1
                one_below = jnp.where(below, one, 0.0)
                two_below = jnp.where(below, two, 0.0)
                first = (d * one - b * two) * det_inv
                second = (a * two - b * one) * det_inv
                for j in range(t + 2, PANEL):
                    r = j - base
                    if j < t + 4:
                        p1, p2 = one[r:r + 1, :], two[r:r + 1, :]
                        m1, m2 = (d * p1 - b * p2) * det_inv, (a * p2 - b * p1) * det_inv
                    else:
                        m1, m2 = first[r:r + 1, :], second[r:r + 1, :]
                    columns[j] = columns[j] - (one_below * m1 + two_below * m2)
                first = jnp.where(below, first, jnp.where(ids == at + 1, b * a_inv, 0.0))
                second = jnp.where(below, second, 0.0)
                s = s - (
                    widen(first, s.shape[1]) * s[at:at + 1, :]
                    + widen(second, s.shape[1]) * s[at + 1:at + 2, :]
                )
                w = w - (
                    widen(first, w.shape[1]) * w[at:at + 1, :]
                    + widen(second, w.shape[1]) * w[at + 1:at + 2, :]
                )
            root = lax.rsqrt(pivots)
            s_done.append(s[:8] * widen(root, s.shape[1]))
            w_done.append(w[:8] * widen(root, w.shape[1]))
            s, w = s[8:], w[8:]
            columns = [c[8:] for c in columns]
        s = jnp.concatenate(s_done, 0)
        w = jnp.concatenate(w_done, 0)
        inverse_ref[start:start + PANEL, :w_hi] = w
        if w_hi < k:
            inverse_ref[start:start + PANEL, w_hi:] = jnp.zeros((PANEL, k - w_hi), jnp.float32)
        if p == panels - 1:
            break
        st = s.T
        for lo, hi in ((p + 1, p + 2), (p + 2, panels)):
            if lo >= hi:
                continue
            left = st[lo * PANEL - s_lo:hi * PANEL - s_lo, :]
            s_lo2 = lo * PANEL // LANES * LANES
            ds = jnp.dot(left, s[:, s_lo2 - s_lo:], precision=HI, preferred_element_type=jnp.float32)
            dw = jnp.dot(left, w, precision=HI, preferred_element_type=jnp.float32)
            for m in range(lo, hi):
                o = (m - lo) * PANEL
                a = upper[m][:, s_lo2:] - ds[o:o + PANEL, :]
                upper[m] = a if s_lo2 == 0 else jnp.concatenate([upper[m][:, :s_lo2], a], 1)
                b = inverse[m][:, :w_hi] - dw[o:o + PANEL, :]
                inverse[m] = b if w_hi == k else jnp.concatenate([b, inverse[m][:, w_hi:]], 1)
    inv = inverse_ref[...]
    nt = (((1,), (1,)), ((), ()))
    orbitals_ref[...] = lax.dot_general(y_ref[...], inv, nt, precision=HI, preferred_element_type=jnp.float32)


def project_kernel(total_rows, inverse_ref, cross_ref, projected_ref):
    inv = inverse_ref[...]
    nt = (((1,), (1,)), ((), ()))
    half = jnp.dot(inv, cross_ref[...], precision=HI, preferred_element_type=jnp.float32)
    full = lax.dot_general(half, inv, nt, precision=HI, preferred_element_type=jnp.float32)
    projected_ref[...] = (full + full.T) * (0.5 / total_rows)


def factorize(gram, y, total_rows):
    k = gram.shape[0]
    f32 = jnp.float32
    return pl.pallas_call(
        functools.partial(factor_kernel, total_rows),
        out_shape=(jax.ShapeDtypeStruct(y.shape, f32), jax.ShapeDtypeStruct((k, k), f32)),
        in_specs=[VMEM] * 2,
        out_specs=(VMEM,) * 2,
        compiler_params=pltpu.CompilerParams(vmem_limit_bytes=32 * 1024 * 1024),
        cost_estimate=pl.CostEstimate(
            flops=0, bytes_accessed=80 * gram.size, transcendentals=0
        ),
        name="factorize",
    )(gram, y)


def project(inverse, cross, total_rows):
    return pl.pallas_call(
        functools.partial(project_kernel, total_rows),
        out_shape=jax.ShapeDtypeStruct(cross.shape, jnp.float32),
        in_specs=[VMEM] * 2,
        out_specs=VMEM,
        compiler_params=pltpu.CompilerParams(vmem_limit_bytes=32 * 1024 * 1024),
        name="project",
    )(inverse, cross)


def exchanged(x, axis, size, apart):
    return lax.ppermute(x, axis, [(i, i ^ apart) for i in range(size)])


def shifted(x, axis, size, step):
    return lax.ppermute(x, axis, [(i, (i + step) % size) for i in range(size)])


def core_swap(x, rows):
    return exchanged(x, "row", rows, 1)


def chip_swap(x, rows, apart):
    return exchanged(x, "row", rows, 2 * apart)


def by_distance(x, index):
    size = x.shape[0]
    bit = 1
    while bit < size:
        pairs = x.reshape(size // (2 * bit), 2, bit, *x.shape[1:])
        flipped = jnp.stack([pairs[:, 1], pairs[:, 0]], 1).reshape(x.shape)
        x = jnp.where((index // bit) % 2 == 1, flipped, x)
        bit *= 2
    return x


def places_of(places_ref, owner):
    ids = lax.broadcasted_iota(jnp.int32, places_ref.shape, 0)
    return jnp.sum(jnp.where(ids == owner, places_ref[...], 0.0), 0, keepdims=True)


def pack_kernel(col_ref, blocks_ref, places_ref, *piece_refs):
    cols = len(piece_refs) + 1
    for s, piece in enumerate(piece_refs, 1):
        owner = lax.rem(col_ref[0] + s, cols)
        piece[:, : BS * BS] = blocks_ref[owner]
        count = places_ref.shape[1]
        row = jnp.broadcast_to(places_of(places_ref, owner), (piece.shape[0], count))
        piece[:, BS * BS : BS * BS + count] = row.astype(jnp.bfloat16)


def pack(col, blocks, places):
    cols, height, _ = blocks.shape
    shape = jax.ShapeDtypeStruct((height, BS * BS + LANES), jnp.bfloat16)
    return pl.pallas_call(
        pack_kernel,
        out_shape=(shape,) * (cols - 1),
        in_specs=[SMEM, VMEM, VMEM],
        out_specs=(VMEM,) * (cols - 1),
        name="pack",
    )(col, blocks, places)


def unflatten(flat_ref, square_ref, groups):
    lower = lax.broadcasted_iota(jnp.int32, (groups, LANES), 1) < BS
    for h in range(BS * BS // LANES):
        even = flat_ref[:groups, h * LANES : (h + 1) * LANES]
        odd = flat_ref[groups:, h * LANES : (h + 1) * LANES]
        first = jnp.where(lower, even, pltpu.roll(odd, BS, 1))
        second = jnp.where(lower, pltpu.roll(even, BS, 1), odd)
        square_ref[pl.ds(2 * h, groups, stride=BS), :] = first
        square_ref[pl.ds(2 * h + 1, groups, stride=BS), :] = second


def mirror_kernel(key_ref, blocks_ref, onsite_ref, out_ref, flat_ref, square_ref):
    height = out_ref.shape[2]
    groups = square_ref.shape[0] // BS
    places = lax.broadcasted_iota(jnp.int32, (2 * groups, key_ref.shape[1]), 0)
    chosen = (places == key_ref[...]).astype(jnp.float32).astype(jnp.bfloat16)
    flat_ref[...] = jnp.dot(chosen, blocks_ref[...], preferred_element_type=jnp.float32)
    for p in range(PB):
        at = p * groups + p
        flat_ref[at : at + 1, :] += onsite_ref[p : p + 1, :].astype(jnp.float32)
    unflatten(flat_ref, square_ref, groups)
    devices = square_ref.shape[0] // height
    for d in range(devices):
        which, at = d // (devices // 2), d % (devices // 2) * LANES
        square = square_ref[d * height : (d + 1) * height, :]
        out_ref[which, at : at + LANES, :] = square.T.astype(jnp.bfloat16)


def mirror(key, blocks, onsite, rows, row_blocks):
    shape = (2, rows // 2 * PB * BS, row_blocks * BS)
    groups = rows * row_blocks
    return pl.pallas_call(
        mirror_kernel,
        out_shape=jax.ShapeDtypeStruct(shape, jnp.bfloat16),
        in_specs=[VMEM, VMEM, VMEM],
        out_specs=VMEM,
        scratch_shapes=[
            pltpu.VMEM((2 * groups, BS * BS), jnp.float32),
            pltpu.VMEM((groups * BS, LANES), jnp.float32),
        ],
        compiler_params=pltpu.CompilerParams(vmem_limit_bytes=40 * 1024 * 1024),
        cost_estimate=pl.CostEstimate(
            flops=4 * groups * blocks.size, bytes_accessed=3 * blocks.size, transcendentals=0
        ),
        name="mirror",
    )(key, blocks, onsite)


def direct_kernel(rows, slots, col_ref, blocks_ref, places_ref, *refs):
    cols = blocks_ref.shape[0]
    piece_refs, out_refs = refs[: cols - 1], refs[cols - 1 : -2]
    flat_ref, square_ref = refs[-2:]
    row_blocks = cols * PB
    groups = rows * row_blocks
    total = jnp.zeros((2 * groups, BS * BS), jnp.float32)
    height = blocks_ref.shape[1]
    for s in range(cols):
        if s == 0:
            place, blocks = places_of(places_ref, col_ref[0]), blocks_ref[col_ref[0]]
        else:
            piece = piece_refs[s - 1]
            place = piece[0:1, BS * BS : BS * BS + height].astype(jnp.float32)
            blocks = piece[:, : BS * BS]
        place = place.astype(jnp.int32)
        block = lax.broadcasted_iota(jnp.int32, (1, height), 1) // slots
        key = place % 2 * groups + place // 2 * row_blocks + s * PB + block
        key = jnp.where(place < 0, -1, key)
        ids = lax.broadcasted_iota(jnp.int32, (2 * groups, height), 0)
        chosen = (ids == key).astype(jnp.float32).astype(jnp.bfloat16)
        total += jnp.dot(chosen, blocks, preferred_element_type=jnp.float32)
    flat_ref[...] = total
    unflatten(flat_ref, square_ref, groups)
    for chip, out in enumerate(out_refs):
        for g in range(2 * cols):
            at = (chip * 2 * cols + g) * LANES
            lane = (g % cols * 2 + g // cols) * LANES
            out[:, lane : lane + LANES] = square_ref[at : at + LANES, :].astype(jnp.bfloat16)


def direct_rows(col, blocks, places, pieces, rows, slots):
    cols = blocks.shape[0]
    groups = rows * cols * PB
    shape = jax.ShapeDtypeStruct((PB * BS, 2 * cols * LANES), jnp.bfloat16)
    return pl.pallas_call(
        functools.partial(direct_kernel, rows, slots),
        out_shape=(shape,) * (rows // 2),
        in_specs=[SMEM] + [VMEM] * (cols + 1),
        out_specs=(VMEM,) * (rows // 2),
        scratch_shapes=[
            pltpu.VMEM((2 * groups, BS * BS), jnp.float32),
            pltpu.VMEM((groups * BS, LANES), jnp.float32),
        ],
        compiler_params=pltpu.CompilerParams(vmem_limit_bytes=48 * 1024 * 1024),
        name="direct_rows",
    )(col, blocks, places, *pieces)


def assemble_kernel(mirrored, mirrored_other, *refs):
    chips = (len(refs) - 1) // 2
    tile = refs[-1]
    size = PB * BS
    cols = mirrored.shape[2] // size
    for chip in range(chips):
        for j in range(2):
            sources = mirrored.at[j], mirrored_other.at[1 - j]
            direct = refs[j * chips + chip]
            rows = slice(chip * size, (chip + 1) * size)
            out_rows = slice((2 * chip + j) * size, (2 * chip + j + 1) * size)
            for s in range(cols):
                for i in range(2):
                    taken = (2 * s + (i ^ j)) * size
                    lane = (2 * s + i) * size
                    tile[out_rows, lane : lane + size] = (
                        sources[i][rows, s * size : (s + 1) * size]
                        + direct[:, taken : taken + size]
                    )


def assemble(mirrored, mirrored_other, direct, direct_other):
    _, height, width = mirrored.shape
    args = (mirrored, mirrored_other, *direct, *direct_other)
    return pl.pallas_call(
        assemble_kernel,
        out_shape=jax.ShapeDtypeStruct((2 * height, 2 * width), jnp.bfloat16),
        in_specs=[VMEM] * len(args),
        out_specs=VMEM,
        compiler_params=pltpu.CompilerParams(vmem_limit_bytes=40 * 1024 * 1024),
        name="assemble",
    )(*args)


def local(orbitals_in, hblocks, block_cols, live_counts, onsite, cut_low, top_bound):
    rows = lax.axis_size("row")
    cols = lax.axis_size("col")
    chips = rows // 2
    row = lax.axis_index("row")
    col = lax.axis_index("col")
    chip, core = row // 2, row % 2
    row_blocks, slots, _ = hblocks.shape
    k = orbitals_in.shape[1]
    local_rows = PB * BS
    total_rows = rows * cols * local_rows

    live = jnp.arange(slots, dtype=jnp.int32)[None, :] < live_counts
    device, block = block_cols // PB, block_cols % PB
    apart = (device % 2) ^ core
    distance = (device // 2) ^ chip
    places = jnp.where(live, (distance * 2 + apart) * PB + block, -1).astype(jnp.float32)
    places = places.reshape(cols, PB * slots)
    block_row = jnp.arange(row_blocks, dtype=jnp.int32)[:, None]
    near_row = (col - block_row // PB) % cols * PB + block_row % PB
    groups = rows * row_blocks
    key = block * groups + (apart * chips + distance) * row_blocks + near_row
    key = jnp.where(live, key, -1).reshape(1, row_blocks * slots)

    half = k // 2
    first_core = core == 0

    def halves(x):
        low, high = x[:, :half], x[:, half:]
        return jnp.where(first_core, low, high), jnp.where(first_core, high, low)

    def joined(own, other, axis):
        ordered = jnp.concatenate([own, other], axis), jnp.concatenate([other, own], axis)
        return jnp.where(first_core, *ordered)

    by_owner = hblocks.reshape(cols, PB * slots, BS * BS)
    pieces = pack(col[None], by_owner, places)
    key, pieces = lax.optimization_barrier((key, pieces))
    pieces = [shifted(piece, "col", cols, s) for s, piece in enumerate(pieces, 1)]

    def gather(v):
        return jnp.concatenate([v] + [shifted(v, "col", cols, s) for s in range(1, cols)], 0)

    def plane_gather(v):
        return jnp.concatenate([v] + [chip_swap(v, rows, s) for s in range(1, chips)], 0)

    def from_other_core(v):
        blocks = core_swap(v, rows).reshape(-1, 2, local_rows, half)
        return jnp.stack([blocks[:, 1], blocks[:, 0]], 1).reshape(v.shape)

    mirrored = mirror(
        key, hblocks.reshape(row_blocks * slots, BS * BS), onsite, rows, row_blocks
    )

    orbitals_in, mirrored = lax.optimization_barrier((orbitals_in, mirrored))
    own, other = halves(orbitals_in)
    start = jnp.concatenate([own, core_swap(other, rows)], 0)

    direct = direct_rows(col[None], by_owner, places, pieces, rows, slots)
    mirrored, direct = lax.optimization_barrier((mirrored, direct))
    mirrored_other = core_swap(mirrored, rows)
    direct = [chip_swap(direct[s], rows, s) if s else direct[s] for s in range(chips)]
    first, mirrored_other = lax.optimization_barrier(
        (start.astype(jnp.bfloat16), mirrored_other)
    )
    first_gathered, direct = lax.optimization_barrier((gather(first), direct))
    direct_other = [core_swap(rows_of_chip, rows) for rows_of_chip in direct]

    tile = assemble(mirrored, mirrored_other, direct, direct_other)

    def partial_product(gathered):
        return jnp.dot(tile, gathered, preferred_element_type=jnp.float32)

    def apply(gathered):
        terms = partial_product(gathered).reshape(chips, 2 * local_rows, half)
        total = terms[0]
        for s in range(1, chips):
            total = total + chip_swap(terms[s], rows, s)
        return total

    centre = 0.5 * (top_bound[0] + cut_low[0])
    halfwidth = 0.5 * (top_bound[0] - cut_low[0])
    previous = start
    current = (apply(first_gathered) - centre * start) / halfwidth
    for degree in range(DEG - 1):
        gathered = gather(current.astype(jnp.bfloat16))
        following = 2.0 * (apply(gathered) - centre * current) / halfwidth - previous
        previous, current = (current, following)

    rounded = current.astype(jnp.bfloat16)
    plane_rows = plane_gather(rounded)
    gathered, plane_rows = lax.optimization_barrier((gather(rounded), plane_rows))
    gathered_other = from_other_core(gathered)
    plane_other = from_other_core(plane_rows)
    filtered = joined(current[:local_rows], core_swap(current[local_rows:], rows), 1)
    contract = (((0,), (0,)), ((), ()))

    def gram_rows(g):
        return lax.dot_general(g, gathered, contract, preferred_element_type=jnp.float32)

    image = partial_product(gathered)

    def cross_rows(g):
        return lax.dot_general(g.astype(jnp.float32), image, contract, precision=HI)

    gram_part = jnp.concatenate([gram_rows(gathered), gram_rows(gathered_other)], 0)
    cross_part = jnp.concatenate([cross_rows(plane_rows), cross_rows(plane_other)], 0)
    share = k // chips
    parts = [x.reshape(chips, share, half) for x in (gram_part, cross_part)]
    parts = by_distance(jnp.stack(parts, 1), chip)
    total = sum([chip_swap(parts[s], rows, s) for s in range(1, chips)], parts[0])

    def chip_shares(x):
        return [x] + [chip_swap(x, rows, s) for s in range(1, chips)]

    def whole(shares):
        x = by_distance(jnp.stack(shares), chip).reshape(k, half)
        x = joined(x[:half], x[half:], 0)
        return joined(x, core_swap(x, rows), 1)

    cross_share = sum([shifted(total[1], "col", cols, s) for s in range(1, cols)], total[1])
    orbitals, inverse = factorize(whole(chip_shares(total[0])), filtered, total_rows)
    inverse, shares = lax.optimization_barrier((inverse, chip_shares(cross_share)))
    return orbitals, project(inverse, whole(shares), total_rows)


def solution(mesh):
    placed = (
        P(("row", "col"), None),
        P("row", "col", None),
        P("row", "col"),
        P("row", "col"),
        P(("row", "col"), None),
        P(),
        P(),
    )
    return jax.shard_map(
        local, mesh=mesh, in_specs=placed, out_specs=(P(("row", "col"), None), P()), check_vma=False
    )
```
